128 devices in a mesh: leaf: 2 (over core), wide: 64 (over z, y, x).
Axes of the slice: x: 4, y: 4, z: 4, core: 2. Of those that a mesh axis runs over, the one named last changes fastest.
Arguments:
- drop_sides: float32 [96, 393216], P(None, ('leaf', 'wide')), may hold values from -6 to 6
- super_index: int32 [393216], P(('leaf', 'wide')), may hold values from 0 to 393215, as said below
- low_inverse: float32 [1024, 384, 384], P(('leaf', 'wide')), may hold values from -2 to 2
- coupling: bfloat16 [393216, 768], P(('leaf', 'wide')), may hold values from -0.0390625 to 0.0390625
- top_sides: float32 [96, 768], P(None, 'leaf'), may hold values from -6 to 6
- top_inverse: float32 [2, 384, 384], P('leaf'), may hold values from -2 to 2
- top_coupling: bfloat16 [2, 2, 384, 384], P(None, 'leaf'), may hold values from -0.21875 to 0.21875
Outputs:
- drop_solution: float32 [96, 393216], P(None, ('leaf', 'wide'))
- top_solution: float32 [96, 768], P(None, 'leaf')
The draws below stay inside these ranges and needn't reach their ends.
Inputs may be any that keep to these rules, and one draw needn't show every extreme that they name: `super_index`: A permutation that keeps each row within its leaf group's 3072 * 64 rows. Each device sends exactly 48 rows to every device of its group, itself included.
All inputs are finite; a program needn't handle non-finite values.
Results may differ from the reference program's by a relative error of at most 0.003.
Values may be sent and summed in bfloat16 or wider, within the bound.
A program may use at most 64 MiB of HBM per device.

```python
import math
import jax
import jax.numpy as jnp
from jax import lax

BLOCK = 384
SIDES = 96
LOW_DEV = 3072
NODES = 1024
LOW_ROWS = 393216
TOP = 2
TOP_ROWS = 768
CAPACITY = 48
N_LEAF = 2
N_WIDE = 64


def draw_low_inverse(key, part):
    key = jax.random.fold_in(key, 11)
    key_diag, key_off = jax.random.split(key)
    diagonal = jax.random.uniform(key_diag, (NODES, BLOCK), jnp.float32, 0.6, 1.4)
    offdiag = jax.random.truncated_normal(key_off, -4.0, 4.0, (NODES, BLOCK, BLOCK), jnp.float32) * (0.4 / math.sqrt(BLOCK))
    identity = jnp.eye(BLOCK, dtype=jnp.float32)
    return offdiag * (1.0 - identity) + diagonal[:, :, None] * identity


def draw_top_inverse(key, part):
    key = jax.random.fold_in(key, 12)
    key_diag, key_off = jax.random.split(key)
    diagonal = jax.random.uniform(key_diag, (TOP, BLOCK), jnp.float32, 0.6, 1.4)
    offdiag = jax.random.truncated_normal(key_off, -4.0, 4.0, (TOP, BLOCK, BLOCK), jnp.float32) * (0.4 / math.sqrt(BLOCK))
    identity = jnp.eye(BLOCK, dtype=jnp.float32)
    return offdiag * (1.0 - identity) + diagonal[:, :, None] * identity


def draw_super_index(key, part):
    key = jax.random.fold_in(key, 13)
    groups = N_LEAF
    members = N_WIDE
    row_count = LOW_DEV
    capacity = CAPACITY
    key_source, key_target = jax.random.split(key, 2)
    slot_ids = jnp.arange(row_count, dtype=jnp.int32)
    block_of = slot_ids // capacity
    source_keys = jax.random.split(key_source, groups * members)
    target_keys = jax.random.split(key_target, groups * members)
    source_order = jax.vmap(lambda one: jax.random.permutation(one, row_count))(source_keys).astype(jnp.int32).reshape(groups, members, row_count)
    target_order = jax.vmap(lambda one: jax.random.permutation(one, row_count))(target_keys).astype(jnp.int32).reshape(groups, members, row_count)
    member_ids = jnp.arange(members, dtype=jnp.int32)
    group_ids = jnp.arange(groups, dtype=jnp.int32)
    target = (member_ids[None, :, None] + block_of[None, None, :]) % members
    target = jnp.broadcast_to(target, (groups, members, row_count))
    source_global = (group_ids[:, None, None] * members + member_ids[None, :, None]) * row_count + source_order
    target_place = jnp.take_along_axis(target_order, target, axis=1)
    target_global = (group_ids[:, None, None] * members + target) * row_count + target_place
    result = jnp.zeros((groups * members * row_count,), jnp.int32)
    return result.at[source_global.reshape(-1)].set(target_global.reshape(-1))


def strengthened(values, rng, source, target, shards_of, factor):
    owner, partner = [(jnp.arange(values.shape[dim]) // (values.shape[dim] // shards_of)).reshape([-1 if axis == dim else 1 for axis in range(values.ndim)]) for dim in (source, target)]
    chosen = jax.random.permutation(rng, shards_of)[partner]
    strong = (owner == chosen) | (owner == (partner + shards_of // 2) % shards_of)
    return jnp.where(strong, factor * values, values)


def level_of(rng, extent, pieces, least, high):
    factor_of = 1.0
    for dim, parts in pieces:
        draws = jax.random.uniform(jax.random.fold_in(jax.random.fold_in(rng, 6), dim), (parts,), jnp.float32, least / len(pieces), high / len(pieces))
        factor_of = factor_of * jnp.repeat(jnp.exp(draws), extent[dim] // parts).reshape((-1,) + (1,) * (len(extent) - 1 - dim))
    return factor_of


def gaussian(stream_key, shape, scale, bound, pieces=(), kind=jnp.bfloat16):
    gain = level_of(stream_key, shape, pieces, -0.22, 0.18) if pieces else 1.0
    values = jax.random.normal(stream_key, shape, jnp.float32) * scale * gain
    return jnp.minimum(jnp.maximum(values, -bound), bound).astype(kind)


def noise_with(key, shape, scale, most, cuts, heavy, kind=jnp.bfloat16):
    array = scale * jax.random.normal(key, shape, jnp.float32)
    if cuts:
        array = array * level_of(key, shape, cuts, -0.22, 0.18)
    return jnp.clip(strengthened(array, jax.random.fold_in(key, 3), *heavy), -most, most).astype(kind)


def setup_inputs(seed: int = 0) -> dict:
    key_list = jax.random.split(jax.random.key(seed), 8)
    drop_sides = gaussian(key_list[0], (SIDES, LOW_ROWS), 1.0, 6.0, ((1, 128),), jnp.float32)
    super_index = draw_super_index(jax.random.fold_in(key_list[7], 71), 0)
    low_inverse = draw_low_inverse(jax.random.fold_in(key_list[7], 71), 0)
    coupling = noise_with(key_list[3], (LOW_ROWS, TOP_ROWS), LOW_ROWS ** -0.5, 0.0390625, ((0, 128),), (0, 1, 128, 5.5))
    top_sides = gaussian(key_list[4], (SIDES, TOP_ROWS), 1.0, 6.0, ((1, 2),), jnp.float32)
    top_inverse = draw_top_inverse(jax.random.fold_in(key_list[7], 71), 0)
    top_coupling = gaussian(key_list[6], (TOP, TOP, BLOCK, BLOCK), TOP_ROWS ** -0.5, 0.21875, ((1, 2),))
    return dict(drop_sides=drop_sides, super_index=super_index, low_inverse=low_inverse, coupling=coupling, top_sides=top_sides, top_inverse=top_inverse, top_coupling=top_coupling)


def reference(drop_sides, super_index, low_inverse, coupling, top_sides, top_inverse, top_coupling):
    super_sides = jnp.zeros_like(drop_sides).at[:, super_index].set(drop_sides)
    low_solved = jnp.einsum("rsb,sbc->rsc", super_sides.reshape(SIDES, -1, BLOCK), low_inverse,
                            precision=lax.Precision.HIGHEST).reshape(SIDES, -1)
    low_half = low_solved.astype(jnp.bfloat16)
    top_residual = top_sides - jnp.dot(low_half, coupling, preferred_element_type=jnp.float32)
    solved_list = []
    half_list = []
    for column in range(TOP):
        current = top_residual[:, column * BLOCK:(column + 1) * BLOCK]
        for earlier in range(column):
            current = current - jnp.dot(half_list[earlier], top_coupling[earlier, column],
                                        preferred_element_type=jnp.float32)
        solved = jnp.dot(current, top_inverse[column], precision=lax.Precision.HIGHEST)
        solved_list.append(solved)
        half_list.append(solved.astype(jnp.bfloat16))
    answer_list = [None] * TOP
    answer_half = [None] * TOP
    for column in range(TOP - 1, -1, -1):
        current = solved_list[column]
        for later in range(column + 1, TOP):
            current = current - jnp.dot(answer_half[later], top_coupling[column, later].T,
                                        preferred_element_type=jnp.float32)
        answer = jnp.dot(current, top_inverse[column].T, precision=lax.Precision.HIGHEST)
        answer_list[column] = answer
        answer_half[column] = answer.astype(jnp.bfloat16)
    top_solution = jnp.concatenate(answer_list, axis=1)
    solution_half = top_solution.astype(jnp.bfloat16)
    low_term = jnp.dot(solution_half, coupling.T, preferred_element_type=jnp.float32)
    low_solution = jnp.einsum("rsb,scb->rsc", (low_solved - low_term).reshape(SIDES, -1, BLOCK), low_inverse,
                              precision=lax.Precision.HIGHEST).reshape(SIDES, -1)
    drop_solution = low_solution[:, super_index]
    return drop_solution, top_solution
```

```python
import functools

import jax
import jax.numpy as jnp
from jax import lax
from jax.experimental import pallas as pl
from jax.experimental.pallas import tpu as pltpu
from jax.sharding import PartitionSpec as P

MESH = pl.DeviceIdType.MESH
F32 = jnp.float32
BF16 = jnp.bfloat16
LANES = 128
TILE = 256


def dot(a, b):
    return jnp.dot(a, b, preferred_element_type=F32)


def dot_t(a, b):
    return lax.dot_general(a, b, (((1,), (1,)), ((), ())), preferred_element_type=F32)


def split(x):
    high = x.astype(BF16)
    return high, (x - high.astype(F32)).astype(BF16)


def iota(shape, dim):
    return lax.broadcasted_iota(jnp.int32, shape, dim)


def onehot(rows, values):
    shape = (rows, values.shape[1])
    match = iota(shape, 0).astype(F32) == jnp.broadcast_to(values, shape)
    return jnp.where(match, 1.0, 0.0).astype(BF16)


def invert_step(high, low, place, rows):
    first = onehot(rows, high).astype(F32)
    lane = iota((rows, LANES), 1).astype(F32)
    left = jnp.concatenate([first * place, first * lane], axis=0).astype(BF16)
    return dot_t(left, onehot(LANES, low))


def pick(data_ref, source, height, blocks):
    high = jnp.floor(source * (1.0 / TILE))
    chooser = onehot(TILE, source - TILE * high)
    result = None
    for block in range(blocks):
        part = dot(data_ref[:height, block * TILE : (block + 1) * TILE], chooser)
        if result is None:
            result = part
        else:
            result = jnp.where(jnp.broadcast_to(high == float(block), part.shape), part, result)
    return result


def row_pair(ref, pair):
    two = ref[pl.ds(2 * pair, 2), :]
    return jnp.concatenate([two[0:1], two[1:2]], axis=1)


def turned(x):
    height = x.shape[0]
    if height < LANES:
        x = jnp.concatenate([x, jnp.zeros((LANES - height, x.shape[1]), x.dtype)], axis=0)
    return x.T


def kernel(
    dims,
    index_ref,
    drop_ref,
    inverse_any,
    coupling_any,
    top_sides_ref,
    top_inverse_any,
    top_coupling_any,
    out_ref,
    top_out_ref,
    inverse_v,
    coupling_v,
    top_inv_f32,
    top_inv_high,
    top_inv_low,
    top_coup,
    inv_high,
    inv_low,
    slot_ref,
    source_ref,
    place_ref,
    data,
    received,
    super_n,
    low_solved,
    low_half,
    low_final,
    returned,
    send_buf,
    recv_buf,
    back_send,
    back_recv,
    partial,
    rs_send,
    rs_recv,
    pair_buf,
    ag_send,
    ag_recv,
    sol,
    load_sem,
    core_send,
    core_recv,
    local_sem,
    there_send,
    there_recv,
    back_send_sem,
    back_recv_sem,
    rs_send_sem,
    rs_recv_sem,
    ag_send_sem,
    ag_recv_sem,
):
    sides, rows, members, cap, nodes, width, owners = dims
    tiles = rows // LANES
    pairs = rows // TILE
    groups = 4
    chunks = members // groups
    group_rows = rows // groups
    group_pairs = pairs // groups
    group_tiles = tiles // groups
    top_cols = 2 * width
    col_tiles = top_cols // LANES
    own_rows = sides // owners
    me = lax.axis_index("wide")
    leaf = lax.axis_index("leaf")

    load_inverse = pltpu.make_async_copy(inverse_any, inverse_v, load_sem.at[0])
    load_coupling = pltpu.make_async_copy(coupling_any, coupling_v, load_sem.at[1])
    load_top = pltpu.make_async_copy(top_inverse_any.at[0], top_inv_f32.at[leaf], load_sem.at[2])
    load_tc = pltpu.make_async_copy(top_coupling_any.at[0, 0], top_coup.at[leaf], load_sem.at[3])
    load_inverse.start()
    load_coupling.start()
    load_top.start()
    load_tc.start()

    barrier = pltpu.get_barrier_semaphore()

    def greet(step, _):
        pl.semaphore_signal(
            barrier,
            inc=1,
            device_id={"wide": lax.rem(me + step, members)},
            device_id_type=MESH,
        )
        return 0

    lax.fori_loop(1, members, greet, 0)
    pl.semaphore_signal(barrier, inc=1, device_id={"leaf": 1 - leaf}, device_id_type=MESH)

    local = index_ref[...] - leaf * (members * rows)
    target = ((local.astype(F32) + 0.5) * (1.0 / rows)).astype(jnp.int32)
    position = (local - target * rows).astype(F32)
    relative = target - me - 1
    relative = jnp.where(relative < 0, relative + members, relative).astype(F32)
    place_high = jnp.floor(position * (1.0 / LANES))
    place_low = position - LANES * place_high
    below = (iota((LANES, LANES), 0) < iota((LANES, LANES), 1)).astype(F32)
    counter = jnp.concatenate([below, jnp.ones((LANES, LANES), F32)], axis=1).astype(BF16)
    carry = jnp.zeros((members, LANES), F32)
    inverse_sum = jnp.zeros((2 * tiles, LANES), F32)
    for tile in range(tiles):
        row = relative[tile : tile + 1]
        here = onehot(members, row)
        counts = dot(here, counter)
        rank = jnp.sum(here.astype(F32) * (counts[:, :LANES] + carry), axis=0, keepdims=True)
        carry = carry + counts[:, LANES:]
        slot = row * cap + rank
        slot_ref[tile : tile + 1, :] = slot
        slot_high = jnp.floor(slot * (1.0 / LANES))
        inverse_sum += invert_step(slot_high, slot - LANES * slot_high, float(tile), tiles)
        extra = iota((16, LANES), 0)
        extra = jnp.where(
            extra == 0, place_high[tile : tile + 1], jnp.where(extra == 1, place_low[tile : tile + 1], 0.0)
        )
        data[sides : sides + 16, tile * LANES : (tile + 1) * LANES] = extra.astype(BF16)
    source_ref[...] = LANES * inverse_sum[:tiles] + inverse_sum[tiles:]
    data[:sides, :] = drop_ref[...].astype(BF16)

    pl.semaphore_wait(barrier, members)

    load_top.wait()
    load_tc.wait()
    core_top = pltpu.make_async_remote_copy(
        src_ref=top_inv_f32.at[leaf],
        dst_ref=top_inv_f32.at[leaf],
        send_sem=core_send.at[0],
        recv_sem=core_recv.at[0],
        device_id={"leaf": 1 - leaf},
        device_id_type=MESH,
    )
    core_tc = pltpu.make_async_remote_copy(
        src_ref=top_coup.at[leaf],
        dst_ref=top_coup.at[leaf],
        send_sem=core_send.at[1],
        recv_sem=core_recv.at[1],
        device_id={"leaf": 1 - leaf},
        device_id_type=MESH,
    )
    core_top.start()
    core_tc.start()

    def there(chunk):
        return pltpu.make_async_remote_copy(
            src_ref=send_buf.at[chunk],
            dst_ref=recv_buf.at[chunk],
            send_sem=there_send,
            recv_sem=there_recv.at[chunk // chunks],
            device_id={"wide": lax.rem(me + 1 + chunk, members)},
            device_id_type=MESH,
        )

    def back(chunk):
        return pltpu.make_async_remote_copy(
            src_ref=back_send.at[chunk],
            dst_ref=back_recv.at[chunk],
            send_sem=back_send_sem,
            recv_sem=back_recv_sem.at[chunk // chunks],
            device_id={"wide": lax.rem(me - 1 - chunk + 2 * members, members)},
            device_id_type=MESH,
        )

    def start_group(copy, group):
        last = (group + 1) * chunks
        if group == groups - 1:
            last -= 1

        def begin(chunk, _):
            copy(chunk).start()
            return 0

        lax.fori_loop(group * chunks, last, begin, 0)

    def wait_group(buf, sem, group, dst=True):
        count = chunks - 1 if group == groups - 1 else chunks
        part = buf.at[pl.ds(group * chunks, count)]
        pltpu.make_async_remote_copy(
            src_ref=part,
            dst_ref=part,
            send_sem=there_send,
            recv_sem=sem.at[group],
            device_id={"wide": me},
            device_id_type=MESH,
        ).wait_recv()

    own_there = pltpu.make_async_copy(
        send_buf.at[members - 1], recv_buf.at[members - 1], local_sem.at[0]
    )
    own_back = pltpu.make_async_copy(
        back_send.at[members - 1], back_recv.at[members - 1], local_sem.at[1]
    )

    def store_chunks(buf, first, block):
        for piece in range(TILE // 16):
            at = first + piece
            buf[at // 3, pl.ds(pl.multiple_of((at % 3) * 16, 16), 16), :] = block[
                piece * 16 : (piece + 1) * 16
            ]

    for group in range(groups):
        for pair in range(group * group_pairs, (group + 1) * group_pairs):
            block = pick(data, row_pair(source_ref, pair), sides + 16, pairs)
            store_chunks(send_buf, pair * (TILE // 16), turned(block).astype(BF16))
        start_group(there, group)
    own_there.start()

    load_inverse.wait()

    def halves(node, _):
        high, low = split(inverse_v[node])
        inv_high[node] = high
        inv_low[node] = low
        return 0

    lax.fori_loop(0, nodes, halves, 0)
    core_top.wait()
    core_tc.wait()
    for half in range(2):
        high, low = split(top_inv_f32[half])
        top_inv_high[half] = high
        top_inv_low[half] = low

    inverse_sum = jnp.zeros((2 * tiles, LANES), F32)
    for group in range(groups):
        wait_group(recv_buf, there_recv, group)
        if group == groups - 1:
            own_there.wait()
        block = recv_buf[group * chunks : (group + 1) * chunks].reshape(group_rows, LANES)
        for tile in range(group_tiles):
            at = group * group_tiles + tile
            columns = block[tile * LANES : (tile + 1) * LANES].astype(F32).T
            received[:, at * LANES : (at + 1) * LANES] = columns[:sides].astype(BF16)
            high = columns[sides : sides + 1]
            low = columns[sides + 1 : sides + 2]
            place_ref[at : at + 1, :] = LANES * high + low
            inverse_sum += invert_step(high, low, float(at), tiles)
    source_ref[...] = LANES * inverse_sum[:tiles] + inverse_sum[tiles:]

    def unpack(pair, _):
        block = pick(received, row_pair(source_ref, pair), sides, pairs)
        super_n[:, pl.ds(pl.multiple_of(pair * TILE, TILE), TILE)] = block.astype(BF16)
        return 0

    lax.fori_loop(0, pairs, unpack, 0)

    def solve(node, _):
        span = pl.ds(pl.multiple_of(node * width, LANES), width)
        side = super_n[:, span]
        value = dot(side, inv_high[node]) + dot(side, inv_low[node])
        low_solved[:, span] = value
        low_half[:, span] = value.astype(BF16)
        return 0

    lax.fori_loop(0, nodes, solve, 0)

    load_coupling.wait()
    for part in range(top_cols // TILE):
        partial[:, part * TILE : (part + 1) * TILE] = dot(
            low_half[...], coupling_v[:, part * TILE : (part + 1) * TILE]
        )
    first = jnp.where(me == 0, 1.0, 0.0).astype(F32)
    own_columns = pl.ds(pl.multiple_of(leaf * width, LANES), width)
    partial[:, own_columns] = partial[:, own_columns] - top_sides_ref[...] * first

    def owner_chip(owner):
        return (owner * members) // owners

    for owner in range(owners):
        for col in range(col_tiles):
            rs_send[owner, col * own_rows : (col + 1) * own_rows, :] = partial[
                owner * own_rows : (owner + 1) * own_rows, col * LANES : (col + 1) * LANES
            ]

    def rs_copy(owner):
        chip = owner_chip(owner)
        return pltpu.make_async_remote_copy(
            src_ref=rs_send.at[owner],
            dst_ref=rs_recv.at[lax.rem(chip - me - 1 + members, members)],
            send_sem=rs_send_sem,
            recv_sem=rs_recv_sem,
            device_id={"wide": chip},
            device_id_type=MESH,
        )

    my_owner = (3 * me + 7) // 8
    is_owner = owner_chip(my_owner) == me

    def send_part(step, _):
        owner = lax.rem(my_owner + step, owners)

        @pl.when(owner_chip(owner) != me)
        def _():
            rs_copy(owner).start()

        return 0

    lax.fori_loop(0, owners, send_part, 0)

    def ag_copy(step):
        return pltpu.make_async_remote_copy(
            src_ref=ag_send,
            dst_ref=ag_recv.at[my_owner],
            send_sem=ag_send_sem,
            recv_sem=ag_recv_sem,
            device_id={"wide": lax.rem(me + step, members)},
            device_id_type=MESH,
        )

    def dummy(src, dst, send, recv):
        return pltpu.make_async_remote_copy(
            src_ref=src,
            dst_ref=dst,
            send_sem=send,
            recv_sem=recv,
            device_id={"wide": me},
            device_id_type=MESH,
        )

    @pl.when(is_owner)
    def _():
        mine = pltpu.make_async_copy(rs_send.at[my_owner], rs_recv.at[members - 1], local_sem.at[2])
        mine.start()
        mine.wait()
        arrived = rs_recv.at[pl.ds(0, members - 1)]
        dummy(arrived, arrived, rs_send_sem, rs_recv_sem).wait_recv()
        pair_buf[0] = jnp.sum(rs_recv[...], axis=0)
        swap = pltpu.make_async_remote_copy(
            src_ref=pair_buf.at[0],
            dst_ref=pair_buf.at[1],
            send_sem=core_send.at[2],
            recv_sem=core_recv.at[2],
            device_id={"leaf": 1 - leaf},
            device_id_type=MESH,
        )
        swap.start()
        swap.wait()
        total = pair_buf[0] + pair_buf[1]

        def columns_of(half):
            begin = half * (col_tiles // 2)
            return jnp.concatenate(
                [
                    total[(begin + col) * own_rows : (begin + col + 1) * own_rows]
                    for col in range(col_tiles // 2)
                ],
                axis=1,
            )

        def times(product, x, half):
            high, low = split(x)
            return (
                product(high, top_inv_high[half])
                + product(low, top_inv_high[half])
                + product(high, top_inv_low[half])
            )

        solved0 = times(dot, -columns_of(0), 0)
        solved1 = times(dot, -columns_of(1) - dot(solved0.astype(BF16), top_coup[1]), 1)
        answer1 = times(dot_t, solved1, 1)
        answer0 = times(dot_t, solved0 - dot_t(answer1.astype(BF16), top_coup[1]), 0)
        for col in range(col_tiles):
            half = (answer0, answer1)[col // (col_tiles // 2)]
            at = (col % (col_tiles // 2)) * LANES
            ag_send[col * own_rows : (col + 1) * own_rows, :] = half[:, at : at + LANES]
        keep = pltpu.make_async_copy(ag_send, ag_recv.at[my_owner], local_sem.at[3])
        keep.start()

        def tell(step, _):
            ag_copy(step).start()
            return 0

        lax.fori_loop(1, members, tell, 0)
        keep.wait()
        arrived = ag_recv.at[pl.ds(0, owners - 1)]
        dummy(arrived, arrived, ag_send_sem, ag_recv_sem).wait_recv()

    @pl.when(jnp.logical_not(is_owner))
    def _():
        dummy(ag_recv, ag_recv, ag_send_sem, ag_recv_sem).wait_recv()

    for owner in range(owners):
        for col in range(col_tiles):
            sol[owner * own_rows : (owner + 1) * own_rows, col * LANES : (col + 1) * LANES] = ag_recv[
                owner, col * own_rows : (col + 1) * own_rows, :
            ]
    top_out_ref[...] = sol[:, own_columns]
    sol_half = sol[...].astype(BF16)

    def finish(node, _):
        span = pl.ds(pl.multiple_of(node * width, LANES), width)
        term = dot_t(sol_half, coupling_v[pl.ds(pl.multiple_of(node * width, width), width), :])
        high, low = split(low_solved[:, span] - term)
        value = dot_t(high, inv_high[node]) + dot_t(low, inv_high[node]) + dot_t(high, inv_low[node])
        low_final[:, span] = value.astype(BF16)
        return 0

    lax.fori_loop(0, nodes, finish, 0)

    for group in range(groups):
        for pair in range(group * group_pairs, (group + 1) * group_pairs):
            block = pick(low_final, row_pair(place_ref, pair), sides, pairs)
            store_chunks(back_send, pair * (TILE // 16), turned(block).astype(BF16))
        start_group(back, group)
    own_back.start()

    for group in range(groups):
        wait_group(back_recv, back_recv_sem, group)
        if group == groups - 1:
            own_back.wait()
        block = back_recv[group * chunks : (group + 1) * chunks].reshape(group_rows, LANES)
        for tile in range(group_tiles):
            at = group * group_tiles + tile
            columns = block[tile * LANES : (tile + 1) * LANES].astype(F32).T
            returned[:, at * LANES : (at + 1) * LANES] = columns[:sides].astype(BF16)

    def last(pair, _):
        out_ref[:, pl.ds(pl.multiple_of(pair * TILE, TILE), TILE)] = pick(
            returned, row_pair(slot_ref, pair), sides, pairs
        )
        return 0

    lax.fori_loop(0, pairs, last, 0)

    sent = send_buf.at[pl.ds(0, members - 1)]
    dummy(sent, sent, there_send, there_send).wait_send()
    sent = back_send.at[pl.ds(0, members - 1)]
    dummy(sent, sent, back_send_sem, back_send_sem).wait_send()

    @pl.when(is_owner)
    def _():
        part = rs_send.at[pl.ds(0, owners - 1)]
        dummy(part, part, rs_send_sem, rs_send_sem).wait_send()
        part = rs_recv.at[pl.ds(0, members - 1)]
        dummy(part, part, ag_send_sem, ag_send_sem).wait_send()

    @pl.when(jnp.logical_not(is_owner))
    def _():
        dummy(rs_send, rs_send, rs_send_sem, rs_send_sem).wait_send()


def shards(drop_sides, super_index, low_inverse, coupling, top_sides, top_inverse, top_coupling):
    sides, rows = drop_sides.shape
    nodes, width, _ = low_inverse.shape
    members = lax.axis_size("wide")
    cap = rows // members
    owners = 24
    top_cols = coupling.shape[1]
    tiles = rows // LANES
    own = (sides // owners) * (top_cols // LANES)
    vmem = pl.BlockSpec(memory_space=pltpu.VMEM)
    anyspace = pl.BlockSpec(memory_space=pl.ANY)
    dma = pltpu.SemaphoreType.DMA
    dims = (sides, rows, members, cap, nodes, width, owners)
    return pl.pallas_call(
        functools.partial(kernel, dims),
        out_shape=(
            jax.ShapeDtypeStruct((sides, rows), F32),
            jax.ShapeDtypeStruct(top_sides.shape, F32),
        ),
        in_specs=[vmem, vmem, anyspace, anyspace, vmem, anyspace, anyspace],
        out_specs=(vmem, vmem),
        scratch_shapes=[
            pltpu.VMEM((nodes, width, width), F32),
            pltpu.VMEM((rows, top_cols), BF16),
            pltpu.VMEM((2, width, width), F32),
            pltpu.VMEM((2, width, width), BF16),
            pltpu.VMEM((2, width, width), BF16),
            pltpu.VMEM((2, width, width), BF16),
            pltpu.VMEM((nodes, width, width), BF16),
            pltpu.VMEM((nodes, width, width), BF16),
            pltpu.VMEM((tiles, LANES), F32),
            pltpu.VMEM((tiles, LANES), F32),
            pltpu.VMEM((tiles, LANES), F32),
            pltpu.VMEM((sides + 16, rows), BF16),
            pltpu.VMEM((sides, rows), BF16),
            pltpu.VMEM((sides, rows), BF16),
            pltpu.VMEM((sides, rows), F32),
            pltpu.VMEM((sides, rows), BF16),
            pltpu.VMEM((sides, rows), BF16),
            pltpu.VMEM((sides, rows), BF16),
            pltpu.VMEM((members, cap, LANES), BF16),
            pltpu.VMEM((members, cap, LANES), BF16),
            pltpu.VMEM((members, cap, LANES), BF16),
            pltpu.VMEM((members, cap, LANES), BF16),
            pltpu.VMEM((sides, top_cols), F32),
            pltpu.VMEM((owners, own, LANES), F32),
            pltpu.VMEM((members, own, LANES), F32),
            pltpu.VMEM((2, own, LANES), F32),
            pltpu.VMEM((own, LANES), F32),
            pltpu.VMEM((owners, own, LANES), F32),
            pltpu.VMEM((sides, top_cols), F32),
            dma((4,)),
            dma((3,)),
            dma((3,)),
            dma((4,)),
            dma,
            dma((4,)),
            dma,
            dma((4,)),
            dma,
            dma,
            dma,
            dma,
        ],
        compiler_params=pltpu.CompilerParams(
            collective_id=0, has_side_effects=True, vmem_limit_bytes=56 << 20
        ),
        name="substitution",
    )(
        super_index.reshape(tiles, LANES),
        drop_sides,
        low_inverse,
        coupling,
        top_sides,
        top_inverse,
        top_coupling,
    )


def solution(mesh):
    placed = (
        P(None, ("leaf", "wide")),
        P(("leaf", "wide")),
        P(("leaf", "wide"), None, None),
        P(("leaf", "wide"), None),
        P(None, "leaf"),
        P("leaf", None, None),
        P(None, "leaf", None, None),
    )
    return jax.shard_map(
        shards,
        mesh=mesh,
        in_specs=placed,
        out_specs=(P(None, ("leaf", "wide")), P(None, "leaf")),
        check_vma=False,
    )
```

```python
import functools

import jax
import jax.numpy as jnp
from jax import lax
from jax.experimental import pallas as pl
from jax.experimental.pallas import tpu as pltpu
from jax.sharding import PartitionSpec as P

MESH = pl.DeviceIdType.MESH
F32 = jnp.float32
BF16 = jnp.bfloat16
LANES = 128
TILE = 256


def dot(a, b):
    return jnp.dot(a, b, preferred_element_type=F32)


def dot_t(a, b):
    return lax.dot_general(a, b, (((1,), (1,)), ((), ())), preferred_element_type=F32)


def split(x):
    high = x.astype(BF16)
    return high, (x - high.astype(F32)).astype(BF16)


def iota(shape, dim):
    return lax.broadcasted_iota(jnp.int32, shape, dim)


def onehot(rows, values):
    shape = (rows, values.shape[1])
    match = iota(shape, 0).astype(F32) == jnp.broadcast_to(values, shape)
    return jnp.where(match, 1.0, 0.0).astype(BF16)


def invert_step(high, low, place, rows):
    first = onehot(rows, high).astype(F32)
    lane = iota((rows, LANES), 1).astype(F32)
    left = jnp.concatenate([first * place, first * lane], axis=0).astype(BF16)
    return dot_t(left, onehot(LANES, low))


def pick(data_ref, source):
    blocks, height, _ = data_ref.shape
    high = jnp.floor(source * (1.0 / TILE))
    chooser = onehot(TILE, source - TILE * high)
    parts = dot(data_ref[...].reshape(blocks * height, TILE), chooser)
    result = parts[:height]
    for block in range(1, blocks):
        part = parts[block * height : (block + 1) * height]
        result = jnp.where(jnp.broadcast_to(high == float(block), part.shape), part, result)
    return result


def row_pair(ref, pair):
    two = ref[pl.ds(2 * pair, 2), :]
    return jnp.concatenate([two[0:1], two[1:2]], axis=1)


def turned(x):
    height = x.shape[0]
    if height < LANES:
        x = jnp.concatenate([x, jnp.zeros((LANES - height, x.shape[1]), x.dtype)], axis=0)
    return x.T


def kernel(
    dims,
    index_ref,
    drop_any,
    inverse_any,
    coupling_any,
    top_sides_ref,
    top_inverse_any,
    top_coupling_any,
    out_ref,
    top_out_ref,
    inverse_v,
    coupling_v,
    top_inv_f32,
    top_inv_high,
    top_inv_low,
    top_coup,
    inv_high,
    inv_low,
    slot_ref,
    source_ref,
    place_ref,
    drop_v,
    data,
    turned_in,
    place_wide,
    super_n,
    low_solved,
    low_half,
    low_final,
    turned_back,
    out_sum,
    send_buf,
    recv_buf,
    back_send,
    back_recv,
    partial,
    rs_send,
    rs_recv,
    pair_buf,
    ag_send,
    ag_recv,
    sol,
    load_sem,
    core_send,
    core_recv,
    local_sem,
    there_send,
    there_recv,
    back_send_sem,
    back_recv_sem,
    rs_send_sem,
    rs_recv_sem,
    ag_send_sem,
    ag_recv_sem,
):
    sides, rows, members, cap, nodes, width, owners = dims
    tiles = rows // LANES
    pairs = rows // TILE
    groups = 4
    chunks = members // groups
    group_rows = rows // groups
    group_pairs = pairs // groups
    group_tiles = tiles // groups
    top_cols = 2 * width
    col_tiles = top_cols // LANES
    own_rows = sides // owners
    me = lax.axis_index("wide")
    leaf = lax.axis_index("leaf")

    barrier = pltpu.get_barrier_semaphore()

    def greet(step, _):
        pl.semaphore_signal(
            barrier,
            inc=1,
            device_id={"wide": lax.rem(me + step, members)},
            device_id_type=MESH,
        )
        return 0

    lax.fori_loop(1, members, greet, 0)
    pl.semaphore_signal(barrier, inc=1, device_id={"leaf": 1 - leaf}, device_id_type=MESH)

    load_drop = pltpu.make_async_copy(drop_any, drop_v, load_sem.at[4])
    load_inverse = pltpu.make_async_copy(inverse_any, inverse_v, load_sem.at[0])
    load_coupling = pltpu.make_async_copy(coupling_any, coupling_v, load_sem.at[1])
    load_top = pltpu.make_async_copy(top_inverse_any.at[0], top_inv_f32.at[leaf], load_sem.at[2])
    load_tc = pltpu.make_async_copy(top_coupling_any.at[0, 0], top_coup.at[leaf], load_sem.at[3])
    load_drop.start()
    load_inverse.start()
    load_coupling.start()
    load_top.start()
    load_tc.start()

    local = index_ref[...] - leaf * (members * rows)
    target = ((local.astype(F32) + 0.5) * (1.0 / rows)).astype(jnp.int32)
    position = (local - target * rows).astype(F32)
    relative = target - me - 1
    relative = jnp.where(relative < 0, relative + members, relative).astype(F32)
    place_high = jnp.floor(position * (1.0 / LANES))
    place_low = position - LANES * place_high
    below = (iota((LANES, LANES), 0) < iota((LANES, LANES), 1)).astype(F32)
    counter = jnp.concatenate([below, jnp.ones((LANES, LANES), F32)], axis=1).astype(BF16)
    carry = jnp.zeros((members, LANES), F32)
    inverse_sum = jnp.zeros((2 * tiles, LANES), F32)
    extras = []
    for tile in range(tiles):
        row = relative[tile : tile + 1]
        here = onehot(members, row)
        counts = dot(here, counter)
        rank = jnp.sum(here.astype(F32) * (counts[:, :LANES] + carry), axis=0, keepdims=True)
        carry = carry + counts[:, LANES:]
        slot = row * cap + rank
        slot_ref[tile : tile + 1, :] = slot
        slot_high = jnp.floor(slot * (1.0 / LANES))
        inverse_sum += invert_step(slot_high, slot - LANES * slot_high, float(tile), tiles)
        extra = iota((16, LANES), 0)
        extra = jnp.where(
            extra == 0, place_high[tile : tile + 1], jnp.where(extra == 1, place_low[tile : tile + 1], 0.0)
        )
        extras.append(extra)
    source_ref[...] = LANES * inverse_sum[:tiles] + inverse_sum[tiles:]

    load_drop.wait()
    for tile in range(tiles):
        block, lanes = tile // 2, pl.ds((tile % 2) * LANES, LANES)
        values = drop_v[:, tile * LANES : (tile + 1) * LANES]
        most = jnp.maximum(jnp.max(jnp.abs(values), axis=0, keepdims=True), 2.0**-100)
        power = jnp.ceil(jnp.log2(most) - 14.99)
        code = jnp.floor(values * jnp.exp2(-power) + 0.5)
        upper = jnp.floor(code * (1.0 / 256.0))
        data[block, 0:sides, lanes] = upper.astype(BF16)
        data[block, sides : 2 * sides, lanes] = (code - 256.0 * upper).astype(BF16)
        extra = jnp.where(iota((16, LANES), 0) == 2, power, extras[tile])
        data[block, 2 * sides : 2 * sides + 16, lanes] = extra.astype(BF16)

    pl.semaphore_wait(barrier, members)

    load_top.wait()
    load_tc.wait()
    core_top = pltpu.make_async_remote_copy(
        src_ref=top_inv_f32.at[leaf],
        dst_ref=top_inv_f32.at[leaf],
        send_sem=core_send.at[0],
        recv_sem=core_recv.at[0],
        device_id={"leaf": 1 - leaf},
        device_id_type=MESH,
    )
    core_tc = pltpu.make_async_remote_copy(
        src_ref=top_coup.at[leaf],
        dst_ref=top_coup.at[leaf],
        send_sem=core_send.at[1],
        recv_sem=core_recv.at[1],
        device_id={"leaf": 1 - leaf},
        device_id_type=MESH,
    )
    core_top.start()
    core_tc.start()

    def there(chunk):
        return pltpu.make_async_remote_copy(
            src_ref=send_buf.at[chunk],
            dst_ref=recv_buf.at[chunk],
            send_sem=there_send,
            recv_sem=there_recv.at[chunk // chunks],
            device_id={"wide": lax.rem(me + 1 + chunk, members)},
            device_id_type=MESH,
        )

    def back(chunk):
        return pltpu.make_async_remote_copy(
            src_ref=back_send.at[chunk],
            dst_ref=back_recv.at[chunk],
            send_sem=back_send_sem,
            recv_sem=back_recv_sem.at[chunk // chunks],
            device_id={"wide": lax.rem(me - 1 - chunk + 2 * members, members)},
            device_id_type=MESH,
        )

    def start_group(copy, group):
        last = (group + 1) * chunks
        if group == groups - 1:
            last -= 1

        def begin(chunk, _):
            copy(chunk).start()
            return 0

        lax.fori_loop(group * chunks, last, begin, 0)

    def wait_group(buf, sem, group, dst=True):
        count = chunks - 1 if group == groups - 1 else chunks
        part = buf.at[pl.ds(group * chunks, count)]
        pltpu.make_async_remote_copy(
            src_ref=part,
            dst_ref=part,
            send_sem=there_send,
            recv_sem=sem.at[group],
            device_id={"wide": me},
            device_id_type=MESH,
        ).wait_recv()

    own_there = pltpu.make_async_copy(
        send_buf.at[members - 1], recv_buf.at[members - 1], local_sem.at[0]
    )
    own_back = pltpu.make_async_copy(
        back_send.at[members - 1], back_recv.at[members - 1], local_sem.at[1]
    )

    def store_chunks(buf, first, block):
        for piece in range(TILE // 16):
            at = first + piece
            buf[at // 3, pl.ds(pl.multiple_of((at % 3) * 16, 16), 16), :] = block[
                piece * 16 : (piece + 1) * 16
            ]

    for group in range(groups):
        for pair in range(group * group_pairs, (group + 1) * group_pairs):
            block = pick(data, row_pair(source_ref, pair))
            code = jnp.concatenate(
                [256.0 * block[:sides] + block[sides : 2 * sides], block[2 * sides :]], axis=0
            )
            code = turned(code).astype(jnp.int32).astype(jnp.int16)
            store_chunks(send_buf, pair * (TILE // 16), code)
        start_group(there, group)
    own_there.start()

    load_inverse.wait()

    def halves(node, _):
        high, low = split(inverse_v[node])
        inv_high[node] = high
        inv_low[node] = low
        return 0

    lax.fori_loop(0, nodes, halves, 0)
    core_top.wait()
    core_tc.wait()
    for half in range(2):
        high, low = split(top_inv_f32[half])
        top_inv_high[half] = high
        top_inv_low[half] = low

    for group in range(groups):
        wait_group(recv_buf, there_recv, group)
        if group == groups - 1:
            own_there.wait()
        for tile in range(group_tiles):
            at = group * group_tiles + tile
            first = group * chunks + (tile * LANES) // cap
            last = group * chunks + ((tile + 1) * LANES - 1) // cap
            skip = (tile * LANES) % cap
            block = recv_buf[first : last + 1].astype(jnp.int32).astype(F32)
            block = block.reshape((last + 1 - first) * cap, LANES)[skip : skip + LANES]
            place = LANES * block[:, sides : sides + 1] + block[:, sides + 1 : sides + 2]
            place_wide[tile * LANES : (tile + 1) * LANES, :] = jnp.broadcast_to(place, (LANES, LANES))
            columns = block.T
            place_ref[at : at + 1, :] = LANES * columns[sides : sides + 1] + columns[sides + 1 : sides + 2]
            values = columns[:sides] * jnp.exp2(columns[sides + 2 : sides + 3])
            high, low = split(values)
            lanes = pl.ds(tile * LANES, LANES)
            turned_in[:sides, lanes] = high
            turned_in[sides:, lanes] = low

        def arrive(pair, _):
            lane = iota((group_rows, LANES), 1).astype(F32) + lax.convert_element_type(pair * TILE, F32)
            there_is = place_wide[...]
            chooser = jnp.concatenate(
                [jnp.where(there_is == lane, 1.0, 0.0), jnp.where(there_is == lane + LANES, 1.0, 0.0)], axis=1
            ).astype(BF16)
            span = pl.ds(pl.multiple_of(pair * TILE, TILE), TILE)
            value = dot(turned_in[...], chooser)
            if group > 0:
                value = value + super_n[:, span]
            super_n[:, span] = value
            return 0

        lax.fori_loop(0, pairs, arrive, 0)

    for node in range(nodes):
        span = pl.ds(node * width, width)
        side = super_n[:, span].astype(BF16)
        value = dot(side, inv_high[node])
        value = value[:sides] + value[sides:] + dot(side[:sides], inv_low[node])
        low_solved[:, span] = value
        low_half[:, span] = value.astype(BF16)

    load_coupling.wait()
    for part in range(top_cols // TILE):
        partial[:, part * TILE : (part + 1) * TILE] = dot(
            low_half[...], coupling_v[:, part * TILE : (part + 1) * TILE]
        )
    first = jnp.where(me == 0, 1.0, 0.0).astype(F32)
    own_columns = pl.ds(pl.multiple_of(leaf * width, LANES), width)
    partial[:, own_columns] = partial[:, own_columns] - top_sides_ref[...] * first

    def owner_chip(owner):
        return (owner * members) // owners

    for owner in range(owners):
        for col in range(col_tiles):
            rs_send[owner, col * own_rows : (col + 1) * own_rows, :] = partial[
                owner * own_rows : (owner + 1) * own_rows, col * LANES : (col + 1) * LANES
            ]

    def rs_copy(owner):
        chip = owner_chip(owner)
        return pltpu.make_async_remote_copy(
            src_ref=rs_send.at[owner],
            dst_ref=rs_recv.at[lax.rem(chip - me - 1 + members, members)],
            send_sem=rs_send_sem,
            recv_sem=rs_recv_sem,
            device_id={"wide": chip},
            device_id_type=MESH,
        )

    my_owner = (3 * me + 7) // 8
    is_owner = owner_chip(my_owner) == me

    def send_part(step, _):
        owner = lax.rem(my_owner + step, owners)

        @pl.when(owner_chip(owner) != me)
        def _():
            rs_copy(owner).start()

        return 0

    lax.fori_loop(0, owners, send_part, 0)

    def ag_copy(step):
        return pltpu.make_async_remote_copy(
            src_ref=ag_send,
            dst_ref=ag_recv.at[my_owner],
            send_sem=ag_send_sem,
            recv_sem=ag_recv_sem,
            device_id={"wide": lax.rem(me + step, members)},
            device_id_type=MESH,
        )

    def dummy(src, dst, send, recv):
        return pltpu.make_async_remote_copy(
            src_ref=src,
            dst_ref=dst,
            send_sem=send,
            recv_sem=recv,
            device_id={"wide": me},
            device_id_type=MESH,
        )

    @pl.when(is_owner)
    def _():
        mine = pltpu.make_async_copy(rs_send.at[my_owner], rs_recv.at[members - 1], local_sem.at[2])
        mine.start()
        mine.wait()
        arrived = rs_recv.at[pl.ds(0, members - 1)]
        dummy(arrived, arrived, rs_send_sem, rs_recv_sem).wait_recv()
        pair_buf[0] = jnp.sum(rs_recv[...], axis=0)
        swap = pltpu.make_async_remote_copy(
            src_ref=pair_buf.at[0],
            dst_ref=pair_buf.at[1],
            send_sem=core_send.at[2],
            recv_sem=core_recv.at[2],
            device_id={"leaf": 1 - leaf},
            device_id_type=MESH,
        )
        swap.start()
        swap.wait()
        total = pair_buf[0] + pair_buf[1]

        def columns_of(half):
            begin = half * (col_tiles // 2)
            return jnp.concatenate(
                [
                    total[(begin + col) * own_rows : (begin + col + 1) * own_rows]
                    for col in range(col_tiles // 2)
                ],
                axis=1,
            )

        def times(product, x, half):
            high, low = split(x)
            return (
                product(high, top_inv_high[half])
                + product(low, top_inv_high[half])
                + product(high, top_inv_low[half])
            )

        solved0 = times(dot, -columns_of(0), 0)
        solved1 = times(dot, -columns_of(1) - dot(solved0.astype(BF16), top_coup[1]), 1)
        answer1 = times(dot_t, solved1, 1)
        answer0 = times(dot_t, solved0 - dot_t(answer1.astype(BF16), top_coup[1]), 0)
        for col in range(col_tiles):
            half = (answer0, answer1)[col // (col_tiles // 2)]
            at = (col % (col_tiles // 2)) * LANES
            ag_send[col * own_rows : (col + 1) * own_rows, :] = half[:, at : at + LANES]
        keep = pltpu.make_async_copy(ag_send, ag_recv.at[my_owner], local_sem.at[3])
        keep.start()

        def tell(step, _):
            ag_copy(step).start()
            return 0

        lax.fori_loop(1, members, tell, 0)
        keep.wait()
        arrived = ag_recv.at[pl.ds(0, owners - 1)]
        dummy(arrived, arrived, ag_send_sem, ag_recv_sem).wait_recv()

    @pl.when(jnp.logical_not(is_owner))
    def _():
        dummy(ag_recv, ag_recv, ag_send_sem, ag_recv_sem).wait_recv()

    for owner in range(owners):
        for col in range(col_tiles):
            sol[owner * own_rows : (owner + 1) * own_rows, col * LANES : (col + 1) * LANES] = ag_recv[
                owner, col * own_rows : (col + 1) * own_rows, :
            ]
    top_out_ref[...] = sol[:, own_columns]
    sol_half = sol[...].astype(BF16)

    for node in range(nodes):
        span = pl.ds(node * width, width)
        term = dot_t(sol_half, coupling_v[node * width : (node + 1) * width, :])
        high, low = split(low_solved[:, span] - term)
        value = dot_t(jnp.concatenate([high, low], axis=0), inv_high[node])
        value = (value[:sides] + value[sides:] + dot_t(high, inv_low[node])).astype(BF16)
        for piece in range(width // LANES):
            at = node * width + piece * LANES
            low_final[at // TILE, :, pl.ds(at % TILE, LANES)] = value[:, piece * LANES : (piece + 1) * LANES]

    for group in range(groups):
        for pair in range(group * group_pairs, (group + 1) * group_pairs):
            block = pick(low_final, row_pair(place_ref, pair))
            store_chunks(back_send, pair * (TILE // 16), turned(block).astype(BF16))
        start_group(back, group)
    own_back.start()

    for group in range(groups):
        wait_group(back_recv, back_recv_sem, group)
        if group == groups - 1:
            own_back.wait()
        block = back_recv[group * chunks : (group + 1) * chunks].reshape(group_rows, LANES)
        for tile in range(group_tiles):
            columns = block[tile * LANES : (tile + 1) * LANES].astype(F32).T
            turned_back[:, tile * LANES : (tile + 1) * LANES] = columns[:sides].astype(BF16)

        def settle(pair, _):
            chooser = onehot(group_rows, row_pair(slot_ref, pair) - float(group * group_rows))
            span = pl.ds(pl.multiple_of(pair * TILE, TILE), TILE)
            value = dot(turned_back[...], chooser)
            if group > 0:
                value = value + out_sum[:, span]
            if group < groups - 1:
                out_sum[:, span] = value
            else:
                out_ref[:, span] = value.astype(BF16)
            return 0

        lax.fori_loop(0, pairs, settle, 0)

    sent = send_buf.at[pl.ds(0, members - 1)]
    dummy(sent, sent, there_send, there_send).wait_send()
    sent = back_send.at[pl.ds(0, members - 1)]
    dummy(sent, sent, back_send_sem, back_send_sem).wait_send()

    @pl.when(is_owner)
    def _():
        part = rs_send.at[pl.ds(0, owners - 1)]
        dummy(part, part, rs_send_sem, rs_send_sem).wait_send()
        part = rs_recv.at[pl.ds(0, members - 1)]
        dummy(part, part, ag_send_sem, ag_send_sem).wait_send()

    @pl.when(jnp.logical_not(is_owner))
    def _():
        dummy(rs_send, rs_send, rs_send_sem, rs_send_sem).wait_send()


def shards(drop_sides, super_index, low_inverse, coupling, top_sides, top_inverse, top_coupling):
    sides, rows = drop_sides.shape
    nodes, width, _ = low_inverse.shape
    members = lax.axis_size("wide")
    cap = rows // members
    owners = 24
    top_cols = coupling.shape[1]
    tiles = rows // LANES
    own = (sides // owners) * (top_cols // LANES)
    vmem = pl.BlockSpec(memory_space=pltpu.VMEM)
    anyspace = pl.BlockSpec(memory_space=pl.ANY)
    dma = pltpu.SemaphoreType.DMA
    dims = (sides, rows, members, cap, nodes, width, owners)
    low, top = pl.pallas_call(
        functools.partial(kernel, dims),
        out_shape=(
            jax.ShapeDtypeStruct((sides, rows), BF16),
            jax.ShapeDtypeStruct(top_sides.shape, F32),
        ),
        in_specs=[vmem, anyspace, anyspace, anyspace, vmem, anyspace, anyspace],
        out_specs=(vmem, vmem),
        scratch_shapes=[
            pltpu.VMEM((nodes, width, width), F32),
            pltpu.VMEM((rows, top_cols), BF16),
            pltpu.VMEM((2, width, width), F32),
            pltpu.VMEM((2, width, width), BF16),
            pltpu.VMEM((2, width, width), BF16),
            pltpu.VMEM((2, width, width), BF16),
            pltpu.VMEM((nodes, width, width), BF16),
            pltpu.VMEM((nodes, width, width), BF16),
            pltpu.VMEM((tiles, LANES), F32),
            pltpu.VMEM((tiles, LANES), F32),
            pltpu.VMEM((tiles, LANES), F32),
            pltpu.VMEM((sides, rows), F32),
            pltpu.VMEM((rows // TILE, 2 * sides + 16, TILE), BF16),
            pltpu.VMEM((2 * sides, rows // 4), BF16),
            pltpu.VMEM((rows // 4, LANES), F32),
            pltpu.VMEM((2 * sides, rows), F32),
            pltpu.VMEM((sides, rows), F32),
            pltpu.VMEM((sides, rows), BF16),
            pltpu.VMEM((rows // TILE, sides, TILE), BF16),
            pltpu.VMEM((sides, rows // 4), BF16),
            pltpu.VMEM((sides, rows), F32),
            pltpu.VMEM((members, cap, LANES), jnp.int16),
            pltpu.VMEM((members, cap, LANES), jnp.int16),
            pltpu.VMEM((members, cap, LANES), BF16),
            pltpu.VMEM((members, cap, LANES), BF16),
            pltpu.VMEM((sides, top_cols), F32),
            pltpu.VMEM((owners, own, LANES), F32),
            pltpu.VMEM((members, own, LANES), F32),
            pltpu.VMEM((2, own, LANES), F32),
            pltpu.VMEM((own, LANES), F32),
            pltpu.VMEM((owners, own, LANES), F32),
            pltpu.VMEM((sides, top_cols), F32),
            dma((5,)),
            dma((3,)),
            dma((3,)),
            dma((4,)),
            dma,
            dma((4,)),
            dma,
            dma((4,)),
            dma,
            dma,
            dma,
            dma,
        ],
        compiler_params=pltpu.CompilerParams(
            collective_id=0, has_side_effects=True, vmem_limit_bytes=56 << 20
        ),
        name="substitution",
    )(
        super_index.reshape(tiles, LANES),
        drop_sides,
        low_inverse,
        coupling,
        top_sides,
        top_inverse,
        top_coupling,
    )
    return low.astype(F32), top


def solution(mesh):
    placed = (
        P(None, ("leaf", "wide")),
        P(("leaf", "wide")),
        P(("leaf", "wide"), None, None),
        P(("leaf", "wide"), None),
        P(None, "leaf"),
        P("leaf", None, None),
        P(None, "leaf", None, None),
    )
    return jax.shard_map(
        shards,
        mesh=mesh,
        in_specs=placed,
        out_specs=(P(None, ("leaf", "wide")), P(None, "leaf")),
        check_vma=False,
    )
```

```python
import functools

import jax
import jax.numpy as jnp
from jax import lax
from jax.experimental import pallas as pl
from jax.experimental.pallas import tpu as pltpu
from jax.sharding import PartitionSpec as P

MESH = pl.DeviceIdType.MESH
F32 = jnp.float32
BF16 = jnp.bfloat16
LANES = 128
TILE = 256


def dot(a, b):
    return jnp.dot(a, b, preferred_element_type=F32)


def dot_t(a, b):
    return lax.dot_general(a, b, (((1,), (1,)), ((), ())), preferred_element_type=F32)


def split(x):
    high = x.astype(BF16)
    return high, (x - high.astype(F32)).astype(BF16)


def iota(shape, dim):
    return lax.broadcasted_iota(jnp.int32, shape, dim)


def onehot(rows, values):
    shape = (rows, values.shape[1])
    match = iota(shape, 0).astype(F32) == jnp.broadcast_to(values, shape)
    return jnp.where(match, 1.0, 0.0).astype(BF16)


def invert_step(high, low, place, rows):
    first = onehot(rows, high).astype(F32)
    lane = iota((rows, LANES), 1).astype(F32)
    left = jnp.concatenate([first * place, first * lane], axis=0).astype(BF16)
    return dot_t(left, onehot(LANES, low))


def pick(data_ref, source):
    blocks, height, _ = data_ref.shape
    high = jnp.floor(source * (1.0 / TILE))
    chooser = onehot(TILE, source - TILE * high)
    parts = dot(data_ref[...].reshape(blocks * height, TILE), chooser)
    result = parts[:height]
    for block in range(1, blocks):
        part = parts[block * height : (block + 1) * height]
        result = jnp.where(jnp.broadcast_to(high == float(block), part.shape), part, result)
    return result


def merge(data_ref, chooser, high, blocks, result):
    count, height, _ = data_ref.shape
    parts = dot(data_ref[...].reshape(count * height, TILE), chooser)
    for at in range(count):
        part = parts[at * height : (at + 1) * height]
        if result is None:
            result = part
        else:
            result = jnp.where(jnp.broadcast_to(high == float(blocks + at), part.shape), part, result)
    return result


def make_choosers(ref, chooser_ref, high_ref):
    def one(pair, _):
        source = row_pair(ref, pair)
        high = jnp.floor(source * (1.0 / TILE))
        chooser_ref[pair] = onehot(TILE, source - TILE * high)
        high_ref[pl.ds(pair, 1), :] = high
        return 0

    lax.fori_loop(0, chooser_ref.shape[0], one, 0)


def row_pair(ref, pair):
    two = ref[pl.ds(2 * pair, 2), :]
    return jnp.concatenate([two[0:1], two[1:2]], axis=1)


def turned(x):
    height = x.shape[0]
    if height < LANES:
        x = jnp.concatenate([x, jnp.zeros((LANES - height, x.shape[1]), x.dtype)], axis=0)
    return x.T


def kernel(
    dims,
    index_ref,
    drop_any,
    inverse_any,
    coupling_any,
    top_sides_ref,
    top_inverse_any,
    top_coupling_any,
    out_ref,
    top_out_ref,
    inverse_v,
    coupling_v,
    top_inv_f32,
    top_inv_high,
    top_inv_low,
    top_coup,
    inv_high,
    inv_low,
    slot_ref,
    source_ref,
    place_ref,
    drop_v,
    data,
    turned_in,
    pos_send,
    pos_recv,
    choose_in,
    choose_out,
    choose_last,
    high_in,
    high_out,
    high_last,
    super_n,
    low_solved,
    low_half,
    low_final,
    turned_back,
    out_sum,
    send_buf,
    recv_buf,
    back_send,
    back_recv,
    partial,
    rs_send,
    rs_recv,
    pair_buf,
    ag_send,
    ag_recv,
    sol,
    load_sem,
    core_send,
    core_recv,
    local_sem,
    there_send,
    there_recv,
    pos_send_sem,
    pos_recv_sem,
    back_send_sem,
    back_recv_sem,
    rs_send_sem,
    rs_recv_sem,
    ag_send_sem,
    ag_recv_sem,
):
    sides, rows, members, cap, nodes, width, owners = dims
    tiles = rows // LANES
    pairs = rows // TILE
    groups = 4
    chunks = members // groups
    group_rows = rows // groups
    group_pairs = pairs // groups
    group_tiles = tiles // groups
    top_cols = 2 * width
    col_tiles = top_cols // LANES
    own_rows = sides // owners
    me = lax.axis_index("wide")
    leaf = lax.axis_index("leaf")

    barrier = pltpu.get_barrier_semaphore()

    def greet(step, _):
        pl.semaphore_signal(
            barrier,
            inc=1,
            device_id={"wide": lax.rem(me + step, members)},
            device_id_type=MESH,
        )
        return 0

    lax.fori_loop(1, members, greet, 0)
    pl.semaphore_signal(barrier, inc=1, device_id={"leaf": 1 - leaf}, device_id_type=MESH)

    load_drop = pltpu.make_async_copy(drop_any, drop_v, load_sem.at[4])
    load_inverse = pltpu.make_async_copy(inverse_any, inverse_v, load_sem.at[0])
    load_coupling = pltpu.make_async_copy(coupling_any, coupling_v, load_sem.at[1])
    load_top = pltpu.make_async_copy(top_inverse_any.at[0], top_inv_f32.at[leaf], load_sem.at[2])
    load_tc = pltpu.make_async_copy(top_coupling_any.at[0, 0], top_coup.at[leaf], load_sem.at[3])
    load_drop.start()
    load_inverse.start()
    load_coupling.start()
    load_top.start()
    load_tc.start()

    local = index_ref[...] - leaf * (members * rows)
    target = ((local.astype(F32) + 0.5) * (1.0 / rows)).astype(jnp.int32)
    position = (local - target * rows).astype(F32)
    relative = target - me - 1
    relative = jnp.where(relative < 0, relative + members, relative).astype(F32)
    place_high = jnp.floor(position * (1.0 / LANES))
    place_low = position - LANES * place_high
    below = (iota((LANES, LANES), 0) < iota((LANES, LANES), 1)).astype(F32)
    counter = jnp.concatenate([below, jnp.ones((LANES, LANES), F32)], axis=1).astype(BF16)
    carry = jnp.zeros((members, LANES), F32)
    inverse_sum = jnp.zeros((2 * tiles, LANES), F32)
    extras = []
    places = jnp.zeros((2 * members, LANES), F32)
    for tile in range(tiles):
        row = relative[tile : tile + 1]
        here = onehot(members, row)
        counts = dot(here, counter)
        rank = jnp.sum(here.astype(F32) * (counts[:, :LANES] + carry), axis=0, keepdims=True)
        carry = carry + counts[:, LANES:]
        slot = row * cap + rank
        slot_ref[tile : tile + 1, :] = slot
        both = jnp.concatenate(
            [here * place_high[tile : tile + 1].astype(BF16), here * place_low[tile : tile + 1].astype(BF16)], axis=0
        )
        places = places + dot_t(both, onehot(LANES, rank))
        slot_high = jnp.floor(slot * (1.0 / LANES))
        inverse_sum += invert_step(slot_high, slot - LANES * slot_high, float(tile), tiles)
        extra = iota((16, LANES), 0)
        extra = jnp.where(
            extra == 0, place_high[tile : tile + 1], jnp.where(extra == 1, place_low[tile : tile + 1], 0.0)
        )
        extras.append(extra)
    source_ref[...] = LANES * inverse_sum[:tiles] + inverse_sum[tiles:]
    places = jnp.where(iota((members, LANES), 1) < cap, LANES * places[:members] + places[members:], -1.0)
    for member in range(members):
        pos_send[member] = places[member : member + 1]
    pos_recv[members - 1] = places[members - 1 : members]

    load_drop.wait()
    for tile in range(tiles):
        block, lanes = tile // 2, pl.ds((tile % 2) * LANES, LANES)
        values = drop_v[:, tile * LANES : (tile + 1) * LANES]
        most = jnp.maximum(jnp.max(jnp.abs(values), axis=0, keepdims=True), 2.0**-100)
        power = jnp.ceil(jnp.log2(most) - 14.99)
        code = jnp.floor(values * jnp.exp2(-power) + 0.5)
        upper = jnp.floor(code * (1.0 / 256.0))
        data[block, 0:sides, lanes] = upper.astype(BF16)
        data[block, sides : 2 * sides, lanes] = (code - 256.0 * upper).astype(BF16)
        extra = jnp.where(iota((16, LANES), 0) == 2, power, extras[tile])
        data[block, 2 * sides : 2 * sides + 16, lanes] = extra.astype(BF16)

    pl.semaphore_wait(barrier, members)

    def dummy(src, dst, send, recv):
        return pltpu.make_async_remote_copy(
            src_ref=src,
            dst_ref=dst,
            send_sem=send,
            recv_sem=recv,
            device_id={"wide": me},
            device_id_type=MESH,
        )

    def ahead(chunk):
        return pltpu.make_async_remote_copy(
            src_ref=pos_send.at[chunk],
            dst_ref=pos_recv.at[chunk],
            send_sem=pos_send_sem,
            recv_sem=pos_recv_sem,
            device_id={"wide": lax.rem(me + 1 + chunk, members)},
            device_id_type=MESH,
        )

    def go_ahead(chunk, _):
        ahead(chunk).start()
        return 0

    lax.fori_loop(0, members - 1, go_ahead, 0)

    load_top.wait()
    load_tc.wait()
    core_top = pltpu.make_async_remote_copy(
        src_ref=top_inv_f32.at[leaf],
        dst_ref=top_inv_f32.at[leaf],
        send_sem=core_send.at[0],
        recv_sem=core_recv.at[0],
        device_id={"leaf": 1 - leaf},
        device_id_type=MESH,
    )
    core_tc = pltpu.make_async_remote_copy(
        src_ref=top_coup.at[leaf],
        dst_ref=top_coup.at[leaf],
        send_sem=core_send.at[1],
        recv_sem=core_recv.at[1],
        device_id={"leaf": 1 - leaf},
        device_id_type=MESH,
    )
    core_top.start()
    core_tc.start()

    def there(chunk):
        return pltpu.make_async_remote_copy(
            src_ref=send_buf.at[chunk],
            dst_ref=recv_buf.at[chunk],
            send_sem=there_send,
            recv_sem=there_recv.at[chunk // chunks],
            device_id={"wide": lax.rem(me + 1 + chunk, members)},
            device_id_type=MESH,
        )

    def back(chunk):
        return pltpu.make_async_remote_copy(
            src_ref=back_send.at[chunk],
            dst_ref=back_recv.at[chunk],
            send_sem=back_send_sem,
            recv_sem=back_recv_sem.at[chunk // chunks],
            device_id={"wide": lax.rem(me - 1 - chunk + 2 * members, members)},
            device_id_type=MESH,
        )

    def start_group(copy, group):
        last = (group + 1) * chunks
        if group == groups - 1:
            last -= 1

        def begin(chunk, _):
            copy(chunk).start()
            return 0

        lax.fori_loop(group * chunks, last, begin, 0)

    def wait_group(buf, sem, group, dst=True):
        count = chunks - 1 if group == groups - 1 else chunks
        part = buf.at[pl.ds(group * chunks, count)]
        pltpu.make_async_remote_copy(
            src_ref=part,
            dst_ref=part,
            send_sem=there_send,
            recv_sem=sem.at[group],
            device_id={"wide": me},
            device_id_type=MESH,
        ).wait_recv()

    own_there = pltpu.make_async_copy(
        send_buf.at[members - 1], recv_buf.at[members - 1], local_sem.at[0]
    )
    own_back = pltpu.make_async_copy(
        back_send.at[members - 1], back_recv.at[members - 1], local_sem.at[1]
    )

    def store_chunks(buf, first, block):
        for piece in range(TILE // 16):
            at = first + piece
            buf[at // 3, pl.ds(pl.multiple_of((at % 3) * 16, 16), 16), :] = block[
                piece * 16 : (piece + 1) * 16
            ]

    for group in range(groups):
        for pair in range(group * group_pairs, (group + 1) * group_pairs):
            block = pick(data, row_pair(source_ref, pair))
            code = jnp.concatenate(
                [256.0 * block[:sides] + block[sides : 2 * sides], block[2 * sides :]], axis=0
            )
            code = turned(code).astype(jnp.int32).astype(jnp.int16)
            store_chunks(send_buf, pair * (TILE // 16), code)
        start_group(there, group)
    own_there.start()

    load_inverse.wait()

    def halves(node, _):
        high, low = split(inverse_v[node])
        inv_high[node] = high
        inv_low[node] = low
        return 0

    lax.fori_loop(0, nodes, halves, 0)
    core_top.wait()
    core_tc.wait()
    for half in range(2):
        high, low = split(top_inv_f32[half])
        top_inv_high[half] = high
        top_inv_low[half] = low

    arrived = pos_recv.at[pl.ds(0, members - 1)]
    dummy(arrived, arrived, pos_send_sem, pos_recv_sem).wait_recv()
    lane = iota((1, LANES), 1)
    second = (lane >= LANES // 2).astype(F32)
    offset = lane.astype(F32) - second * (LANES // 2)
    inverse_sum = jnp.zeros((2 * tiles, LANES), F32)
    for member in range(members // 2):
        other = pltpu.roll(pos_recv[member + members // 2], LANES // 2, 1)
        place = jnp.where(lane < LANES // 2, pos_recv[member], other)
        high = jnp.floor(place * (1.0 / LANES))
        first = onehot(tiles, high).astype(F32)
        left = jnp.concatenate([first * (second * (members // 2) + float(member)), first * offset], axis=0)
        inverse_sum += dot_t(left.astype(BF16), onehot(LANES, place - LANES * high))
    source_ref[...] = cap * inverse_sum[:tiles] + inverse_sum[tiles:]
    make_choosers(source_ref, choose_in, high_in)
    make_choosers(slot_ref, choose_last, high_last)

    for group in range(groups):
        wait_group(recv_buf, there_recv, group)
        if group == groups - 1:
            own_there.wait()
        for tile in range(group_tiles):
            at = group * group_tiles + tile
            first = group * chunks + (tile * LANES) // cap
            last = group * chunks + ((tile + 1) * LANES - 1) // cap
            skip = (tile * LANES) % cap
            block = recv_buf[first : last + 1].astype(jnp.int32).astype(F32)
            columns = block.reshape((last + 1 - first) * cap, LANES)[skip : skip + LANES].T
            place_ref[at : at + 1, :] = LANES * columns[sides : sides + 1] + columns[sides + 1 : sides + 2]
            values = columns[:sides] * jnp.exp2(columns[sides + 2 : sides + 3])
            high, low = split(values)
            lanes = pl.ds((tile % 2) * LANES, LANES)
            turned_in[tile // 2, :sides, lanes] = high
            turned_in[tile // 2, sides:, lanes] = low

        for pair in range(pairs):
            span = pl.ds(pair * TILE, TILE)
            before = super_n[:, span] if group > 0 else None
            super_n[:, span] = merge(
                turned_in, choose_in[pair], high_in[pair : pair + 1], group * group_pairs, before
            )

    for node in range(nodes):
        span = pl.ds(node * width, width)
        side = super_n[:, span].astype(BF16)
        value = dot(side, inv_high[node])
        value = value[:sides] + value[sides:] + dot(side[:sides], inv_low[node])
        low_solved[:, span] = value
        low_half[:, span] = value.astype(BF16)

    load_coupling.wait()
    for part in range(top_cols // TILE):
        partial[:, part * TILE : (part + 1) * TILE] = dot(
            low_half[...], coupling_v[:, part * TILE : (part + 1) * TILE]
        )
    first = jnp.where(me == 0, 1.0, 0.0).astype(F32)
    own_columns = pl.ds(pl.multiple_of(leaf * width, LANES), width)
    partial[:, own_columns] = partial[:, own_columns] - top_sides_ref[...] * first

    def owner_chip(owner):
        return (owner * members) // owners

    for owner in range(owners):
        for col in range(col_tiles):
            rs_send[owner, col * own_rows : (col + 1) * own_rows, :] = partial[
                owner * own_rows : (owner + 1) * own_rows, col * LANES : (col + 1) * LANES
            ]

    def rs_copy(owner):
        chip = owner_chip(owner)
        return pltpu.make_async_remote_copy(
            src_ref=rs_send.at[owner],
            dst_ref=rs_recv.at[lax.rem(chip - me - 1 + members, members)],
            send_sem=rs_send_sem,
            recv_sem=rs_recv_sem,
            device_id={"wide": chip},
            device_id_type=MESH,
        )

    my_owner = (3 * me + 7) // 8
    is_owner = owner_chip(my_owner) == me

    def send_part(step, _):
        owner = lax.rem(my_owner + step, owners)

        @pl.when(owner_chip(owner) != me)
        def _():
            rs_copy(owner).start()

        return 0

    lax.fori_loop(0, owners, send_part, 0)

    make_choosers(place_ref, choose_out, high_out)

    def ag_copy(step):
        return pltpu.make_async_remote_copy(
            src_ref=ag_send,
            dst_ref=ag_recv.at[my_owner],
            send_sem=ag_send_sem,
            recv_sem=ag_recv_sem,
            device_id={"wide": lax.rem(me + step, members)},
            device_id_type=MESH,
        )

    @pl.when(is_owner)
    def _():
        mine = pltpu.make_async_copy(rs_send.at[my_owner], rs_recv.at[members - 1], local_sem.at[2])
        mine.start()
        mine.wait()
        arrived = rs_recv.at[pl.ds(0, members - 1)]
        dummy(arrived, arrived, rs_send_sem, rs_recv_sem).wait_recv()
        pair_buf[0] = jnp.sum(rs_recv[...], axis=0)
        swap = pltpu.make_async_remote_copy(
            src_ref=pair_buf.at[0],
            dst_ref=pair_buf.at[1],
            send_sem=core_send.at[2],
            recv_sem=core_recv.at[2],
            device_id={"leaf": 1 - leaf},
            device_id_type=MESH,
        )
        swap.start()
        swap.wait()
        total = pair_buf[0] + pair_buf[1]

        def columns_of(half):
            begin = half * (col_tiles // 2)
            return jnp.concatenate(
                [
                    total[(begin + col) * own_rows : (begin + col + 1) * own_rows]
                    for col in range(col_tiles // 2)
                ],
                axis=1,
            )

        def times(product, x, half):
            high, low = split(x)
            return (
                product(high, top_inv_high[half])
                + product(low, top_inv_high[half])
                + product(high, top_inv_low[half])
            )

        solved0 = times(dot, -columns_of(0), 0)
        solved1 = times(dot, -columns_of(1) - dot(solved0.astype(BF16), top_coup[1]), 1)
        answer1 = times(dot_t, solved1, 1)
        answer0 = times(dot_t, solved0 - dot_t(answer1.astype(BF16), top_coup[1]), 0)
        for col in range(col_tiles):
            half = (answer0, answer1)[col // (col_tiles // 2)]
            at = (col % (col_tiles // 2)) * LANES
            ag_send[col * own_rows : (col + 1) * own_rows, :] = half[:, at : at + LANES]
        keep = pltpu.make_async_copy(ag_send, ag_recv.at[my_owner], local_sem.at[3])
        keep.start()

        def tell(step, _):
            ag_copy(step).start()
            return 0

        lax.fori_loop(1, members, tell, 0)
        keep.wait()
        arrived = ag_recv.at[pl.ds(0, owners - 1)]
        dummy(arrived, arrived, ag_send_sem, ag_recv_sem).wait_recv()

    @pl.when(jnp.logical_not(is_owner))
    def _():
        dummy(ag_recv, ag_recv, ag_send_sem, ag_recv_sem).wait_recv()

    for owner in range(owners):
        for col in range(col_tiles):
            sol[owner * own_rows : (owner + 1) * own_rows, col * LANES : (col + 1) * LANES] = ag_recv[
                owner, col * own_rows : (col + 1) * own_rows, :
            ]
    top_out_ref[...] = sol[:, own_columns]
    sol_half = sol[...].astype(BF16)

    for node in range(nodes):
        span = pl.ds(node * width, width)
        term = dot_t(sol_half, coupling_v[node * width : (node + 1) * width, :])
        high, low = split(low_solved[:, span] - term)
        value = dot_t(jnp.concatenate([high, low], axis=0), inv_high[node])
        value = (value[:sides] + value[sides:] + dot_t(high, inv_low[node])).astype(BF16)
        for piece in range(width // LANES):
            at = node * width + piece * LANES
            low_final[at // TILE, :, pl.ds(at % TILE, LANES)] = value[:, piece * LANES : (piece + 1) * LANES]

    for group in range(groups):
        for pair in range(group * group_pairs, (group + 1) * group_pairs):
            block = merge(low_final, choose_out[pair], high_out[pair : pair + 1], 0, None)
            store_chunks(back_send, pair * (TILE // 16), turned(block).astype(BF16))
        start_group(back, group)
    own_back.start()

    for group in range(groups):
        wait_group(back_recv, back_recv_sem, group)
        if group == groups - 1:
            own_back.wait()
        block = back_recv[group * chunks : (group + 1) * chunks].reshape(group_rows, LANES)
        for tile in range(group_tiles):
            columns = block[tile * LANES : (tile + 1) * LANES].astype(F32).T
            turned_back[tile // 2, :, pl.ds((tile % 2) * LANES, LANES)] = columns[:sides].astype(BF16)

        for pair in range(pairs):
            span = pl.ds(pair * TILE, TILE)
            before = out_sum[:, span] if group > 0 else None
            value = merge(
                turned_back, choose_last[pair], high_last[pair : pair + 1], group * group_pairs, before
            )
            if group < groups - 1:
                out_sum[:, span] = value
            else:
                out_ref[:, span] = value.astype(BF16)

    sent = pos_send.at[pl.ds(0, members - 1)]
    dummy(sent, sent, pos_send_sem, pos_send_sem).wait_send()
    sent = send_buf.at[pl.ds(0, members - 1)]
    dummy(sent, sent, there_send, there_send).wait_send()
    sent = back_send.at[pl.ds(0, members - 1)]
    dummy(sent, sent, back_send_sem, back_send_sem).wait_send()

    @pl.when(is_owner)
    def _():
        part = rs_send.at[pl.ds(0, owners - 1)]
        dummy(part, part, rs_send_sem, rs_send_sem).wait_send()
        part = rs_recv.at[pl.ds(0, members - 1)]
        dummy(part, part, ag_send_sem, ag_send_sem).wait_send()

    @pl.when(jnp.logical_not(is_owner))
    def _():
        dummy(rs_send, rs_send, rs_send_sem, rs_send_sem).wait_send()


def shards(drop_sides, super_index, low_inverse, coupling, top_sides, top_inverse, top_coupling):
    sides, rows = drop_sides.shape
    nodes, width, _ = low_inverse.shape
    members = lax.axis_size("wide")
    cap = rows // members
    owners = 24
    top_cols = coupling.shape[1]
    tiles = rows // LANES
    own = (sides // owners) * (top_cols // LANES)
    vmem = pl.BlockSpec(memory_space=pltpu.VMEM)
    anyspace = pl.BlockSpec(memory_space=pl.ANY)
    dma = pltpu.SemaphoreType.DMA
    dims = (sides, rows, members, cap, nodes, width, owners)
    low, top = pl.pallas_call(
        functools.partial(kernel, dims),
        out_shape=(
            jax.ShapeDtypeStruct((sides, rows), BF16),
            jax.ShapeDtypeStruct(top_sides.shape, F32),
        ),
        in_specs=[vmem, anyspace, anyspace, anyspace, vmem, anyspace, anyspace],
        out_specs=(vmem, vmem),
        scratch_shapes=[
            pltpu.VMEM((nodes, width, width), F32),
            pltpu.VMEM((rows, top_cols), BF16),
            pltpu.VMEM((2, width, width), F32),
            pltpu.VMEM((2, width, width), BF16),
            pltpu.VMEM((2, width, width), BF16),
            pltpu.VMEM((2, width, width), BF16),
            pltpu.VMEM((nodes, width, width), BF16),
            pltpu.VMEM((nodes, width, width), BF16),
            pltpu.VMEM((tiles, LANES), F32),
            pltpu.VMEM((tiles, LANES), F32),
            pltpu.VMEM((tiles, LANES), F32),
            pltpu.VMEM((sides, rows), F32),
            pltpu.VMEM((rows // TILE, 2 * sides + 16, TILE), BF16),
            pltpu.VMEM((rows // TILE // 4, 2 * sides, TILE), BF16),
            pltpu.VMEM((members, 1, LANES), F32),
            pltpu.VMEM((members, 1, LANES), F32),
            pltpu.VMEM((rows // TILE, TILE, TILE), BF16),
            pltpu.VMEM((rows // TILE, TILE, TILE), BF16),
            pltpu.VMEM((rows // TILE, TILE, TILE), BF16),
            pltpu.VMEM((rows // TILE, TILE), F32),
            pltpu.VMEM((rows // TILE, TILE), F32),
            pltpu.VMEM((rows // TILE, TILE), F32),
            pltpu.VMEM((2 * sides, rows), F32),
            pltpu.VMEM((sides, rows), F32),
            pltpu.VMEM((sides, rows), BF16),
            pltpu.VMEM((rows // TILE, sides, TILE), BF16),
            pltpu.VMEM((rows // TILE // 4, sides, TILE), BF16),
            pltpu.VMEM((sides, rows), F32),
            pltpu.VMEM((members, cap, LANES), jnp.int16),
            pltpu.VMEM((members, cap, LANES), jnp.int16),
            pltpu.VMEM((members, cap, LANES), BF16),
            pltpu.VMEM((members, cap, LANES), BF16),
            pltpu.VMEM((sides, top_cols), F32),
            pltpu.VMEM((owners, own, LANES), F32),
            pltpu.VMEM((members, own, LANES), F32),
            pltpu.VMEM((2, own, LANES), F32),
            pltpu.VMEM((own, LANES), F32),
            pltpu.VMEM((owners, own, LANES), F32),
            pltpu.VMEM((sides, top_cols), F32),
            dma((5,)),
            dma((3,)),
            dma((3,)),
            dma((4,)),
            dma,
            dma((4,)),
            dma,
            dma,
            dma,
            dma((4,)),
            dma,
            dma,
            dma,
            dma,
        ],
        compiler_params=pltpu.CompilerParams(
            collective_id=0, has_side_effects=True, vmem_limit_bytes=56 << 20
        ),
        name="substitution",
    )(
        super_index.reshape(tiles, LANES),
        drop_sides,
        low_inverse,
        coupling,
        top_sides,
        top_inverse,
        top_coupling,
    )
    return low.astype(F32), top


def solution(mesh):
    placed = (
        P(None, ("leaf", "wide")),
        P(("leaf", "wide")),
        P(("leaf", "wide"), None, None),
        P(("leaf", "wide"), None),
        P(None, "leaf"),
        P("leaf", None, None),
        P(None, "leaf", None, None),
    )
    return jax.shard_map(
        shards,
        mesh=mesh,
        in_specs=placed,
        out_specs=(P(None, ("leaf", "wide")), P(None, "leaf")),
        check_vma=False,
    )
```

```python
import functools

import jax
import jax.numpy as jnp
from jax import lax
from jax.experimental import pallas as pl
from jax.experimental.pallas import tpu as pltpu
from jax.sharding import PartitionSpec as P

MESH = pl.DeviceIdType.MESH
F32 = jnp.float32
BF16 = jnp.bfloat16
LANES = 128
TILE = 256


def dot(a, b):
    return jnp.dot(a, b, preferred_element_type=F32)


def dot_t(a, b):
    return lax.dot_general(a, b, (((1,), (1,)), ((), ())), preferred_element_type=F32)


def split(x):
    high = x.astype(BF16)
    return high, (x - high.astype(F32)).astype(BF16)


def iota(shape, dim):
    return lax.broadcasted_iota(jnp.int32, shape, dim)


def onehot(rows, values):
    shape = (rows, values.shape[1])
    match = iota(shape, 0).astype(F32) == jnp.broadcast_to(values, shape)
    return jnp.where(match, 1.0, 0.0).astype(BF16)


def invert_step(high, low, place, rows):
    first = onehot(rows, high).astype(F32)
    lane = iota((rows, LANES), 1).astype(F32)
    left = jnp.concatenate([first * place, first * lane], axis=0).astype(BF16)
    return dot_t(left, onehot(LANES, low))


def pick(data_ref, source):
    blocks, height, _ = data_ref.shape
    high = jnp.floor(source * (1.0 / TILE))
    chooser = onehot(TILE, source - TILE * high)
    parts = dot(data_ref[...].reshape(blocks * height, TILE), chooser)
    result = parts[:height]
    for block in range(1, blocks):
        part = parts[block * height : (block + 1) * height]
        result = jnp.where(jnp.broadcast_to(high == float(block), part.shape), part, result)
    return result


def merge(data_ref, chooser, high, blocks, result):
    count, height, _ = data_ref.shape
    parts = dot(data_ref[...].reshape(count * height, TILE), chooser)
    for at in range(count):
        part = parts[at * height : (at + 1) * height]
        if result is None:
            result = part
        else:
            result = jnp.where(jnp.broadcast_to(high == float(blocks + at), part.shape), part, result)
    return result


def make_choosers(ref, chooser_ref, high_ref):
    def one(pair, _):
        source = row_pair(ref, pair)
        high = jnp.floor(source * (1.0 / TILE))
        chooser_ref[pair] = onehot(TILE, source - TILE * high)
        high_ref[pl.ds(pair, 1), :] = high
        return 0

    lax.fori_loop(0, chooser_ref.shape[0], one, 0)


def row_pair(ref, pair):
    two = ref[pl.ds(2 * pair, 2), :]
    return jnp.concatenate([two[0:1], two[1:2]], axis=1)


def turned(x):
    height = x.shape[0]
    if height < LANES:
        x = jnp.concatenate([x, jnp.zeros((LANES - height, x.shape[1]), x.dtype)], axis=0)
    return x.T


def kernel(
    dims,
    index_ref,
    drop_any,
    inverse_any,
    coupling_any,
    top_sides_ref,
    top_inverse_any,
    top_coupling_any,
    out_ref,
    top_out_ref,
    inverse_v,
    coupling_v,
    top_inv_f32,
    top_inv_high,
    top_inv_low,
    top_coup,
    inv_high,
    inv_low,
    slot_ref,
    source_ref,
    place_ref,
    drop_v,
    data,
    turned_in,
    pos_send,
    pos_recv,
    choose_in,
    choose_out,
    choose_last,
    high_in,
    high_out,
    high_last,
    super_n,
    low_solved,
    low_half,
    low_final,
    turned_back,
    out_sum,
    send_buf,
    recv_buf,
    back_send,
    back_recv,
    partial,
    half_send,
    half_recv,
    rs_send,
    rs_recv,
    pair_buf,
    ag_send,
    ag_recv,
    sol_half,
    load_sem,
    core_send,
    core_recv,
    local_sem,
    there_send,
    there_recv,
    pos_send_sem,
    pos_recv_sem,
    back_send_sem,
    back_recv_sem,
    rs_send_sem,
    rs_recv_sem,
    ag_send_sem,
    ag_recv_sem,
):
    sides, rows, members, cap, nodes, width, owners = dims
    tiles = rows // LANES
    pairs = rows // TILE
    groups = 4
    chunks = members // groups
    group_rows = rows // groups
    group_pairs = pairs // groups
    group_tiles = tiles // groups
    own_rows = sides // owners
    me = lax.axis_index("wide")
    leaf = lax.axis_index("leaf")

    barrier = pltpu.get_barrier_semaphore()

    def greet(step, _):
        pl.semaphore_signal(
            barrier,
            inc=1,
            device_id={"wide": lax.rem(me + step, members)},
            device_id_type=MESH,
        )
        return 0

    lax.fori_loop(1, members, greet, 0)
    pl.semaphore_signal(barrier, inc=1, device_id={"leaf": 1 - leaf}, device_id_type=MESH)

    load_drop = pltpu.make_async_copy(drop_any, drop_v, load_sem.at[4])
    load_inverse = pltpu.make_async_copy(inverse_any, inverse_v, load_sem.at[0])
    load_coupling = pltpu.make_async_copy(coupling_any, coupling_v, load_sem.at[1])
    load_top = pltpu.make_async_copy(top_inverse_any.at[0], top_inv_f32.at[leaf], load_sem.at[2])
    load_tc = pltpu.make_async_copy(top_coupling_any.at[0, 0], top_coup.at[leaf], load_sem.at[3])
    load_drop.start()
    load_inverse.start()
    load_coupling.start()
    load_top.start()
    load_tc.start()

    local = index_ref[...] - leaf * (members * rows)
    target = ((local.astype(F32) + 0.5) * (1.0 / rows)).astype(jnp.int32)
    position = (local - target * rows).astype(F32)
    relative = target - me - 1
    relative = jnp.where(relative < 0, relative + members, relative).astype(F32)
    place_high = jnp.floor(position * (1.0 / LANES))
    place_low = position - LANES * place_high
    below = (iota((LANES, LANES), 0) < iota((LANES, LANES), 1)).astype(F32)
    counter = jnp.concatenate([below, jnp.ones((LANES, LANES), F32)], axis=1).astype(BF16)
    carry = jnp.zeros((members, LANES), F32)
    inverse_sum = jnp.zeros((2 * tiles, LANES), F32)
    extras = []
    places = jnp.zeros((2 * members, LANES), F32)
    for tile in range(tiles):
        row = relative[tile : tile + 1]
        here = onehot(members, row)
        counts = dot(here, counter)
        rank = jnp.sum(here.astype(F32) * (counts[:, :LANES] + carry), axis=0, keepdims=True)
        carry = carry + counts[:, LANES:]
        slot = row * cap + rank
        slot_ref[tile : tile + 1, :] = slot
        both = jnp.concatenate(
            [here * place_high[tile : tile + 1].astype(BF16), here * place_low[tile : tile + 1].astype(BF16)], axis=0
        )
        places = places + dot_t(both, onehot(LANES, rank))
        slot_high = jnp.floor(slot * (1.0 / LANES))
        inverse_sum += invert_step(slot_high, slot - LANES * slot_high, float(tile), tiles)
        extra = iota((16, LANES), 0)
        extra = jnp.where(
            extra == 0, place_high[tile : tile + 1], jnp.where(extra == 1, place_low[tile : tile + 1], 0.0)
        )
        extras.append(extra)
    source_ref[...] = LANES * inverse_sum[:tiles] + inverse_sum[tiles:]
    places = jnp.where(iota((members, LANES), 1) < cap, LANES * places[:members] + places[members:], -1.0)
    for member in range(members):
        pos_send[member] = places[member : member + 1]
    pos_recv[members - 1] = places[members - 1 : members]

    load_drop.wait()
    for tile in range(tiles):
        block, lanes = tile // 2, pl.ds((tile % 2) * LANES, LANES)
        values = drop_v[:, tile * LANES : (tile + 1) * LANES]
        most = jnp.maximum(jnp.max(jnp.abs(values), axis=0, keepdims=True), 2.0**-100)
        power = jnp.ceil(jnp.log2(most) - 14.99)
        code = jnp.floor(values * jnp.exp2(-power) + 0.5)
        upper = jnp.floor(code * (1.0 / 256.0))
        data[block, 0:sides, lanes] = upper.astype(BF16)
        data[block, sides : 2 * sides, lanes] = (code - 256.0 * upper).astype(BF16)
        extra = jnp.where(iota((16, LANES), 0) == 2, power, extras[tile])
        data[block, 2 * sides : 2 * sides + 16, lanes] = extra.astype(BF16)

    pl.semaphore_wait(barrier, members)

    def dummy(src, dst, send, recv):
        return pltpu.make_async_remote_copy(
            src_ref=src,
            dst_ref=dst,
            send_sem=send,
            recv_sem=recv,
            device_id={"wide": me},
            device_id_type=MESH,
        )

    def ahead(chunk):
        return pltpu.make_async_remote_copy(
            src_ref=pos_send.at[chunk],
            dst_ref=pos_recv.at[chunk],
            send_sem=pos_send_sem,
            recv_sem=pos_recv_sem,
            device_id={"wide": lax.rem(me + 1 + chunk, members)},
            device_id_type=MESH,
        )

    def go_ahead(chunk, _):
        ahead(chunk).start()
        return 0

    lax.fori_loop(0, members - 1, go_ahead, 0)

    load_top.wait()
    load_tc.wait()
    core_top = pltpu.make_async_remote_copy(
        src_ref=top_inv_f32.at[leaf],
        dst_ref=top_inv_f32.at[leaf],
        send_sem=core_send.at[0],
        recv_sem=core_recv.at[0],
        device_id={"leaf": 1 - leaf},
        device_id_type=MESH,
    )
    core_tc = pltpu.make_async_remote_copy(
        src_ref=top_coup.at[leaf],
        dst_ref=top_coup.at[leaf],
        send_sem=core_send.at[1],
        recv_sem=core_recv.at[1],
        device_id={"leaf": 1 - leaf},
        device_id_type=MESH,
    )
    core_top.start()
    core_tc.start()

    def there(chunk):
        return pltpu.make_async_remote_copy(
            src_ref=send_buf.at[chunk],
            dst_ref=recv_buf.at[chunk],
            send_sem=there_send,
            recv_sem=there_recv.at[chunk // chunks],
            device_id={"wide": lax.rem(me + 1 + chunk, members)},
            device_id_type=MESH,
        )

    def back(chunk):
        return pltpu.make_async_remote_copy(
            src_ref=back_send.at[chunk],
            dst_ref=back_recv.at[chunk],
            send_sem=back_send_sem,
            recv_sem=back_recv_sem.at[chunk // chunks],
            device_id={"wide": lax.rem(me - 1 - chunk + 2 * members, members)},
            device_id_type=MESH,
        )

    def start_group(copy, group):
        last = (group + 1) * chunks
        if group == groups - 1:
            last -= 1

        def begin(chunk, _):
            copy(chunk).start()
            return 0

        lax.fori_loop(group * chunks, last, begin, 0)

    def wait_group(buf, sem, group, dst=True):
        count = chunks - 1 if group == groups - 1 else chunks
        part = buf.at[pl.ds(group * chunks, count)]
        pltpu.make_async_remote_copy(
            src_ref=part,
            dst_ref=part,
            send_sem=there_send,
            recv_sem=sem.at[group],
            device_id={"wide": me},
            device_id_type=MESH,
        ).wait_recv()

    own_there = pltpu.make_async_copy(
        send_buf.at[members - 1], recv_buf.at[members - 1], local_sem.at[0]
    )
    own_back = pltpu.make_async_copy(
        back_send.at[members - 1], back_recv.at[members - 1], local_sem.at[1]
    )

    def store_chunks(buf, first, block):
        for piece in range(TILE // 16):
            at = first + piece
            buf[at // 3, pl.ds(pl.multiple_of((at % 3) * 16, 16), 16), :] = block[
                piece * 16 : (piece + 1) * 16
            ]

    for group in range(groups):
        for pair in range(group * group_pairs, (group + 1) * group_pairs):
            block = pick(data, row_pair(source_ref, pair))
            code = jnp.concatenate(
                [256.0 * block[:sides] + block[sides : 2 * sides], block[2 * sides :]], axis=0
            )
            code = turned(code).astype(jnp.int32).astype(jnp.int16)
            store_chunks(send_buf, pair * (TILE // 16), code)
        start_group(there, group)
    own_there.start()

    load_inverse.wait()

    def halves(node, _):
        high, low = split(inverse_v[node])
        inv_high[node] = high
        inv_low[node] = low
        return 0

    lax.fori_loop(0, nodes, halves, 0)
    core_top.wait()
    core_tc.wait()
    for half in range(2):
        high, low = split(top_inv_f32[half])
        top_inv_high[half] = high
        top_inv_low[half] = low

    arrived = pos_recv.at[pl.ds(0, members - 1)]
    dummy(arrived, arrived, pos_send_sem, pos_recv_sem).wait_recv()
    lane = iota((1, LANES), 1)
    second = (lane >= LANES // 2).astype(F32)
    offset = lane.astype(F32) - second * (LANES // 2)
    inverse_sum = jnp.zeros((2 * tiles, LANES), F32)
    for member in range(members // 2):
        other = pltpu.roll(pos_recv[member + members // 2], LANES // 2, 1)
        place = jnp.where(lane < LANES // 2, pos_recv[member], other)
        high = jnp.floor(place * (1.0 / LANES))
        first = onehot(tiles, high).astype(F32)
        left = jnp.concatenate([first * (second * (members // 2) + float(member)), first * offset], axis=0)
        inverse_sum += dot_t(left.astype(BF16), onehot(LANES, place - LANES * high))
    source_ref[...] = cap * inverse_sum[:tiles] + inverse_sum[tiles:]
    make_choosers(source_ref, choose_in, high_in)
    make_choosers(slot_ref, choose_last, high_last)

    for group in range(groups):
        wait_group(recv_buf, there_recv, group)
        if group == groups - 1:
            own_there.wait()
        for tile in range(group_tiles):
            at = group * group_tiles + tile
            first = group * chunks + (tile * LANES) // cap
            last = group * chunks + ((tile + 1) * LANES - 1) // cap
            skip = (tile * LANES) % cap
            block = recv_buf[first : last + 1].astype(jnp.int32).astype(F32)
            columns = block.reshape((last + 1 - first) * cap, LANES)[skip : skip + LANES].T
            place_ref[at : at + 1, :] = LANES * columns[sides : sides + 1] + columns[sides + 1 : sides + 2]
            values = columns[:sides] * jnp.exp2(columns[sides + 2 : sides + 3])
            high, low = split(values)
            lanes = pl.ds((tile % 2) * LANES, LANES)
            turned_in[tile // 2, :sides, lanes] = high
            turned_in[tile // 2, sides:, lanes] = low

        for pair in range(pairs):
            span = pl.ds(pair * TILE, TILE)
            before = super_n[:, span] if group > 0 else None
            super_n[:, span] = merge(
                turned_in, choose_in[pair], high_in[pair : pair + 1], group * group_pairs, before
            )

    for node in range(nodes):
        span = pl.ds(node * width, width)
        side = super_n[:, span].astype(BF16)
        value = dot(side, inv_high[node])
        value = value[:sides] + value[sides:] + dot(side[:sides], inv_low[node])
        low_solved[:, span] = value
        low_half[:, span] = value.astype(BF16)

    load_coupling.wait()

    def half_sum(half):
        return dot(low_half[...], coupling_v[:, pl.ds(pl.multiple_of(half * width, LANES), width)])

    half_send[...] = half_sum(1 - leaf)
    core_half = pltpu.make_async_remote_copy(
        src_ref=half_send,
        dst_ref=half_recv,
        send_sem=core_send.at[3],
        recv_sem=core_recv.at[3],
        device_id={"leaf": 1 - leaf},
        device_id_type=MESH,
    )
    core_half.start()
    first = jnp.where(me == 0, 1.0, 0.0).astype(F32)
    partial[...] = half_sum(leaf) - top_sides_ref[...] * first
    core_half.wait()
    partial[...] = partial[...] + half_recv[...]
    for owner in range(owners):
        rs_send[owner] = partial[owner * own_rows : (owner + 1) * own_rows, :]

    def owner_chip(owner):
        line = owner // 3
        return 4 * line + lax.rem(owner - 3 * line + line + line // 4, 4)

    my_line = me // 4
    my_turn = lax.rem(me - 4 * my_line + 8 * members - my_line - my_line // 4, 4)
    is_owner = my_turn < 3
    my_owner = 3 * my_line + jnp.minimum(my_turn, 2)

    def rs_copy(owner):
        chip = owner_chip(owner)
        return pltpu.make_async_remote_copy(
            src_ref=rs_send.at[owner],
            dst_ref=rs_recv.at[lax.rem(chip - me - 1 + members, members)],
            send_sem=rs_send_sem,
            recv_sem=rs_recv_sem,
            device_id={"wide": chip},
            device_id_type=MESH,
        )

    def send_part(step, _):
        owner = lax.rem(my_owner + step, owners)

        @pl.when(owner_chip(owner) != me)
        def _():
            rs_copy(owner).start()

        return 0

    lax.fori_loop(0, owners, send_part, 0)
    make_choosers(place_ref, choose_out, high_out)

    def ag_copy(step):
        return pltpu.make_async_remote_copy(
            src_ref=ag_send,
            dst_ref=ag_recv.at[my_owner],
            send_sem=ag_send_sem,
            recv_sem=ag_recv_sem,
            device_id={"wide": lax.rem(me + step, members)},
            device_id_type=MESH,
        )

    @pl.when(is_owner)
    def _():
        rs_recv[members - 1] = rs_send[my_owner]
        arrived = rs_recv.at[pl.ds(0, members - 1)]
        dummy(arrived, arrived, rs_send_sem, rs_recv_sem).wait_recv()
        pair_buf[leaf] = jnp.sum(rs_recv[...], axis=0)
        swap = pltpu.make_async_remote_copy(
            src_ref=pair_buf.at[leaf],
            dst_ref=pair_buf.at[leaf],
            send_sem=core_send.at[2],
            recv_sem=core_recv.at[2],
            device_id={"leaf": 1 - leaf},
            device_id_type=MESH,
        )
        swap.start()
        swap.wait()

        def times(product, x, half):
            high, low = split(x)
            return (
                product(high, top_inv_high[half])
                + product(low, top_inv_high[half])
                + product(high, top_inv_low[half])
            )

        solved0 = times(dot, -pair_buf[0], 0)
        solved1 = times(dot, -pair_buf[1] - dot(solved0.astype(BF16), top_coup[1]), 1)
        answer1 = times(dot_t, solved1, 1)
        answer0 = times(dot_t, solved0 - dot_t(answer1.astype(BF16), top_coup[1]), 0)
        ag_send[...] = jnp.where(leaf == 0, answer0, answer1)
        ag_recv[my_owner] = ag_send[...]

        def tell(step, _):
            ag_copy(step).start()
            return 0

        lax.fori_loop(1, members, tell, 0)
        arrived = ag_recv.at[pl.ds(0, owners - 1)]
        dummy(arrived, arrived, ag_send_sem, ag_recv_sem).wait_recv()

    @pl.when(jnp.logical_not(is_owner))
    def _():
        dummy(ag_recv, ag_recv, ag_send_sem, ag_recv_sem).wait_recv()

    for owner in range(owners):
        top_out_ref[owner * own_rows : (owner + 1) * own_rows, :] = ag_recv[owner]
    sol_half[leaf] = top_out_ref[...].astype(BF16)
    core_sol = pltpu.make_async_remote_copy(
        src_ref=sol_half.at[leaf],
        dst_ref=sol_half.at[leaf],
        send_sem=core_send.at[4],
        recv_sem=core_recv.at[4],
        device_id={"leaf": 1 - leaf},
        device_id_type=MESH,
    )
    core_sol.start()
    core_sol.wait()

    for node in range(nodes):
        span = pl.ds(node * width, width)
        rows_here = slice(node * width, (node + 1) * width)
        term = dot_t(sol_half[0], coupling_v[rows_here, :width]) + dot_t(sol_half[1], coupling_v[rows_here, width:])
        high, low = split(low_solved[:, span] - term)
        value = dot_t(jnp.concatenate([high, low], axis=0), inv_high[node])
        value = (value[:sides] + value[sides:] + dot_t(high, inv_low[node])).astype(BF16)
        for piece in range(width // LANES):
            at = node * width + piece * LANES
            low_final[at // TILE, :, pl.ds(at % TILE, LANES)] = value[:, piece * LANES : (piece + 1) * LANES]

    for group in range(groups):
        for pair in range(group * group_pairs, (group + 1) * group_pairs):
            block = merge(low_final, choose_out[pair], high_out[pair : pair + 1], 0, None)
            store_chunks(back_send, pair * (TILE // 16), turned(block).astype(BF16))
        start_group(back, group)
    own_back.start()

    for group in range(groups):
        wait_group(back_recv, back_recv_sem, group)
        if group == groups - 1:
            own_back.wait()
        block = back_recv[group * chunks : (group + 1) * chunks].reshape(group_rows, LANES)
        for tile in range(group_tiles):
            columns = block[tile * LANES : (tile + 1) * LANES].astype(F32).T
            turned_back[tile // 2, :, pl.ds((tile % 2) * LANES, LANES)] = columns[:sides].astype(BF16)

        for pair in range(pairs):
            span = pl.ds(pair * TILE, TILE)
            before = out_sum[:, span] if group > 0 else None
            value = merge(
                turned_back, choose_last[pair], high_last[pair : pair + 1], group * group_pairs, before
            )
            if group < groups - 1:
                out_sum[:, span] = value
            else:
                out_ref[:, span] = value.astype(BF16)

    sent = pos_send.at[pl.ds(0, members - 1)]
    dummy(sent, sent, pos_send_sem, pos_send_sem).wait_send()
    sent = send_buf.at[pl.ds(0, members - 1)]
    dummy(sent, sent, there_send, there_send).wait_send()
    sent = back_send.at[pl.ds(0, members - 1)]
    dummy(sent, sent, back_send_sem, back_send_sem).wait_send()

    @pl.when(is_owner)
    def _():
        part = rs_send.at[pl.ds(0, owners - 1)]
        dummy(part, part, rs_send_sem, rs_send_sem).wait_send()
        part = rs_recv.at[pl.ds(0, members - 1)]
        dummy(part, part, ag_send_sem, ag_send_sem).wait_send()

    @pl.when(jnp.logical_not(is_owner))
    def _():
        dummy(rs_send, rs_send, rs_send_sem, rs_send_sem).wait_send()


def widen(low_ref, top_ref, out_ref, top_out_ref):
    out_ref[...] = low_ref[...].astype(F32)

    @pl.when(pl.program_id(0) == 0)
    def _():
        top_out_ref[...] = top_ref[...]


def shards(drop_sides, super_index, low_inverse, coupling, top_sides, top_inverse, top_coupling):
    sides, rows = drop_sides.shape
    nodes, width, _ = low_inverse.shape
    members = lax.axis_size("wide")
    cap = rows // members
    owners = 48
    top_cols = coupling.shape[1]
    tiles = rows // LANES
    own = sides // owners
    vmem = pl.BlockSpec(memory_space=pltpu.VMEM)
    anyspace = pl.BlockSpec(memory_space=pl.ANY)
    dma = pltpu.SemaphoreType.DMA
    dims = (sides, rows, members, cap, nodes, width, owners)
    low, top = pl.pallas_call(
        functools.partial(kernel, dims),
        out_shape=(
            jax.ShapeDtypeStruct((sides, rows), BF16),
            jax.ShapeDtypeStruct(top_sides.shape, F32),
        ),
        in_specs=[vmem, anyspace, anyspace, anyspace, vmem, anyspace, anyspace],
        out_specs=(vmem, vmem),
        scratch_shapes=[
            pltpu.VMEM((nodes, width, width), F32),
            pltpu.VMEM((rows, top_cols), BF16),
            pltpu.VMEM((2, width, width), F32),
            pltpu.VMEM((2, width, width), BF16),
            pltpu.VMEM((2, width, width), BF16),
            pltpu.VMEM((2, width, width), BF16),
            pltpu.VMEM((nodes, width, width), BF16),
            pltpu.VMEM((nodes, width, width), BF16),
            pltpu.VMEM((tiles, LANES), F32),
            pltpu.VMEM((tiles, LANES), F32),
            pltpu.VMEM((tiles, LANES), F32),
            pltpu.VMEM((sides, rows), F32),
            pltpu.VMEM((rows // TILE, 2 * sides + 16, TILE), BF16),
            pltpu.VMEM((rows // TILE // 4, 2 * sides, TILE), BF16),
            pltpu.VMEM((members, 1, LANES), F32),
            pltpu.VMEM((members, 1, LANES), F32),
            pltpu.VMEM((rows // TILE, TILE, TILE), BF16),
            pltpu.VMEM((rows // TILE, TILE, TILE), BF16),
            pltpu.VMEM((rows // TILE, TILE, TILE), BF16),
            pltpu.VMEM((rows // TILE, TILE), F32),
            pltpu.VMEM((rows // TILE, TILE), F32),
            pltpu.VMEM((rows // TILE, TILE), F32),
            pltpu.VMEM((2 * sides, rows), F32),
            pltpu.VMEM((sides, rows), F32),
            pltpu.VMEM((sides, rows), BF16),
            pltpu.VMEM((rows // TILE, sides, TILE), BF16),
            pltpu.VMEM((rows // TILE // 4, sides, TILE), BF16),
            pltpu.VMEM((sides, rows), F32),
            pltpu.VMEM((members, cap, LANES), jnp.int16),
            pltpu.VMEM((members, cap, LANES), jnp.int16),
            pltpu.VMEM((members, cap, LANES), BF16),
            pltpu.VMEM((members, cap, LANES), BF16),
            pltpu.VMEM((sides, width), F32),
            pltpu.VMEM((sides, width), F32),
            pltpu.VMEM((sides, width), F32),
            pltpu.VMEM((owners, own, width), F32),
            pltpu.VMEM((members, own, width), F32),
            pltpu.VMEM((2, own, width), F32),
            pltpu.VMEM((own, width), F32),
            pltpu.VMEM((owners, own, width), F32),
            pltpu.VMEM((2, sides, width), BF16),
            dma((5,)),
            dma((5,)),
            dma((5,)),
            dma((4,)),
            dma,
            dma((4,)),
            dma,
            dma,
            dma,
            dma((4,)),
            dma,
            dma,
            dma,
            dma,
        ],
        compiler_params=pltpu.CompilerParams(
            collective_id=0, has_side_effects=True, vmem_limit_bytes=56 << 20
        ),
        name="substitution",
    )(
        super_index.reshape(tiles, LANES),
        drop_sides,
        low_inverse,
        coupling,
        top_sides,
        top_inverse,
        top_coupling,
    )
    return pl.pallas_call(
        widen,
        grid=(4,),
        out_shape=(jax.ShapeDtypeStruct((sides, rows), F32), jax.ShapeDtypeStruct(top_sides.shape, F32)),
        in_specs=[
            pl.BlockSpec((sides, rows // 4), lambda at: (0, at)),
            pl.BlockSpec(top_sides.shape, lambda at: (0, 0)),
        ],
        out_specs=(
            pl.BlockSpec((sides, rows // 4), lambda at: (0, at)),
            pl.BlockSpec(top_sides.shape, lambda at: (0, 0)),
        ),
        name="widen",
    )(low, top)


def solution(mesh):
    placed = (
        P(None, ("leaf", "wide")),
        P(("leaf", "wide")),
        P(("leaf", "wide"), None, None),
        P(("leaf", "wide"), None),
        P(None, "leaf"),
        P("leaf", None, None),
        P(None, "leaf", None, None),
    )
    return jax.shard_map(
        shards,
        mesh=mesh,
        in_specs=placed,
        out_specs=(P(None, ("leaf", "wide")), P(None, "leaf")),
        check_vma=False,
    )
```

```python
import functools
import random

import jax
import jax.numpy as jnp
from jax import lax
from jax.experimental import pallas as pl
from jax.experimental.pallas import tpu as pltpu
from jax.sharding import PartitionSpec as P

MESH = pl.DeviceIdType.MESH
F32 = jnp.float32
BF16 = jnp.bfloat16
LANES = 128
TILE = 256


def order_of_partners():
    steps = [(z, y, x) for z in range(4) for y in range(4) for x in range(4)][1:]
    random.Random(2).shuffle(steps)
    return sorted(steps, key=lambda step: -sum((0, 1, 2, 1)[one] for one in step)) + [(0, 0, 0)]


ORDER = order_of_partners()


def dot(a, b):
    return jnp.dot(a, b, preferred_element_type=F32)


def dot_t(a, b):
    return lax.dot_general(a, b, (((1,), (1,)), ((), ())), preferred_element_type=F32)


def split(x):
    high = x.astype(BF16)
    return high, (x - high.astype(F32)).astype(BF16)


def iota(shape, dim):
    return lax.broadcasted_iota(jnp.int32, shape, dim)


def onehot(rows, values):
    shape = (rows, values.shape[1])
    match = iota(shape, 0).astype(F32) == jnp.broadcast_to(values, shape)
    return jnp.where(match, 1.0, 0.0).astype(BF16)


def invert_step(high, low, place, rows):
    first = onehot(rows, high).astype(F32)
    lane = iota((rows, LANES), 1).astype(F32)
    left = jnp.concatenate([first * place, first * lane], axis=0).astype(BF16)
    return dot_t(left, onehot(LANES, low))


def pick(data_ref, source):
    blocks, height, _ = data_ref.shape
    high = jnp.floor(source * (1.0 / TILE))
    chooser = onehot(TILE, source - TILE * high)
    parts = dot(data_ref[...].reshape(blocks * height, TILE), chooser)
    result = parts[:height]
    for block in range(1, blocks):
        part = parts[block * height : (block + 1) * height]
        result = jnp.where(jnp.broadcast_to(high == float(block), part.shape), part, result)
    return result


def merge(data_ref, chooser, high, blocks, result):
    count, height, _ = data_ref.shape
    parts = dot(data_ref[...].reshape(count * height, TILE), chooser)
    for at in range(count):
        part = parts[at * height : (at + 1) * height]
        if result is None:
            result = part
        else:
            result = jnp.where(jnp.broadcast_to(high == float(blocks + at), part.shape), part, result)
    return result


def make_choosers(ref, chooser_ref, high_ref):
    def one(pair, _):
        source = row_pair(ref, pair)
        high = jnp.floor(source * (1.0 / TILE))
        chooser_ref[pair] = onehot(TILE, source - TILE * high)
        high_ref[pl.ds(pair, 1), :] = high
        return 0

    lax.fori_loop(0, chooser_ref.shape[0], one, 0)


def row_pair(ref, pair):
    two = ref[pl.ds(2 * pair, 2), :]
    return jnp.concatenate([two[0:1], two[1:2]], axis=1)


def turned(x):
    height = x.shape[0]
    if height < LANES:
        x = jnp.concatenate([x, jnp.zeros((LANES - height, x.shape[1]), x.dtype)], axis=0)
    return x.T


def kernel(
    dims,
    index_any,
    drop_any,
    inverse_any,
    coupling_any,
    top_sides_any,
    top_inverse_any,
    top_coupling_any,
    out_any,
    top_out_any,
    index_v,
    top_sides_v,
    out_v,
    top_out_v,
    here_ref,
    left_slot,
    right_slot,
    left_place,
    right_place,
    inverse_v,
    coupling_v,
    top_inv_f32,
    top_inv_high,
    top_inv_low,
    top_coup,
    inv_high,
    inv_low,
    slot_ref,
    source_ref,
    place_ref,
    drop_v,
    data,
    turned_in,
    pos_send,
    pos_recv,
    choose_in,
    choose_out,
    choose_last,
    high_in,
    high_out,
    high_last,
    super_n,
    low_solved,
    low_half,
    low_final,
    turned_back,
    out_sum,
    send_buf,
    recv_buf,
    back_send,
    back_recv,
    partial,
    half_send,
    half_recv,
    rs_send,
    rs_recv,
    pair_buf,
    ag_send,
    ag_recv,
    sol_half,
    load_sem,
    core_send,
    core_recv,
    local_sem,
    there_send,
    there_recv,
    pos_send_sem,
    pos_recv_sem,
    back_send_sem,
    back_recv_sem,
    rs_send_sem,
    rs_recv_sem,
    ag_send_sem,
    ag_recv_sem,
    out_sem,
):
    sides, rows, members, cap, nodes, width, owners = dims
    tiles = rows // LANES
    pairs = rows // TILE
    groups = 4
    chunks = members // groups
    group_rows = rows // groups
    group_pairs = pairs // groups
    group_tiles = tiles // groups
    own_rows = sides // owners
    me = lax.axis_index("wide")
    leaf = lax.axis_index("leaf")
    my_z, my_y, my_x = me // 16, lax.rem(me // 4, 4), lax.rem(me, 4)
    z_at = [16 * lax.rem(my_z + step, 4) for step in range(4)]
    y_at = [4 * lax.rem(my_y + step, 4) for step in range(4)]
    x_at = [lax.rem(my_x + step, 4) for step in range(4)]

    def partner(chunk):
        dz, dy, dx = ORDER[chunk]
        return z_at[dz] + y_at[dy] + x_at[dx]

    def origin(chunk):
        dz, dy, dx = ORDER[chunk]
        return z_at[(4 - dz) % 4] + y_at[(4 - dy) % 4] + x_at[(4 - dx) % 4]


    barrier = pltpu.get_barrier_semaphore()

    def greet(step, _):
        pl.semaphore_signal(
            barrier,
            inc=1,
            device_id={"wide": lax.rem(me + step, members)},
            device_id_type=MESH,
        )
        return 0

    lax.fori_loop(1, members, greet, 0)
    pl.semaphore_signal(barrier, inc=1, device_id={"leaf": 1 - leaf}, device_id_type=MESH)

    load_index = pltpu.make_async_copy(index_any, index_v, load_sem.at[5])
    load_sides = pltpu.make_async_copy(top_sides_any, top_sides_v, load_sem.at[6])
    load_drop = pltpu.make_async_copy(drop_any, drop_v, load_sem.at[4])
    load_inverse = pltpu.make_async_copy(inverse_any, inverse_v, load_sem.at[0])
    load_coupling = pltpu.make_async_copy(coupling_any, coupling_v, load_sem.at[1])
    load_top = pltpu.make_async_copy(top_inverse_any.at[0], top_inv_f32.at[leaf], load_sem.at[2])
    load_tc = pltpu.make_async_copy(top_coupling_any.at[0, 0], top_coup.at[leaf], load_sem.at[3])
    load_index.start()
    load_drop.start()
    load_inverse.start()
    load_coupling.start()
    load_top.start()
    load_tc.start()
    load_sides.start()

    order = jnp.zeros((members, LANES), F32)
    chunk_of = iota((members, LANES), 0)
    for chunk, (dz, dy, dx) in enumerate(ORDER):
        order = jnp.where(chunk_of == chunk, float(16 * dz + 4 * dy + dx), order)
    begin = (cap * chunk_of).astype(F32)
    below = (iota((LANES, LANES), 0) < iota((LANES, LANES), 1)).astype(F32)
    counter = jnp.concatenate([below, jnp.ones((LANES, LANES), F32)], axis=1).astype(BF16)
    load_index.wait()
    local = index_v[...] - leaf * (members * rows)
    target = ((local.astype(F32) + 0.5) * (1.0 / rows)).astype(jnp.int32)
    position = (local - target * rows).astype(F32)
    step_of = (
        16 * (((target >> 4) - my_z) & 3) + 4 * (((target >> 2) - my_y) & 3) + ((target - my_x) & 3)
    ).astype(F32)
    place_high = jnp.floor(position * (1.0 / LANES))
    place_low = position - LANES * place_high

    def here_of(tile):
        return jnp.where(order == step_of[tile : tile + 1], 1.0, 0.0)

    for tile in range(tiles):
        here_ref[tile * members : (tile + 1) * members, :] = here_of(tile).astype(BF16)
    counts = dot(here_ref[...], counter)
    carry = jnp.zeros((members, LANES), F32)
    lane = iota((tiles, LANES), 1).astype(F32)
    extras = []
    for tile in range(tiles):
        here = here_of(tile)
        count = counts[tile * members : (tile + 1) * members]
        rank = jnp.sum(here * (count[:, :LANES] + carry), axis=0, keepdims=True)
        slot = rank + jnp.sum(here * begin, axis=0, keepdims=True)
        carry = carry + count[:, LANES:]
        slot_ref[tile : tile + 1, :] = slot
        slot_high = jnp.floor(slot * (1.0 / LANES))
        span = pl.ds(tile * LANES, LANES)
        first = onehot(tiles, slot_high).astype(F32)
        left_slot[:, span] = jnp.concatenate([first * float(tile), first * lane], axis=0).astype(BF16)
        right_slot[:, span] = onehot(LANES, slot - LANES * slot_high)
        left_place[:, span] = jnp.concatenate(
            [here * place_high[tile : tile + 1], here * place_low[tile : tile + 1]], axis=0
        ).astype(BF16)
        right_place[:, span] = onehot(LANES, rank)
        extra = iota((16, LANES), 0)
        extras.append(
            jnp.where(
                extra == 0, place_high[tile : tile + 1], jnp.where(extra == 1, place_low[tile : tile + 1], 0.0)
            )
        )
    inverse_sum = dot_t(left_slot[...], right_slot[...])
    source_ref[...] = LANES * inverse_sum[:tiles] + inverse_sum[tiles:]
    places = dot_t(left_place[...], right_place[...])
    places = jnp.where(iota((members, LANES), 1) < cap, LANES * places[:members] + places[members:], -1.0)
    for member in range(members):
        pos_send[member] = places[member : member + 1]
    pos_recv[members - 1] = places[members - 1 : members]

    load_drop.wait()
    for tile in range(tiles):
        block, lanes = tile // 2, pl.ds((tile % 2) * LANES, LANES)
        values = drop_v[:, tile * LANES : (tile + 1) * LANES]
        most = jnp.maximum(jnp.max(jnp.abs(values), axis=0, keepdims=True), 2.0**-100)
        power = jnp.ceil(jnp.log2(most) - 14.99)
        code = jnp.floor(values * jnp.exp2(-power) + 0.5)
        upper = jnp.floor(code * (1.0 / 256.0))
        data[block, 0:sides, lanes] = upper.astype(BF16)
        data[block, sides : 2 * sides, lanes] = (code - 256.0 * upper).astype(BF16)
        extra = jnp.where(iota((16, LANES), 0) == 2, power, extras[tile])
        data[block, 2 * sides : 2 * sides + 16, lanes] = extra.astype(BF16)

    pl.semaphore_wait(barrier, members)

    def dummy(src, dst, send, recv):
        return pltpu.make_async_remote_copy(
            src_ref=src,
            dst_ref=dst,
            send_sem=send,
            recv_sem=recv,
            device_id={"wide": me},
            device_id_type=MESH,
        )

    def ahead(chunk):
        return pltpu.make_async_remote_copy(
            src_ref=pos_send.at[chunk],
            dst_ref=pos_recv.at[chunk],
            send_sem=pos_send_sem,
            recv_sem=pos_recv_sem,
            device_id={"wide": partner(chunk)},
            device_id_type=MESH,
        )

    for chunk in range(members - 1):
        ahead(chunk).start()

    load_top.wait()
    load_tc.wait()
    core_top = pltpu.make_async_remote_copy(
        src_ref=top_inv_f32.at[leaf],
        dst_ref=top_inv_f32.at[leaf],
        send_sem=core_send.at[0],
        recv_sem=core_recv.at[0],
        device_id={"leaf": 1 - leaf},
        device_id_type=MESH,
    )
    core_tc = pltpu.make_async_remote_copy(
        src_ref=top_coup.at[leaf],
        dst_ref=top_coup.at[leaf],
        send_sem=core_send.at[1],
        recv_sem=core_recv.at[1],
        device_id={"leaf": 1 - leaf},
        device_id_type=MESH,
    )
    core_top.start()
    core_tc.start()

    def there(chunk):
        return pltpu.make_async_remote_copy(
            src_ref=send_buf.at[chunk],
            dst_ref=recv_buf.at[chunk],
            send_sem=there_send,
            recv_sem=there_recv.at[chunk // chunks],
            device_id={"wide": partner(chunk)},
            device_id_type=MESH,
        )

    def back(chunk):
        return pltpu.make_async_remote_copy(
            src_ref=back_send.at[chunk],
            dst_ref=back_recv.at[chunk],
            send_sem=back_send_sem,
            recv_sem=back_recv_sem.at[chunk // chunks],
            device_id={"wide": origin(chunk)},
            device_id_type=MESH,
        )

    def start_group(copy, group):
        last = (group + 1) * chunks
        if group == groups - 1:
            last -= 1

        for chunk in range(group * chunks, last):
            copy(chunk).start()

    def wait_group(buf, sem, group, dst=True):
        count = chunks - 1 if group == groups - 1 else chunks
        part = buf.at[pl.ds(group * chunks, count)]
        pltpu.make_async_remote_copy(
            src_ref=part,
            dst_ref=part,
            send_sem=there_send,
            recv_sem=sem.at[group],
            device_id={"wide": me},
            device_id_type=MESH,
        ).wait_recv()

    own_there = pltpu.make_async_copy(
        send_buf.at[members - 1], recv_buf.at[members - 1], local_sem.at[0]
    )
    own_back = pltpu.make_async_copy(
        back_send.at[members - 1], back_recv.at[members - 1], local_sem.at[1]
    )

    def store_chunks(buf, first, block):
        for piece in range(TILE // 16):
            at = first + piece
            buf[at // 3, pl.ds(pl.multiple_of((at % 3) * 16, 16), 16), :] = block[
                piece * 16 : (piece + 1) * 16
            ]

    for group in range(groups):
        for pair in range(group * group_pairs, (group + 1) * group_pairs):
            block = pick(data, row_pair(source_ref, pair))
            code = jnp.concatenate(
                [256.0 * block[:sides] + block[sides : 2 * sides], block[2 * sides :]], axis=0
            )
            code = turned(code).astype(jnp.int32).astype(jnp.int16)
            store_chunks(send_buf, pair * (TILE // 16), code)
        start_group(there, group)
    own_there.start()

    load_inverse.wait()

    def halves(node, _):
        high, low = split(inverse_v[node])
        inv_high[node] = high
        inv_low[node] = low
        return 0

    lax.fori_loop(0, nodes, halves, 0)
    core_top.wait()
    core_tc.wait()
    for half in range(2):
        high, low = split(top_inv_f32[half])
        top_inv_high[half] = high
        top_inv_low[half] = low

    arrived = pos_recv.at[pl.ds(0, members - 1)]
    dummy(arrived, arrived, pos_send_sem, pos_recv_sem).wait_recv()
    lane = iota((1, LANES), 1)
    second = (lane >= LANES // 2).astype(F32)
    offset = lane.astype(F32) - second * (LANES // 2)
    inverse_sum = jnp.zeros((2 * tiles, LANES), F32)
    for member in range(members // 2):
        other = pltpu.roll(pos_recv[member + members // 2], LANES // 2, 1)
        place = jnp.where(lane < LANES // 2, pos_recv[member], other)
        high = jnp.floor(place * (1.0 / LANES))
        first = onehot(tiles, high).astype(F32)
        left = jnp.concatenate([first * (second * (members // 2) + float(member)), first * offset], axis=0)
        inverse_sum += dot_t(left.astype(BF16), onehot(LANES, place - LANES * high))
    source_ref[...] = cap * inverse_sum[:tiles] + inverse_sum[tiles:]
    make_choosers(source_ref, choose_in, high_in)
    make_choosers(slot_ref, choose_last, high_last)

    for group in range(groups):
        wait_group(recv_buf, there_recv, group)
        if group == groups - 1:
            own_there.wait()
        for tile in range(group_tiles):
            at = group * group_tiles + tile
            first = group * chunks + (tile * LANES) // cap
            last = group * chunks + ((tile + 1) * LANES - 1) // cap
            skip = (tile * LANES) % cap
            block = recv_buf[first : last + 1].astype(jnp.int32).astype(F32)
            columns = block.reshape((last + 1 - first) * cap, LANES)[skip : skip + LANES].T
            place_ref[at : at + 1, :] = LANES * columns[sides : sides + 1] + columns[sides + 1 : sides + 2]
            values = columns[:sides] * jnp.exp2(columns[sides + 2 : sides + 3])
            high, low = split(values)
            lanes = pl.ds((tile % 2) * LANES, LANES)
            turned_in[tile // 2, :sides, lanes] = high
            turned_in[tile // 2, sides:, lanes] = low

        for pair in range(pairs):
            span = pl.ds(pair * TILE, TILE)
            before = super_n[:, span] if group > 0 else None
            super_n[:, span] = merge(
                turned_in, choose_in[pair], high_in[pair : pair + 1], group * group_pairs, before
            )

    for node in range(nodes):
        span = pl.ds(node * width, width)
        side = super_n[:, span].astype(BF16)
        value = dot(side, inv_high[node])
        value = value[:sides] + value[sides:] + dot(side[:sides], inv_low[node])
        low_solved[:, span] = value
        low_half[:, span] = value.astype(BF16)

    load_coupling.wait()

    def half_sum(half):
        return dot(low_half[...], coupling_v[:, pl.ds(pl.multiple_of(half * width, LANES), width)])

    half_send[...] = half_sum(1 - leaf)
    core_half = pltpu.make_async_remote_copy(
        src_ref=half_send,
        dst_ref=half_recv,
        send_sem=core_send.at[3],
        recv_sem=core_recv.at[3],
        device_id={"leaf": 1 - leaf},
        device_id_type=MESH,
    )
    core_half.start()
    first = jnp.where(me == 0, 1.0, 0.0).astype(F32)
    load_sides.wait()
    partial[...] = half_sum(leaf) - top_sides_v[...] * first
    core_half.wait()
    partial[...] = partial[...] + half_recv[...]
    for owner in range(owners):
        rs_send[owner] = partial[owner * own_rows : (owner + 1) * own_rows, :]

    def turn_of(chip):
        line = chip // 4
        return lax.rem(chip - 4 * line + 8 * members - line - line // 4, 4)

    my_turn = turn_of(me)
    is_owner = my_turn < 3
    my_owner = 3 * (me // 4) + jnp.minimum(my_turn, 2)

    def send_part(chunk):
        chip = partner(chunk)
        turn = turn_of(chip)

        @pl.when(turn < 3)
        def _():
            pltpu.make_async_remote_copy(
                src_ref=rs_send.at[3 * (chip // 4) + jnp.minimum(turn, 2)],
                dst_ref=rs_recv.at[chunk],
                send_sem=rs_send_sem,
                recv_sem=rs_recv_sem,
                device_id={"wide": chip},
                device_id_type=MESH,
            ).start()

    for chunk in range(members - 1):
        send_part(chunk)
    make_choosers(place_ref, choose_out, high_out)

    def ag_copy(chunk):
        return pltpu.make_async_remote_copy(
            src_ref=ag_send,
            dst_ref=ag_recv.at[my_owner],
            send_sem=ag_send_sem,
            recv_sem=ag_recv_sem,
            device_id={"wide": partner(chunk)},
            device_id_type=MESH,
        )

    @pl.when(is_owner)
    def _():
        rs_recv[members - 1] = rs_send[my_owner]
        arrived = rs_recv.at[pl.ds(0, members - 1)]
        dummy(arrived, arrived, rs_send_sem, rs_recv_sem).wait_recv()
        pair_buf[leaf] = jnp.sum(rs_recv[...], axis=0)
        swap = pltpu.make_async_remote_copy(
            src_ref=pair_buf.at[leaf],
            dst_ref=pair_buf.at[leaf],
            send_sem=core_send.at[2],
            recv_sem=core_recv.at[2],
            device_id={"leaf": 1 - leaf},
            device_id_type=MESH,
        )
        swap.start()
        swap.wait()

        def times(product, x, half):
            high, low = split(x)
            return (
                product(high, top_inv_high[half])
                + product(low, top_inv_high[half])
                + product(high, top_inv_low[half])
            )

        solved0 = times(dot, -pair_buf[0], 0)
        solved1 = times(dot, -pair_buf[1] - dot(solved0.astype(BF16), top_coup[1]), 1)
        answer1 = times(dot_t, solved1, 1)
        answer0 = times(dot_t, solved0 - dot_t(answer1.astype(BF16), top_coup[1]), 0)
        ag_send[...] = jnp.where(leaf == 0, answer0, answer1)
        ag_recv[my_owner] = ag_send[...]

        for chunk in range(members - 1):
            ag_copy(chunk).start()
        arrived = ag_recv.at[pl.ds(0, owners - 1)]
        dummy(arrived, arrived, ag_send_sem, ag_recv_sem).wait_recv()

    @pl.when(jnp.logical_not(is_owner))
    def _():
        dummy(ag_recv, ag_recv, ag_send_sem, ag_recv_sem).wait_recv()

    for owner in range(owners):
        top_out_v[owner * own_rows : (owner + 1) * own_rows, :] = ag_recv[owner]
    sol_half[leaf] = top_out_v[...].astype(BF16)
    core_sol = pltpu.make_async_remote_copy(
        src_ref=sol_half.at[leaf],
        dst_ref=sol_half.at[leaf],
        send_sem=core_send.at[4],
        recv_sem=core_recv.at[4],
        device_id={"leaf": 1 - leaf},
        device_id_type=MESH,
    )
    core_sol.start()
    store_top = pltpu.make_async_copy(top_out_v, top_out_any, local_sem.at[2])
    store_top.start()
    core_sol.wait()

    for node in range(nodes):
        span = pl.ds(node * width, width)
        rows_here = slice(node * width, (node + 1) * width)
        term = dot_t(sol_half[0], coupling_v[rows_here, :width]) + dot_t(sol_half[1], coupling_v[rows_here, width:])
        high, low = split(low_solved[:, span] - term)
        value = dot_t(jnp.concatenate([high, low], axis=0), inv_high[node])
        value = (value[:sides] + value[sides:] + dot_t(high, inv_low[node])).astype(BF16)
        for piece in range(width // LANES):
            at = node * width + piece * LANES
            low_final[at // TILE, :, pl.ds(at % TILE, LANES)] = value[:, piece * LANES : (piece + 1) * LANES]

    for group in range(groups):
        for pair in range(group * group_pairs, (group + 1) * group_pairs):
            block = merge(low_final, choose_out[pair], high_out[pair : pair + 1], 0, None)
            store_chunks(back_send, pair * (TILE // 16), turned(block).astype(BF16))
        start_group(back, group)
    own_back.start()

    def store_out(part):
        span = pl.ds(part * 3 * TILE, 3 * TILE)
        return pltpu.make_async_copy(out_v.at[:, span], out_any.at[:, span], out_sem.at[part])

    for group in range(groups):
        wait_group(back_recv, back_recv_sem, group)
        if group == groups - 1:
            own_back.wait()
        block = back_recv[group * chunks : (group + 1) * chunks].reshape(group_rows, LANES)
        for tile in range(group_tiles):
            columns = block[tile * LANES : (tile + 1) * LANES].astype(F32).T
            turned_back[tile // 2, :, pl.ds((tile % 2) * LANES, LANES)] = columns[:sides].astype(BF16)

        for pair in range(pairs):
            span = pl.ds(pair * TILE, TILE)
            before = out_sum[:, span] if group > 0 else None
            value = merge(
                turned_back, choose_last[pair], high_last[pair : pair + 1], group * group_pairs, before
            )
            if group < groups - 1:
                out_sum[:, span] = value
            else:
                out_v[:, span] = value.astype(BF16)
                if pair % 3 == 2:
                    store_out(pair // 3).start()

    store_top.wait()
    for part in range(pairs // 3):
        store_out(part).wait()
    sent = pos_send.at[pl.ds(0, members - 1)]
    dummy(sent, sent, pos_send_sem, pos_send_sem).wait_send()
    sent = send_buf.at[pl.ds(0, members - 1)]
    dummy(sent, sent, there_send, there_send).wait_send()
    sent = back_send.at[pl.ds(0, members - 1)]
    dummy(sent, sent, back_send_sem, back_send_sem).wait_send()

    @pl.when(is_owner)
    def _():
        part = rs_send.at[pl.ds(0, owners - 1)]
        dummy(part, part, rs_send_sem, rs_send_sem).wait_send()
        part = rs_recv.at[pl.ds(0, members - 1)]
        dummy(part, part, ag_send_sem, ag_send_sem).wait_send()

    @pl.when(jnp.logical_not(is_owner))
    def _():
        dummy(rs_send, rs_send, rs_send_sem, rs_send_sem).wait_send()


def widen(low_ref, top_ref, out_ref, top_out_ref):
    out_ref[...] = low_ref[...].astype(F32)

    @pl.when(pl.program_id(0) == 0)
    def _():
        top_out_ref[...] = top_ref[...]


def shards(drop_sides, super_index, low_inverse, coupling, top_sides, top_inverse, top_coupling):
    sides, rows = drop_sides.shape
    nodes, width, _ = low_inverse.shape
    members = lax.axis_size("wide")
    cap = rows // members
    owners = 48
    top_cols = coupling.shape[1]
    tiles = rows // LANES
    own = sides // owners
    anyspace = pl.BlockSpec(memory_space=pl.ANY)
    dma = pltpu.SemaphoreType.DMA
    dims = (sides, rows, members, cap, nodes, width, owners)
    low, top = pl.pallas_call(
        functools.partial(kernel, dims),
        out_shape=(
            jax.ShapeDtypeStruct((sides, rows), BF16),
            jax.ShapeDtypeStruct(top_sides.shape, F32),
        ),
        in_specs=[anyspace] * 7,
        out_specs=(anyspace, anyspace),
        scratch_shapes=[
            pltpu.VMEM((tiles, LANES), jnp.int32),
            pltpu.VMEM((sides, width), F32),
            pltpu.VMEM((sides, rows), BF16),
            pltpu.VMEM((sides, width), F32),
            pltpu.VMEM((tiles * members, LANES), BF16),
            pltpu.VMEM((2 * tiles, rows), BF16),
            pltpu.VMEM((LANES, rows), BF16),
            pltpu.VMEM((2 * members, rows), BF16),
            pltpu.VMEM((LANES, rows), BF16),
            pltpu.VMEM((nodes, width, width), F32),
            pltpu.VMEM((rows, top_cols), BF16),
            pltpu.VMEM((2, width, width), F32),
            pltpu.VMEM((2, width, width), BF16),
            pltpu.VMEM((2, width, width), BF16),
            pltpu.VMEM((2, width, width), BF16),
            pltpu.VMEM((nodes, width, width), BF16),
            pltpu.VMEM((nodes, width, width), BF16),
            pltpu.VMEM((tiles, LANES), F32),
            pltpu.VMEM((tiles, LANES), F32),
            pltpu.VMEM((tiles, LANES), F32),
            pltpu.VMEM((sides, rows), F32),
            pltpu.VMEM((rows // TILE, 2 * sides + 16, TILE), BF16),
            pltpu.VMEM((rows // TILE // 4, 2 * sides, TILE), BF16),
            pltpu.VMEM((members, 1, LANES), F32),
            pltpu.VMEM((members, 1, LANES), F32),
            pltpu.VMEM((rows // TILE, TILE, TILE), BF16),
            pltpu.VMEM((rows // TILE, TILE, TILE), BF16),
            pltpu.VMEM((rows // TILE, TILE, TILE), BF16),
            pltpu.VMEM((rows // TILE, TILE), F32),
            pltpu.VMEM((rows // TILE, TILE), F32),
            pltpu.VMEM((rows // TILE, TILE), F32),
            pltpu.VMEM((2 * sides, rows), F32),
            pltpu.VMEM((sides, rows), F32),
            pltpu.VMEM((sides, rows), BF16),
            pltpu.VMEM((rows // TILE, sides, TILE), BF16),
            pltpu.VMEM((rows // TILE // 4, sides, TILE), BF16),
            pltpu.VMEM((sides, rows), F32),
            pltpu.VMEM((members, cap, LANES), jnp.int16),
            pltpu.VMEM((members, cap, LANES), jnp.int16),
            pltpu.VMEM((members, cap, LANES), BF16),
            pltpu.VMEM((members, cap, LANES), BF16),
            pltpu.VMEM((sides, width), F32),
            pltpu.VMEM((sides, width), F32),
            pltpu.VMEM((sides, width), F32),
            pltpu.VMEM((owners, own, width), F32),
            pltpu.VMEM((members, own, width), F32),
            pltpu.VMEM((2, own, width), F32),
            pltpu.VMEM((own, width), F32),
            pltpu.VMEM((owners, own, width), F32),
            pltpu.VMEM((2, sides, width), BF16),
            dma((7,)),
            dma((5,)),
            dma((5,)),
            dma((4,)),
            dma,
            dma((4,)),
            dma,
            dma,
            dma,
            dma((4,)),
            dma,
            dma,
            dma,
            dma,
            dma((4,)),
        ],
        compiler_params=pltpu.CompilerParams(
            collective_id=0, has_side_effects=True, vmem_limit_bytes=56 << 20
        ),
        name="substitution",
    )(
        super_index.reshape(tiles, LANES),
        drop_sides,
        low_inverse,
        coupling,
        top_sides,
        top_inverse,
        top_coupling,
    )
    return pl.pallas_call(
        widen,
        grid=(2,),
        out_shape=(jax.ShapeDtypeStruct((sides, rows), F32), jax.ShapeDtypeStruct(top_sides.shape, F32)),
        in_specs=[
            pl.BlockSpec((sides, rows // 2), lambda at: (0, at)),
            pl.BlockSpec(top_sides.shape, lambda at: (0, 0)),
        ],
        out_specs=(
            pl.BlockSpec((sides, rows // 2), lambda at: (0, at)),
            pl.BlockSpec(top_sides.shape, lambda at: (0, 0)),
        ),
        name="widen",
    )(low, top)


def solution(mesh):
    placed = (
        P(None, ("leaf", "wide")),
        P(("leaf", "wide")),
        P(("leaf", "wide"), None, None),
        P(("leaf", "wide"), None),
        P(None, "leaf"),
        P("leaf", None, None),
        P(None, "leaf", None, None),
    )
    return jax.shard_map(
        shards,
        mesh=mesh,
        in_specs=placed,
        out_specs=(P(None, ("leaf", "wide")), P(None, "leaf")),
        check_vma=False,
    )
```

```python
import functools
import random

import jax
import jax.numpy as jnp
from jax import lax
from jax.experimental import pallas as pl
from jax.experimental.pallas import tpu as pltpu
from jax.sharding import PartitionSpec as P

MESH = pl.DeviceIdType.MESH
F32 = jnp.float32
BF16 = jnp.bfloat16
LANES = 128
TILE = 256


def order_of_partners():
    steps = [(z, y, x) for z in range(4) for y in range(4) for x in range(4)][1:]
    random.Random(2).shuffle(steps)
    return sorted(steps, key=lambda step: -sum((0, 1, 2, 1)[one] for one in step)) + [(0, 0, 0)]


ORDER = order_of_partners()


def dot(a, b):
    return jnp.dot(a, b, preferred_element_type=F32)


def dot_t(a, b):
    return lax.dot_general(a, b, (((1,), (1,)), ((), ())), preferred_element_type=F32)


def split(x):
    high = x.astype(BF16)
    return high, (x - high.astype(F32)).astype(BF16)


def iota(shape, dim):
    return lax.broadcasted_iota(jnp.int32, shape, dim)


def onehot(rows, values):
    shape = (rows, values.shape[1])
    match = iota(shape, 0).astype(F32) == jnp.broadcast_to(values, shape)
    return jnp.where(match, 1.0, 0.0).astype(BF16)


def invert_step(high, low, place, rows):
    first = onehot(rows, high).astype(F32)
    lane = iota((rows, LANES), 1).astype(F32)
    left = jnp.concatenate([first * place, first * lane], axis=0).astype(BF16)
    return dot_t(left, onehot(LANES, low))


def pick(data_ref, source):
    blocks, height, _ = data_ref.shape
    high = jnp.floor(source * (1.0 / TILE))
    chooser = onehot(TILE, source - TILE * high)
    parts = dot(data_ref[...].reshape(blocks * height, TILE), chooser)
    result = parts[:height]
    for block in range(1, blocks):
        part = parts[block * height : (block + 1) * height]
        result = jnp.where(jnp.broadcast_to(high == float(block), part.shape), part, result)
    return result


def merge(data_ref, chooser, high, blocks, result):
    count, height, _ = data_ref.shape
    parts = dot(data_ref[...].reshape(count * height, TILE), chooser)
    for at in range(count):
        part = parts[at * height : (at + 1) * height]
        if result is None:
            result = part
        else:
            result = jnp.where(jnp.broadcast_to(high == float(blocks + at), part.shape), part, result)
    return result


def make_choosers(ref, chooser_ref, high_ref):
    def one(pair, _):
        source = row_pair(ref, pair)
        high = jnp.floor(source * (1.0 / TILE))
        chooser_ref[pair] = onehot(TILE, source - TILE * high)
        high_ref[pl.ds(pair, 1), :] = high
        return 0

    lax.fori_loop(0, chooser_ref.shape[0], one, 0)


def row_pair(ref, pair):
    two = ref[pl.ds(2 * pair, 2), :]
    return jnp.concatenate([two[0:1], two[1:2]], axis=1)


def turned(x):
    height = x.shape[0]
    if height < LANES:
        x = jnp.concatenate([x, jnp.zeros((LANES - height, x.shape[1]), x.dtype)], axis=0)
    return x.T


def kernel(
    dims,
    index_any,
    drop_any,
    inverse_any,
    coupling_any,
    top_sides_any,
    top_inverse_any,
    top_coupling_any,
    out_any,
    top_out_any,
    index_v,
    top_sides_v,
    out_v,
    top_out_v,
    here_ref,
    left_slot,
    right_slot,
    left_place,
    right_place,
    inverse_v,
    coupling_v,
    top_inv_f32,
    top_inv_high,
    top_inv_low,
    top_coup,
    inv_high,
    inv_low,
    slot_ref,
    source_ref,
    place_ref,
    drop_v,
    data,
    turned_in,
    pos_send,
    pos_recv,
    choose_in,
    choose_out,
    choose_last,
    high_in,
    high_out,
    high_last,
    super_n,
    low_solved,
    base,
    weighed,
    low_half,
    low_final,
    turned_back,
    out_sum,
    send_buf,
    recv_buf,
    back_send,
    back_recv,
    partial,
    half_send,
    half_recv,
    rs_send,
    rs_recv,
    pair_buf,
    ag_send,
    ag_recv,
    sol_half,
    load_sem,
    core_send,
    core_recv,
    local_sem,
    there_send,
    there_recv,
    pos_send_sem,
    pos_recv_sem,
    back_send_sem,
    back_recv_sem,
    rs_send_sem,
    rs_recv_sem,
    ag_send_sem,
    ag_recv_sem,
    out_sem,
):
    sides, rows, members, cap, nodes, width, owners = dims
    tiles = rows // LANES
    pairs = rows // TILE
    groups = 4
    chunks = members // groups
    group_rows = rows // groups
    group_pairs = pairs // groups
    group_tiles = tiles // groups
    own_rows = sides // owners
    me = lax.axis_index("wide")
    leaf = lax.axis_index("leaf")
    my_z, my_y, my_x = me // 16, lax.rem(me // 4, 4), lax.rem(me, 4)
    z_at = [16 * lax.rem(my_z + step, 4) for step in range(4)]
    y_at = [4 * lax.rem(my_y + step, 4) for step in range(4)]
    x_at = [lax.rem(my_x + step, 4) for step in range(4)]

    def partner(chunk):
        dz, dy, dx = ORDER[chunk]
        return z_at[dz] + y_at[dy] + x_at[dx]

    def origin(chunk):
        dz, dy, dx = ORDER[chunk]
        return z_at[(4 - dz) % 4] + y_at[(4 - dy) % 4] + x_at[(4 - dx) % 4]


    barrier = pltpu.get_barrier_semaphore()

    def greet(step, _):
        pl.semaphore_signal(
            barrier,
            inc=1,
            device_id={"wide": lax.rem(me + step, members)},
            device_id_type=MESH,
        )
        return 0

    lax.fori_loop(1, members, greet, 0)
    pl.semaphore_signal(barrier, inc=1, device_id={"leaf": 1 - leaf}, device_id_type=MESH)

    load_index = pltpu.make_async_copy(index_any, index_v, load_sem.at[5])
    load_sides = pltpu.make_async_copy(top_sides_any, top_sides_v, load_sem.at[6])
    load_drop = pltpu.make_async_copy(drop_any, drop_v, load_sem.at[4])
    load_inverse = pltpu.make_async_copy(inverse_any, inverse_v, load_sem.at[0])
    load_coupling = pltpu.make_async_copy(coupling_any, coupling_v, load_sem.at[1])
    load_top = pltpu.make_async_copy(top_inverse_any.at[0], top_inv_f32.at[leaf], load_sem.at[2])
    load_tc = pltpu.make_async_copy(top_coupling_any.at[0, 0], top_coup.at[leaf], load_sem.at[3])
    load_index.start()
    load_drop.start()
    load_inverse.start()
    load_coupling.start()
    load_top.start()
    load_tc.start()
    load_sides.start()

    order = jnp.zeros((members, LANES), F32)
    chunk_of = iota((members, LANES), 0)
    for chunk, (dz, dy, dx) in enumerate(ORDER):
        order = jnp.where(chunk_of == chunk, float(16 * dz + 4 * dy + dx), order)
    begin = (cap * chunk_of).astype(F32)
    below = (iota((LANES, LANES), 0) < iota((LANES, LANES), 1)).astype(F32)
    counter = jnp.concatenate([below, jnp.ones((LANES, LANES), F32)], axis=1).astype(BF16)
    load_index.wait()
    local = index_v[...] - leaf * (members * rows)
    target = ((local.astype(F32) + 0.5) * (1.0 / rows)).astype(jnp.int32)
    position = (local - target * rows).astype(F32)
    step_of = (
        16 * (((target >> 4) - my_z) & 3) + 4 * (((target >> 2) - my_y) & 3) + ((target - my_x) & 3)
    ).astype(F32)
    place_high = jnp.floor(position * (1.0 / LANES))
    place_low = position - LANES * place_high

    def here_of(tile):
        return jnp.where(order == step_of[tile : tile + 1], 1.0, 0.0)

    for tile in range(tiles):
        here_ref[tile * members : (tile + 1) * members, :] = here_of(tile).astype(BF16)
    counts = dot(here_ref[...], counter)
    carry = jnp.zeros((members, LANES), F32)
    lane = iota((tiles, LANES), 1).astype(F32)
    extras = []
    for tile in range(tiles):
        here = here_of(tile)
        count = counts[tile * members : (tile + 1) * members]
        rank = jnp.sum(here * (count[:, :LANES] + carry), axis=0, keepdims=True)
        slot = rank + jnp.sum(here * begin, axis=0, keepdims=True)
        carry = carry + count[:, LANES:]
        slot_ref[tile : tile + 1, :] = slot
        slot_high = jnp.floor(slot * (1.0 / LANES))
        span = pl.ds(tile * LANES, LANES)
        first = onehot(tiles, slot_high).astype(F32)
        left_slot[:, span] = jnp.concatenate(
            [first * float(tile), first * lane, jnp.zeros((LANES - 2 * tiles, LANES), F32)], axis=0
        ).astype(BF16)
        right_slot[:, span] = onehot(LANES, slot - LANES * slot_high)
        left_place[:, span] = jnp.concatenate(
            [here * place_high[tile : tile + 1], here * place_low[tile : tile + 1]], axis=0
        ).astype(BF16)
        right_place[:, span] = onehot(LANES, rank)
        extra = iota((16, LANES), 0)
        extras.append(
            jnp.where(
                extra == 0, place_high[tile : tile + 1], jnp.where(extra == 1, place_low[tile : tile + 1], 0.0)
            )
        )
    inverse_sum = dot_t(right_slot[...], left_slot[...]).T
    source_ref[...] = LANES * inverse_sum[:tiles] + inverse_sum[tiles : 2 * tiles]
    places = dot_t(left_place[...], right_place[...])
    places = jnp.where(iota((members, LANES), 1) < cap, LANES * places[:members] + places[members:], -1.0)
    for member in range(members):
        pos_send[member] = places[member : member + 1]
    pos_recv[members - 1] = places[members - 1 : members]

    load_drop.wait()
    for tile in range(tiles):
        block, lanes = tile // 2, pl.ds((tile % 2) * LANES, LANES)
        values = drop_v[:, tile * LANES : (tile + 1) * LANES]
        most = jnp.maximum(jnp.max(jnp.abs(values), axis=0, keepdims=True), 2.0**-100)
        power = jnp.ceil(jnp.log2(most) - 14.99)
        code = jnp.floor(values * jnp.exp2(-power) + 0.5)
        upper = jnp.floor(code * (1.0 / 256.0))
        data[block, 0:sides, lanes] = upper.astype(BF16)
        data[block, sides : 2 * sides, lanes] = (code - 256.0 * upper).astype(BF16)
        extra = jnp.where(iota((16, LANES), 0) == 2, power, extras[tile])
        data[block, 2 * sides : 2 * sides + 16, lanes] = extra.astype(BF16)

    def store_chunks(buf, first, block):
        for piece in range(TILE // 16):
            at = first + piece
            buf[at // 3, pl.ds(pl.multiple_of((at % 3) * 16, 16), 16), :] = block[
                piece * 16 : (piece + 1) * 16
            ]

    for group in range(groups):
        for pair in range(group * group_pairs, (group + 1) * group_pairs):
            block = pick(data, row_pair(source_ref, pair))
            code = jnp.concatenate(
                [256.0 * block[:sides] + block[sides : 2 * sides], block[2 * sides :]], axis=0
            )
            code = turned(code).astype(jnp.int32).astype(jnp.int16)
            store_chunks(send_buf, pair * (TILE // 16), code)

    pl.semaphore_wait(barrier, members)

    def dummy(src, dst, send, recv):
        return pltpu.make_async_remote_copy(
            src_ref=src,
            dst_ref=dst,
            send_sem=send,
            recv_sem=recv,
            device_id={"wide": me},
            device_id_type=MESH,
        )

    def ahead(chunk):
        return pltpu.make_async_remote_copy(
            src_ref=pos_send.at[chunk],
            dst_ref=pos_recv.at[chunk],
            send_sem=pos_send_sem,
            recv_sem=pos_recv_sem,
            device_id={"wide": partner(chunk)},
            device_id_type=MESH,
        )

    for chunk in range(members - 1):
        ahead(chunk).start()

    load_top.wait()
    load_tc.wait()
    core_top = pltpu.make_async_remote_copy(
        src_ref=top_inv_f32.at[leaf],
        dst_ref=top_inv_f32.at[leaf],
        send_sem=core_send.at[0],
        recv_sem=core_recv.at[0],
        device_id={"leaf": 1 - leaf},
        device_id_type=MESH,
    )
    core_tc = pltpu.make_async_remote_copy(
        src_ref=top_coup.at[leaf],
        dst_ref=top_coup.at[leaf],
        send_sem=core_send.at[1],
        recv_sem=core_recv.at[1],
        device_id={"leaf": 1 - leaf},
        device_id_type=MESH,
    )
    core_top.start()
    core_tc.start()

    def there(chunk):
        return pltpu.make_async_remote_copy(
            src_ref=send_buf.at[chunk],
            dst_ref=recv_buf.at[chunk],
            send_sem=there_send,
            recv_sem=there_recv.at[chunk // chunks],
            device_id={"wide": partner(chunk)},
            device_id_type=MESH,
        )

    def back(chunk):
        return pltpu.make_async_remote_copy(
            src_ref=back_send.at[chunk],
            dst_ref=back_recv.at[chunk],
            send_sem=back_send_sem,
            recv_sem=back_recv_sem.at[chunk // chunks],
            device_id={"wide": origin(chunk)},
            device_id_type=MESH,
        )

    def start_group(copy, group):
        last = (group + 1) * chunks
        if group == groups - 1:
            last -= 1

        for chunk in range(group * chunks, last):
            copy(chunk).start()

    def wait_group(buf, sem, group, dst=True):
        count = chunks - 1 if group == groups - 1 else chunks
        part = buf.at[pl.ds(group * chunks, count)]
        pltpu.make_async_remote_copy(
            src_ref=part,
            dst_ref=part,
            send_sem=there_send,
            recv_sem=sem.at[group],
            device_id={"wide": me},
            device_id_type=MESH,
        ).wait_recv()

    own_there = pltpu.make_async_copy(
        send_buf.at[members - 1], recv_buf.at[members - 1], local_sem.at[0]
    )
    own_back = pltpu.make_async_copy(
        back_send.at[members - 1], back_recv.at[members - 1], local_sem.at[1]
    )

    for group in range(groups):
        start_group(there, group)
    own_there.start()

    load_inverse.wait()

    def halves(node, _):
        high, low = split(inverse_v[node])
        inv_high[node] = high
        inv_low[node] = low
        return 0

    lax.fori_loop(0, nodes, halves, 0)
    core_top.wait()
    core_tc.wait()
    for half in range(2):
        high, low = split(top_inv_f32[half])
        top_inv_high[half] = high
        top_inv_low[half] = low

    arrived = pos_recv.at[pl.ds(0, members - 1)]
    dummy(arrived, arrived, pos_send_sem, pos_recv_sem).wait_recv()
    lane = iota((1, LANES), 1)
    second = (lane >= LANES // 2).astype(F32)
    offset = lane.astype(F32) - second * (LANES // 2)
    inverse_sum = jnp.zeros((2 * tiles, LANES), F32)
    for member in range(members // 2):
        other = pltpu.roll(pos_recv[member + members // 2], LANES // 2, 1)
        place = jnp.where(lane < LANES // 2, pos_recv[member], other)
        high = jnp.floor(place * (1.0 / LANES))
        first = onehot(tiles, high).astype(F32)
        left = jnp.concatenate([first * (second * (members // 2) + float(member)), first * offset], axis=0)
        inverse_sum += dot_t(left.astype(BF16), onehot(LANES, place - LANES * high))
    source_ref[...] = cap * inverse_sum[:tiles] + inverse_sum[tiles:]
    make_choosers(source_ref, choose_in, high_in)
    make_choosers(slot_ref, choose_last, high_last)

    for group in range(groups):
        wait_group(recv_buf, there_recv, group)
        if group == groups - 1:
            own_there.wait()
        for tile in range(group_tiles):
            at = group * group_tiles + tile
            first = group * chunks + (tile * LANES) // cap
            last = group * chunks + ((tile + 1) * LANES - 1) // cap
            skip = (tile * LANES) % cap
            block = recv_buf[first : last + 1].astype(jnp.int32).astype(F32)
            columns = block.reshape((last + 1 - first) * cap, LANES)[skip : skip + LANES].T
            place_ref[at : at + 1, :] = LANES * columns[sides : sides + 1] + columns[sides + 1 : sides + 2]
            values = columns[:sides] * jnp.exp2(columns[sides + 2 : sides + 3])
            high, low = split(values)
            lanes = pl.ds((tile % 2) * LANES, LANES)
            turned_in[tile // 2, :sides, lanes] = high
            turned_in[tile // 2, sides:, lanes] = low

        for pair in range(pairs):
            span = pl.ds(pair * TILE, TILE)
            before = super_n[:, span] if group > 0 else None
            super_n[:, span] = merge(
                turned_in, choose_in[pair], high_in[pair : pair + 1], group * group_pairs, before
            )

    for node in range(nodes):
        span = pl.ds(node * width, width)
        side = super_n[:, span].astype(BF16)
        value = dot(side, inv_high[node])
        value = value[:sides] + value[sides:] + dot(side[:sides], inv_low[node])
        low_solved[:, span] = value
        low_half[:, span] = value.astype(BF16)

    load_coupling.wait()

    def half_sum(half):
        return dot(low_half[...], coupling_v[:, pl.ds(pl.multiple_of(half * width, LANES), width)])

    half_send[...] = half_sum(1 - leaf)
    core_half = pltpu.make_async_remote_copy(
        src_ref=half_send,
        dst_ref=half_recv,
        send_sem=core_send.at[3],
        recv_sem=core_recv.at[3],
        device_id={"leaf": 1 - leaf},
        device_id_type=MESH,
    )
    core_half.start()
    first = jnp.where(me == 0, 1.0, 0.0).astype(F32)
    load_sides.wait()
    partial[...] = half_sum(leaf) - top_sides_v[...] * first
    core_half.wait()
    partial[...] = partial[...] + half_recv[...]
    for owner in range(owners):
        rs_send[owner] = partial[owner * own_rows : (owner + 1) * own_rows, :]

    def turn_of(chip):
        line = chip // 4
        return lax.rem(chip - 4 * line + 8 * members - line - line // 4, 4)

    my_turn = turn_of(me)
    is_owner = my_turn < 3
    my_owner = 3 * (me // 4) + jnp.minimum(my_turn, 2)

    def send_part(chunk):
        chip = partner(chunk)
        turn = turn_of(chip)

        @pl.when(turn < 3)
        def _():
            pltpu.make_async_remote_copy(
                src_ref=rs_send.at[3 * (chip // 4) + jnp.minimum(turn, 2)],
                dst_ref=rs_recv.at[chunk],
                send_sem=rs_send_sem,
                recv_sem=rs_recv_sem,
                device_id={"wide": chip},
                device_id_type=MESH,
            ).start()

    for chunk in range(members - 1):
        send_part(chunk)
    make_choosers(place_ref, choose_out, high_out)

    for node in range(nodes):
        span = pl.ds(node * width, width)
        high, low = split(low_solved[:, span])
        value = dot_t(jnp.concatenate([high, low], axis=0), inv_high[node])
        base[:, span] = value[:sides] + value[sides:] + dot_t(high, inv_low[node])

    def weigh(node, _):
        span = pl.ds(pl.multiple_of(node * width, width), width)
        block = coupling_v[span, :]
        weighed[span, :] = (dot(inv_high[node], block) + dot(inv_low[node], block)).astype(BF16)
        return 0

    lax.fori_loop(0, nodes // 2, weigh, 0)

    def ag_copy(chunk):
        return pltpu.make_async_remote_copy(
            src_ref=ag_send,
            dst_ref=ag_recv.at[my_owner],
            send_sem=ag_send_sem,
            recv_sem=ag_recv_sem,
            device_id={"wide": partner(chunk)},
            device_id_type=MESH,
        )

    @pl.when(is_owner)
    def _():
        rs_recv[members - 1] = rs_send[my_owner]
        arrived = rs_recv.at[pl.ds(0, members - 1)]
        dummy(arrived, arrived, rs_send_sem, rs_recv_sem).wait_recv()
        pair_buf[leaf] = jnp.sum(rs_recv[...], axis=0)
        swap = pltpu.make_async_remote_copy(
            src_ref=pair_buf.at[leaf],
            dst_ref=pair_buf.at[leaf],
            send_sem=core_send.at[2],
            recv_sem=core_recv.at[2],
            device_id={"leaf": 1 - leaf},
            device_id_type=MESH,
        )
        swap.start()
        swap.wait()

        def times(product, x, half):
            high, low = split(x)
            both = product(jnp.concatenate([high, low], axis=0), top_inv_high[half])
            return both[:own_rows] + both[own_rows:] + product(high, top_inv_low[half])

        solved0 = times(dot, -pair_buf[0], 0)
        solved1 = times(dot, -pair_buf[1] - dot(solved0.astype(BF16), top_coup[1]), 1)
        answer1 = times(dot_t, solved1, 1)
        answer0 = times(dot_t, solved0 - dot_t(answer1.astype(BF16), top_coup[1]), 0)
        ag_send[...] = jnp.where(leaf == 0, answer0, answer1)
        ag_recv[my_owner] = ag_send[...]

        for chunk in range(members - 1):
            ag_copy(chunk).start()

    lax.fori_loop(nodes // 2, nodes, weigh, 0)

    @pl.when(is_owner)
    def _():
        arrived = ag_recv.at[pl.ds(0, owners - 1)]
        dummy(arrived, arrived, ag_send_sem, ag_recv_sem).wait_recv()

    @pl.when(jnp.logical_not(is_owner))
    def _():
        dummy(ag_recv, ag_recv, ag_send_sem, ag_recv_sem).wait_recv()

    for owner in range(owners):
        top_out_v[owner * own_rows : (owner + 1) * own_rows, :] = ag_recv[owner]
    sol_half[leaf] = top_out_v[...].astype(BF16)
    core_sol = pltpu.make_async_remote_copy(
        src_ref=sol_half.at[leaf],
        dst_ref=sol_half.at[leaf],
        send_sem=core_send.at[4],
        recv_sem=core_recv.at[4],
        device_id={"leaf": 1 - leaf},
        device_id_type=MESH,
    )
    core_sol.start()
    store_top = pltpu.make_async_copy(top_out_v, top_out_any, local_sem.at[2])
    store_top.start()
    core_sol.wait()

    for node in range(nodes):
        span = pl.ds(node * width, width)
        rows_here = slice(node * width, (node + 1) * width)
        term = dot_t(sol_half[0], weighed[rows_here, :width]) + dot_t(sol_half[1], weighed[rows_here, width:])
        value = (base[:, span] - term).astype(BF16)
        for piece in range(width // LANES):
            at = node * width + piece * LANES
            low_final[at // TILE, :, pl.ds(at % TILE, LANES)] = value[:, piece * LANES : (piece + 1) * LANES]

    for group in range(groups):
        for pair in range(group * group_pairs, (group + 1) * group_pairs):
            block = merge(low_final, choose_out[pair], high_out[pair : pair + 1], 0, None)
            store_chunks(back_send, pair * (TILE // 16), turned(block).astype(BF16))
        start_group(back, group)
    own_back.start()

    def store_out(part):
        span = pl.ds(part * 3 * TILE, 3 * TILE)
        return pltpu.make_async_copy(out_v.at[:, span], out_any.at[:, span], out_sem.at[part])

    for group in range(groups):
        wait_group(back_recv, back_recv_sem, group)
        if group == groups - 1:
            own_back.wait()
        block = back_recv[group * chunks : (group + 1) * chunks].reshape(group_rows, LANES)
        for tile in range(group_tiles):
            columns = block[tile * LANES : (tile + 1) * LANES].astype(F32).T
            turned_back[tile // 2, :, pl.ds((tile % 2) * LANES, LANES)] = columns[:sides].astype(BF16)

        for pair in range(pairs):
            span = pl.ds(pair * TILE, TILE)
            before = out_sum[:, span] if group > 0 else None
            value = merge(
                turned_back, choose_last[pair], high_last[pair : pair + 1], group * group_pairs, before
            )
            if group < groups - 1:
                out_sum[:, span] = value
            else:
                out_v[:, span] = value.astype(BF16)
                if pair % 3 == 2:
                    store_out(pair // 3).start()

    store_top.wait()
    for part in range(pairs // 3):
        store_out(part).wait()
    sent = pos_send.at[pl.ds(0, members - 1)]
    dummy(sent, sent, pos_send_sem, pos_send_sem).wait_send()
    sent = send_buf.at[pl.ds(0, members - 1)]
    dummy(sent, sent, there_send, there_send).wait_send()
    sent = back_send.at[pl.ds(0, members - 1)]
    dummy(sent, sent, back_send_sem, back_send_sem).wait_send()

    @pl.when(is_owner)
    def _():
        part = rs_send.at[pl.ds(0, owners - 1)]
        dummy(part, part, rs_send_sem, rs_send_sem).wait_send()
        part = rs_recv.at[pl.ds(0, members - 1)]
        dummy(part, part, ag_send_sem, ag_send_sem).wait_send()

    @pl.when(jnp.logical_not(is_owner))
    def _():
        dummy(rs_send, rs_send, rs_send_sem, rs_send_sem).wait_send()


def widen(low_ref, top_ref, out_ref, top_out_ref):
    out_ref[...] = low_ref[...].astype(F32)

    @pl.when(pl.program_id(0) == 0)
    def _():
        top_out_ref[...] = top_ref[...]


def shards(drop_sides, super_index, low_inverse, coupling, top_sides, top_inverse, top_coupling):
    sides, rows = drop_sides.shape
    nodes, width, _ = low_inverse.shape
    members = lax.axis_size("wide")
    cap = rows // members
    owners = 48
    top_cols = coupling.shape[1]
    tiles = rows // LANES
    own = sides // owners
    anyspace = pl.BlockSpec(memory_space=pl.ANY)
    dma = pltpu.SemaphoreType.DMA
    dims = (sides, rows, members, cap, nodes, width, owners)
    low, top = pl.pallas_call(
        functools.partial(kernel, dims),
        out_shape=(
            jax.ShapeDtypeStruct((sides, rows), BF16),
            jax.ShapeDtypeStruct(top_sides.shape, F32),
        ),
        in_specs=[anyspace] * 7,
        out_specs=(anyspace, anyspace),
        scratch_shapes=[
            pltpu.VMEM((tiles, LANES), jnp.int32),
            pltpu.VMEM((sides, width), F32),
            pltpu.VMEM((sides, rows), BF16),
            pltpu.VMEM((sides, width), F32),
            pltpu.VMEM((tiles * members, LANES), BF16),
            pltpu.VMEM((LANES, rows), BF16),
            pltpu.VMEM((LANES, rows), BF16),
            pltpu.VMEM((2 * members, rows), BF16),
            pltpu.VMEM((LANES, rows), BF16),
            pltpu.VMEM((nodes, width, width), F32),
            pltpu.VMEM((rows, top_cols), BF16),
            pltpu.VMEM((2, width, width), F32),
            pltpu.VMEM((2, width, width), BF16),
            pltpu.VMEM((2, width, width), BF16),
            pltpu.VMEM((2, width, width), BF16),
            pltpu.VMEM((nodes, width, width), BF16),
            pltpu.VMEM((nodes, width, width), BF16),
            pltpu.VMEM((tiles, LANES), F32),
            pltpu.VMEM((tiles, LANES), F32),
            pltpu.VMEM((tiles, LANES), F32),
            pltpu.VMEM((sides, rows), F32),
            pltpu.VMEM((rows // TILE, 2 * sides + 16, TILE), BF16),
            pltpu.VMEM((rows // TILE // 4, 2 * sides, TILE), BF16),
            pltpu.VMEM((members, 1, LANES), F32),
            pltpu.VMEM((members, 1, LANES), F32),
            pltpu.VMEM((rows // TILE, TILE, TILE), BF16),
            pltpu.VMEM((rows // TILE, TILE, TILE), BF16),
            pltpu.VMEM((rows // TILE, TILE, TILE), BF16),
            pltpu.VMEM((rows // TILE, TILE), F32),
            pltpu.VMEM((rows // TILE, TILE), F32),
            pltpu.VMEM((rows // TILE, TILE), F32),
            pltpu.VMEM((2 * sides, rows), F32),
            pltpu.VMEM((sides, rows), F32),
            pltpu.VMEM((sides, rows), F32),
            pltpu.VMEM((rows, top_cols), BF16),
            pltpu.VMEM((sides, rows), BF16),
            pltpu.VMEM((rows // TILE, sides, TILE), BF16),
            pltpu.VMEM((rows // TILE // 4, sides, TILE), BF16),
            pltpu.VMEM((sides, rows), F32),
            pltpu.VMEM((members, cap, LANES), jnp.int16),
            pltpu.VMEM((members, cap, LANES), jnp.int16),
            pltpu.VMEM((members, cap, LANES), BF16),
            pltpu.VMEM((members, cap, LANES), BF16),
            pltpu.VMEM((sides, width), F32),
            pltpu.VMEM((sides, width), F32),
            pltpu.VMEM((sides, width), F32),
            pltpu.VMEM((owners, own, width), F32),
            pltpu.VMEM((members, own, width), F32),
            pltpu.VMEM((2, own, width), F32),
            pltpu.VMEM((own, width), F32),
            pltpu.VMEM((owners, own, width), F32),
            pltpu.VMEM((2, sides, width), BF16),
            dma((7,)),
            dma((5,)),
            dma((5,)),
            dma((4,)),
            dma,
            dma((4,)),
            dma,
            dma,
            dma,
            dma((4,)),
            dma,
            dma,
            dma,
            dma,
            dma((4,)),
        ],
        compiler_params=pltpu.CompilerParams(
            collective_id=0, has_side_effects=True, vmem_limit_bytes=56 << 20
        ),
        name="substitution",
    )(
        super_index.reshape(tiles, LANES),
        drop_sides,
        low_inverse,
        coupling,
        top_sides,
        top_inverse,
        top_coupling,
    )
    return pl.pallas_call(
        widen,
        grid=(2,),
        out_shape=(jax.ShapeDtypeStruct((sides, rows), F32), jax.ShapeDtypeStruct(top_sides.shape, F32)),
        in_specs=[
            pl.BlockSpec((sides, rows // 2), lambda at: (0, at)),
            pl.BlockSpec(top_sides.shape, lambda at: (0, 0)),
        ],
        out_specs=(
            pl.BlockSpec((sides, rows // 2), lambda at: (0, at)),
            pl.BlockSpec(top_sides.shape, lambda at: (0, 0)),
        ),
        name="widen",
    )(low, top)


def solution(mesh):
    placed = (
        P(None, ("leaf", "wide")),
        P(("leaf", "wide")),
        P(("leaf", "wide"), None, None),
        P(("leaf", "wide"), None),
        P(None, "leaf"),
        P("leaf", None, None),
        P(None, "leaf", None, None),
    )
    return jax.shard_map(
        shards,
        mesh=mesh,
        in_specs=placed,
        out_specs=(P(None, ("leaf", "wide")), P(None, "leaf")),
        check_vma=False,
    )
```

```python
import functools
import random

import jax
import jax.numpy as jnp
from jax import lax
from jax.experimental import pallas as pl
from jax.experimental.pallas import tpu as pltpu
from jax.sharding import PartitionSpec as P

MESH = pl.DeviceIdType.MESH
F32 = jnp.float32
BF16 = jnp.bfloat16
LANES = 128
TILE = 256


def order_of_partners():
    steps = [(z, y, x) for z in range(4) for y in range(4) for x in range(4)][1:]
    random.Random(2).shuffle(steps)
    return sorted(steps, key=lambda step: -sum((0, 1, 2, 1)[one] for one in step)) + [(0, 0, 0)]


ORDER = order_of_partners()


def dot(a, b):
    return jnp.dot(a, b, preferred_element_type=F32)


def dot_t(a, b):
    return lax.dot_general(a, b, (((1,), (1,)), ((), ())), preferred_element_type=F32)


def split(x):
    high = x.astype(BF16)
    return high, (x - high.astype(F32)).astype(BF16)


def iota(shape, dim):
    return lax.broadcasted_iota(jnp.int32, shape, dim)


def onehot(rows, values):
    shape = (rows, values.shape[1])
    match = iota(shape, 0).astype(F32) == jnp.broadcast_to(values, shape)
    return jnp.where(match, 1.0, 0.0).astype(BF16)


def invert_step(high, low, place, rows):
    first = onehot(rows, high).astype(F32)
    lane = iota((rows, LANES), 1).astype(F32)
    left = jnp.concatenate([first * place, first * lane], axis=0).astype(BF16)
    return dot_t(left, onehot(LANES, low))


def pick(data_ref, source):
    blocks, height, _ = data_ref.shape
    high = jnp.floor(source * (1.0 / TILE))
    chooser = onehot(TILE, source - TILE * high)
    parts = dot(data_ref[...].reshape(blocks * height, TILE), chooser)
    result = parts[:height]
    for block in range(1, blocks):
        part = parts[block * height : (block + 1) * height]
        result = jnp.where(jnp.broadcast_to(high == float(block), part.shape), part, result)
    return result


def merge(data_ref, chooser, high, blocks, result):
    count, height, _ = data_ref.shape
    parts = dot(data_ref[...].reshape(count * height, TILE), chooser)
    for at in range(count):
        part = parts[at * height : (at + 1) * height]
        if result is None:
            result = part
        else:
            result = jnp.where(jnp.broadcast_to(high == float(blocks + at), part.shape), part, result)
    return result


def make_choosers(ref, chooser_ref, high_ref):
    def one(pair, _):
        source = row_pair(ref, pair)
        high = jnp.floor(source * (1.0 / TILE))
        chooser_ref[pair] = onehot(TILE, source - TILE * high)
        high_ref[pl.ds(pair, 1), :] = high
        return 0

    lax.fori_loop(0, chooser_ref.shape[0], one, 0)


def row_pair(ref, pair):
    two = ref[pl.ds(2 * pair, 2), :]
    return jnp.concatenate([two[0:1], two[1:2]], axis=1)


def turned(x):
    height = x.shape[0]
    if height < LANES:
        x = jnp.concatenate([x, jnp.zeros((LANES - height, x.shape[1]), x.dtype)], axis=0)
    return x.T


def kernel(
    dims,
    index_any,
    drop_any,
    inverse_any,
    coupling_any,
    top_sides_any,
    top_inverse_any,
    top_coupling_any,
    out_any,
    top_out_any,
    index_v,
    top_sides_v,
    out_v,
    top_out_v,
    here_ref,
    left_slot,
    right_slot,
    left_place,
    right_place,
    inverse_v,
    coupling_v,
    top_inv_f32,
    top_inv_high,
    top_inv_low,
    top_coup,
    inv_high,
    inv_low,
    slot_ref,
    source_ref,
    place_ref,
    drop_v,
    data,
    turned_in,
    pos_send,
    pos_recv,
    choose_in,
    choose_out,
    choose_last,
    high_in,
    high_out,
    high_last,
    super_n,
    low_solved,
    base,
    weighed,
    low_half,
    low_final,
    turned_back,
    out_sum,
    send_buf,
    recv_buf,
    back_send,
    back_recv,
    partial,
    half_send,
    half_recv,
    rs_send,
    rs_recv,
    pair_buf,
    ag_send,
    ag_recv,
    sol_half,
    load_sem,
    core_send,
    core_recv,
    local_sem,
    there_send,
    there_recv,
    pos_send_sem,
    pos_recv_sem,
    back_send_sem,
    back_recv_sem,
    rs_send_sem,
    rs_recv_sem,
    ag_send_sem,
    ag_recv_sem,
    out_sem,
):
    sides, rows, members, cap, nodes, width, owners = dims
    tiles = rows // LANES
    pairs = rows // TILE
    groups = 4
    chunks = members // groups
    group_rows = rows // groups
    group_pairs = pairs // groups
    group_tiles = tiles // groups
    own_rows = sides // owners
    me = lax.axis_index("wide")
    leaf = lax.axis_index("leaf")
    my_z, my_y, my_x = me // 16, lax.rem(me // 4, 4), lax.rem(me, 4)
    z_at = [16 * lax.rem(my_z + step, 4) for step in range(4)]
    y_at = [4 * lax.rem(my_y + step, 4) for step in range(4)]
    x_at = [lax.rem(my_x + step, 4) for step in range(4)]

    def partner(chunk):
        dz, dy, dx = ORDER[chunk]
        return z_at[dz] + y_at[dy] + x_at[dx]

    def origin(chunk):
        dz, dy, dx = ORDER[chunk]
        return z_at[(4 - dz) % 4] + y_at[(4 - dy) % 4] + x_at[(4 - dx) % 4]


    barrier = pltpu.get_barrier_semaphore()

    def greet(step, _):
        pl.semaphore_signal(
            barrier,
            inc=1,
            device_id={"wide": lax.rem(me + step, members)},
            device_id_type=MESH,
        )
        return 0

    lax.fori_loop(1, members, greet, 0)
    pl.semaphore_signal(barrier, inc=1, device_id={"leaf": 1 - leaf}, device_id_type=MESH)

    load_index = pltpu.make_async_copy(index_any, index_v, load_sem.at[5])
    load_sides = pltpu.make_async_copy(top_sides_any, top_sides_v, load_sem.at[6])
    load_drop = pltpu.make_async_copy(drop_any, drop_v, load_sem.at[4])
    load_inverse = pltpu.make_async_copy(inverse_any, inverse_v, load_sem.at[0])
    load_coupling = pltpu.make_async_copy(coupling_any, coupling_v, load_sem.at[1])
    load_top = pltpu.make_async_copy(top_inverse_any.at[0], top_inv_f32.at[leaf], load_sem.at[2])
    load_tc = pltpu.make_async_copy(top_coupling_any.at[0, 0], top_coup.at[leaf], load_sem.at[3])
    load_index.start()
    load_drop.start()
    load_inverse.start()
    load_coupling.start()
    load_top.start()
    load_tc.start()
    load_sides.start()

    order = jnp.zeros((members, LANES), F32)
    chunk_of = iota((members, LANES), 0)
    for chunk, (dz, dy, dx) in enumerate(ORDER):
        order = jnp.where(chunk_of == chunk, float(16 * dz + 4 * dy + dx), order)
    begin = (cap * chunk_of).astype(F32)
    below = (iota((LANES, LANES), 0) < iota((LANES, LANES), 1)).astype(F32)
    counter = jnp.concatenate([below, jnp.ones((LANES, LANES), F32)], axis=1).astype(BF16)
    load_index.wait()
    local = index_v[...] - leaf * (members * rows)
    target = ((local.astype(F32) + 0.5) * (1.0 / rows)).astype(jnp.int32)
    position = (local - target * rows).astype(F32)
    step_of = (
        16 * (((target >> 4) - my_z) & 3) + 4 * (((target >> 2) - my_y) & 3) + ((target - my_x) & 3)
    ).astype(F32)
    place_high = jnp.floor(position * (1.0 / LANES))
    place_low = position - LANES * place_high

    def here_of(tile):
        return jnp.where(order == step_of[tile : tile + 1], 1.0, 0.0)

    for tile in range(tiles):
        here_ref[tile * members : (tile + 1) * members, :] = here_of(tile).astype(BF16)
    counts = dot(here_ref[...], counter)
    carry = jnp.zeros((members, LANES), F32)
    lane = iota((tiles, LANES), 1).astype(F32)
    extras = []
    for tile in range(tiles):
        here = here_of(tile)
        count = counts[tile * members : (tile + 1) * members]
        rank = jnp.sum(here * (count[:, :LANES] + carry), axis=0, keepdims=True)
        slot = rank + jnp.sum(here * begin, axis=0, keepdims=True)
        carry = carry + count[:, LANES:]
        slot_ref[tile : tile + 1, :] = slot
        slot_high = jnp.floor(slot * (1.0 / LANES))
        span = pl.ds(tile * LANES, LANES)
        first = onehot(tiles, slot_high).astype(F32)
        left_slot[:, span] = jnp.concatenate(
            [first * float(tile), first * lane, jnp.zeros((LANES - 2 * tiles, LANES), F32)], axis=0
        ).astype(BF16)
        right_slot[:, span] = onehot(LANES, slot - LANES * slot_high)
        left_place[:, span] = jnp.concatenate(
            [here * place_high[tile : tile + 1], here * place_low[tile : tile + 1]], axis=0
        ).astype(BF16)
        right_place[:, span] = onehot(LANES, rank)
        extra = iota((16, LANES), 0)
        extras.append(
            jnp.where(
                extra == 0, place_high[tile : tile + 1], jnp.where(extra == 1, place_low[tile : tile + 1], 0.0)
            )
        )
    inverse_sum = dot_t(right_slot[...], left_slot[...]).T
    source_ref[...] = LANES * inverse_sum[:tiles] + inverse_sum[tiles : 2 * tiles]
    places = dot_t(left_place[...], right_place[...])
    places = jnp.where(iota((members, LANES), 1) < cap, LANES * places[:members] + places[members:], -1.0)
    for member in range(members):
        pos_send[member] = places[member : member + 1]
    pos_recv[members - 1] = places[members - 1 : members]

    load_drop.wait()
    for tile in range(tiles):
        block, lanes = tile // 2, pl.ds((tile % 2) * LANES, LANES)
        values = drop_v[:, tile * LANES : (tile + 1) * LANES]
        most = jnp.maximum(jnp.max(jnp.abs(values), axis=0, keepdims=True), 2.0**-100)
        power = jnp.ceil(jnp.log2(most) - 14.99)
        code = jnp.floor(values * jnp.exp2(-power) + 0.5)
        upper = jnp.floor(code * (1.0 / 256.0))
        data[block, 0:sides, lanes] = upper.astype(BF16)
        data[block, sides : 2 * sides, lanes] = (code - 256.0 * upper).astype(BF16)
        extra = jnp.where(iota((16, LANES), 0) == 2, power, extras[tile])
        data[block, 2 * sides : 2 * sides + 16, lanes] = extra.astype(BF16)

    def store_chunks(buf, first, block):
        for piece in range(TILE // 16):
            at = first + piece
            buf[at // 3, pl.ds(pl.multiple_of((at % 3) * 16, 16), 16), :] = block[
                piece * 16 : (piece + 1) * 16
            ]

    def pack(group):
        for pair in range(group * group_pairs, (group + 1) * group_pairs):
            block = pick(data, row_pair(source_ref, pair))
            code = jnp.concatenate(
                [256.0 * block[:sides] + block[sides : 2 * sides], block[2 * sides :]], axis=0
            )
            code = turned(code).astype(jnp.int32).astype(jnp.int16)
            store_chunks(send_buf, pair * (TILE // 16), code)

    pack(0)

    pl.semaphore_wait(barrier, members)

    def dummy(src, dst, send, recv):
        return pltpu.make_async_remote_copy(
            src_ref=src,
            dst_ref=dst,
            send_sem=send,
            recv_sem=recv,
            device_id={"wide": me},
            device_id_type=MESH,
        )

    def ahead(chunk):
        return pltpu.make_async_remote_copy(
            src_ref=pos_send.at[chunk],
            dst_ref=pos_recv.at[chunk],
            send_sem=pos_send_sem,
            recv_sem=pos_recv_sem,
            device_id={"wide": partner(chunk)},
            device_id_type=MESH,
        )

    for chunk in range(members - 1):
        ahead(chunk).start()

    load_top.wait()
    load_tc.wait()
    core_top = pltpu.make_async_remote_copy(
        src_ref=top_inv_f32.at[leaf],
        dst_ref=top_inv_f32.at[leaf],
        send_sem=core_send.at[0],
        recv_sem=core_recv.at[0],
        device_id={"leaf": 1 - leaf},
        device_id_type=MESH,
    )
    core_tc = pltpu.make_async_remote_copy(
        src_ref=top_coup.at[leaf],
        dst_ref=top_coup.at[leaf],
        send_sem=core_send.at[1],
        recv_sem=core_recv.at[1],
        device_id={"leaf": 1 - leaf},
        device_id_type=MESH,
    )
    core_top.start()
    core_tc.start()

    def there(chunk):
        return pltpu.make_async_remote_copy(
            src_ref=send_buf.at[chunk],
            dst_ref=recv_buf.at[chunk],
            send_sem=there_send,
            recv_sem=there_recv.at[chunk // chunks],
            device_id={"wide": partner(chunk)},
            device_id_type=MESH,
        )

    def back(chunk):
        return pltpu.make_async_remote_copy(
            src_ref=back_send.at[chunk],
            dst_ref=back_recv.at[chunk],
            send_sem=back_send_sem,
            recv_sem=back_recv_sem.at[chunk // chunks],
            device_id={"wide": origin(chunk)},
            device_id_type=MESH,
        )

    def start_group(copy, group):
        last = (group + 1) * chunks
        if group == groups - 1:
            last -= 1

        for chunk in range(group * chunks, last):
            copy(chunk).start()

    def wait_group(buf, sem, group, dst=True):
        count = chunks - 1 if group == groups - 1 else chunks
        part = buf.at[pl.ds(group * chunks, count)]
        pltpu.make_async_remote_copy(
            src_ref=part,
            dst_ref=part,
            send_sem=there_send,
            recv_sem=sem.at[group],
            device_id={"wide": me},
            device_id_type=MESH,
        ).wait_recv()

    own_there = pltpu.make_async_copy(
        send_buf.at[members - 1], recv_buf.at[members - 1], local_sem.at[0]
    )
    own_back = pltpu.make_async_copy(
        back_send.at[members - 1], back_recv.at[members - 1], local_sem.at[1]
    )

    start_group(there, 0)
    for group in range(1, groups):
        pack(group)
        start_group(there, group)
    own_there.start()

    load_inverse.wait()

    def halves(node, _):
        high, low = split(inverse_v[node])
        inv_high[node] = high
        inv_low[node] = low
        return 0

    lax.fori_loop(0, nodes, halves, 0)
    core_top.wait()
    core_tc.wait()
    for half in range(2):
        high, low = split(top_inv_f32[half])
        top_inv_high[half] = high
        top_inv_low[half] = low

    arrived = pos_recv.at[pl.ds(0, members - 1)]
    dummy(arrived, arrived, pos_send_sem, pos_recv_sem).wait_recv()
    lane = iota((1, LANES), 1)
    second = (lane >= LANES // 2).astype(F32)
    offset = lane.astype(F32) - second * (LANES // 2)
    inverse_sum = jnp.zeros((2 * tiles, LANES), F32)
    for member in range(members // 2):
        other = pltpu.roll(pos_recv[member + members // 2], LANES // 2, 1)
        place = jnp.where(lane < LANES // 2, pos_recv[member], other)
        high = jnp.floor(place * (1.0 / LANES))
        first = onehot(tiles, high).astype(F32)
        left = jnp.concatenate([first * (second * (members // 2) + float(member)), first * offset], axis=0)
        inverse_sum += dot_t(left.astype(BF16), onehot(LANES, place - LANES * high))
    source_ref[...] = cap * inverse_sum[:tiles] + inverse_sum[tiles:]
    make_choosers(source_ref, choose_in, high_in)
    make_choosers(slot_ref, choose_last, high_last)

    for group in range(groups):
        wait_group(recv_buf, there_recv, group)
        if group == groups - 1:
            own_there.wait()
        for tile in range(group_tiles):
            at = group * group_tiles + tile
            first = group * chunks + (tile * LANES) // cap
            last = group * chunks + ((tile + 1) * LANES - 1) // cap
            skip = (tile * LANES) % cap
            block = recv_buf[first : last + 1].astype(jnp.int32).astype(F32)
            columns = block.reshape((last + 1 - first) * cap, LANES)[skip : skip + LANES].T
            place_ref[at : at + 1, :] = LANES * columns[sides : sides + 1] + columns[sides + 1 : sides + 2]
            values = columns[:sides] * jnp.exp2(columns[sides + 2 : sides + 3])
            high, low = split(values)
            lanes = pl.ds((tile % 2) * LANES, LANES)
            turned_in[tile // 2, :sides, lanes] = high
            turned_in[tile // 2, sides:, lanes] = low

        for pair in range(pairs):
            span = pl.ds(pair * TILE, TILE)
            before = super_n[:, span] if group > 0 else None
            super_n[:, span] = merge(
                turned_in, choose_in[pair], high_in[pair : pair + 1], group * group_pairs, before
            )

    for node in range(nodes):
        span = pl.ds(node * width, width)
        side = super_n[:, span].astype(BF16)
        value = dot(side, inv_high[node])
        value = value[:sides] + value[sides:] + dot(side[:sides], inv_low[node])
        low_solved[:, span] = value
        low_half[:, span] = value.astype(BF16)

    load_coupling.wait()

    def half_sum(half):
        return dot(low_half[...], coupling_v[:, pl.ds(pl.multiple_of(half * width, LANES), width)])

    half_send[...] = half_sum(1 - leaf)
    core_half = pltpu.make_async_remote_copy(
        src_ref=half_send,
        dst_ref=half_recv,
        send_sem=core_send.at[3],
        recv_sem=core_recv.at[3],
        device_id={"leaf": 1 - leaf},
        device_id_type=MESH,
    )
    core_half.start()
    first = jnp.where(me == 0, 1.0, 0.0).astype(F32)
    load_sides.wait()
    partial[...] = half_sum(leaf) - top_sides_v[...] * first
    core_half.wait()
    partial[...] = partial[...] + half_recv[...]
    for owner in range(owners):
        rs_send[owner] = partial[owner * own_rows : (owner + 1) * own_rows, :]

    def turn_of(chip):
        line = chip // 4
        return lax.rem(chip - 4 * line + 8 * members - line - line // 4, 4)

    my_turn = turn_of(me)
    is_owner = my_turn < 3
    my_owner = 3 * (me // 4) + jnp.minimum(my_turn, 2)

    def send_part(chunk):
        chip = partner(chunk)
        turn = turn_of(chip)

        @pl.when(turn < 3)
        def _():
            pltpu.make_async_remote_copy(
                src_ref=rs_send.at[3 * (chip // 4) + jnp.minimum(turn, 2)],
                dst_ref=rs_recv.at[chunk],
                send_sem=rs_send_sem,
                recv_sem=rs_recv_sem,
                device_id={"wide": chip},
                device_id_type=MESH,
            ).start()

    for chunk in range(members - 1):
        send_part(chunk)
    make_choosers(place_ref, choose_out, high_out)

    def weigh(node, _):
        span = pl.ds(pl.multiple_of(node * width, width), width)
        block = coupling_v[span, :]
        weighed[span, :] = (dot(inv_high[node], block) + dot(inv_low[node], block)).astype(BF16)
        return 0

    lax.fori_loop(0, nodes // 2, weigh, 0)

    def ag_copy(chunk):
        return pltpu.make_async_remote_copy(
            src_ref=ag_send,
            dst_ref=ag_recv.at[my_owner],
            send_sem=ag_send_sem,
            recv_sem=ag_recv_sem,
            device_id={"wide": partner(chunk)},
            device_id_type=MESH,
        )

    @pl.when(is_owner)
    def _():
        rs_recv[members - 1] = rs_send[my_owner]
        arrived = rs_recv.at[pl.ds(0, members - 1)]
        dummy(arrived, arrived, rs_send_sem, rs_recv_sem).wait_recv()
        pair_buf[leaf] = jnp.sum(rs_recv[...], axis=0)
        swap = pltpu.make_async_remote_copy(
            src_ref=pair_buf.at[leaf],
            dst_ref=pair_buf.at[leaf],
            send_sem=core_send.at[2],
            recv_sem=core_recv.at[2],
            device_id={"leaf": 1 - leaf},
            device_id_type=MESH,
        )
        swap.start()
        swap.wait()

        def times(product, x, half):
            high, low = split(x)
            both = product(jnp.concatenate([high, low], axis=0), top_inv_high[half])
            return both[:own_rows] + both[own_rows:] + product(high, top_inv_low[half])

        solved0 = times(dot, -pair_buf[0], 0)
        solved1 = times(dot, -pair_buf[1] - dot(solved0.astype(BF16), top_coup[1]), 1)
        answer1 = times(dot_t, solved1, 1)
        answer0 = times(dot_t, solved0 - dot_t(answer1.astype(BF16), top_coup[1]), 0)
        ag_send[...] = jnp.where(leaf == 0, answer0, answer1)
        ag_recv[my_owner] = ag_send[...]

        for chunk in range(members - 1):
            ag_copy(chunk).start()

    for node in range(nodes):
        span = pl.ds(node * width, width)
        high, low = split(low_solved[:, span])
        value = dot_t(jnp.concatenate([high, low], axis=0), inv_high[node])
        base[:, span] = value[:sides] + value[sides:] + dot_t(high, inv_low[node])

    lax.fori_loop(nodes // 2, nodes, weigh, 0)

    @pl.when(is_owner)
    def _():
        arrived = ag_recv.at[pl.ds(0, owners - 1)]
        dummy(arrived, arrived, ag_send_sem, ag_recv_sem).wait_recv()

    @pl.when(jnp.logical_not(is_owner))
    def _():
        dummy(ag_recv, ag_recv, ag_send_sem, ag_recv_sem).wait_recv()

    for owner in range(owners):
        top_out_v[owner * own_rows : (owner + 1) * own_rows, :] = ag_recv[owner]
    sol_half[leaf] = top_out_v[...].astype(BF16)
    core_sol = pltpu.make_async_remote_copy(
        src_ref=sol_half.at[leaf],
        dst_ref=sol_half.at[leaf],
        send_sem=core_send.at[4],
        recv_sem=core_recv.at[4],
        device_id={"leaf": 1 - leaf},
        device_id_type=MESH,
    )
    core_sol.start()
    store_top = pltpu.make_async_copy(top_out_v, top_out_any, local_sem.at[2])
    store_top.start()
    core_sol.wait()

    for node in range(nodes):
        span = pl.ds(node * width, width)
        rows_here = slice(node * width, (node + 1) * width)
        term = dot_t(sol_half[0], weighed[rows_here, :width]) + dot_t(sol_half[1], weighed[rows_here, width:])
        value = (base[:, span] - term).astype(BF16)
        for piece in range(width // LANES):
            at = node * width + piece * LANES
            low_final[at // TILE, :, pl.ds(at % TILE, LANES)] = value[:, piece * LANES : (piece + 1) * LANES]

    for group in range(groups):
        for pair in range(group * group_pairs, (group + 1) * group_pairs):
            block = merge(low_final, choose_out[pair], high_out[pair : pair + 1], 0, None)
            store_chunks(back_send, pair * (TILE // 16), turned(block).astype(BF16))
        start_group(back, group)
    own_back.start()

    def store_out(part):
        span = pl.ds(part * 3 * TILE, 3 * TILE)
        return pltpu.make_async_copy(out_v.at[:, span], out_any.at[:, span], out_sem.at[part])

    for group in range(groups):
        wait_group(back_recv, back_recv_sem, group)
        if group == groups - 1:
            own_back.wait()
        block = back_recv[group * chunks : (group + 1) * chunks].reshape(group_rows, LANES)
        for tile in range(group_tiles):
            columns = block[tile * LANES : (tile + 1) * LANES].astype(F32).T
            turned_back[tile // 2, :, pl.ds((tile % 2) * LANES, LANES)] = columns[:sides].astype(BF16)

        for pair in range(pairs):
            span = pl.ds(pair * TILE, TILE)
            before = out_sum[:, span] if group > 0 else None
            value = merge(
                turned_back, choose_last[pair], high_last[pair : pair + 1], group * group_pairs, before
            )
            if group < groups - 1:
                out_sum[:, span] = value
            else:
                out_v[:, span] = value.astype(BF16)
                if pair % 3 == 2:
                    store_out(pair // 3).start()

    store_top.wait()
    for part in range(pairs // 3):
        store_out(part).wait()
    sent = pos_send.at[pl.ds(0, members - 1)]
    dummy(sent, sent, pos_send_sem, pos_send_sem).wait_send()
    sent = send_buf.at[pl.ds(0, members - 1)]
    dummy(sent, sent, there_send, there_send).wait_send()
    sent = back_send.at[pl.ds(0, members - 1)]
    dummy(sent, sent, back_send_sem, back_send_sem).wait_send()

    @pl.when(is_owner)
    def _():
        part = rs_send.at[pl.ds(0, owners - 1)]
        dummy(part, part, rs_send_sem, rs_send_sem).wait_send()
        part = rs_recv.at[pl.ds(0, members - 1)]
        dummy(part, part, ag_send_sem, ag_send_sem).wait_send()

    @pl.when(jnp.logical_not(is_owner))
    def _():
        dummy(rs_send, rs_send, rs_send_sem, rs_send_sem).wait_send()


def widen(low_ref, top_ref, out_ref, top_out_ref):
    out_ref[...] = low_ref[...].astype(F32)

    @pl.when(pl.program_id(0) == 0)
    def _():
        top_out_ref[...] = top_ref[...]


def shards(drop_sides, super_index, low_inverse, coupling, top_sides, top_inverse, top_coupling):
    sides, rows = drop_sides.shape
    nodes, width, _ = low_inverse.shape
    members = lax.axis_size("wide")
    cap = rows // members
    owners = 48
    top_cols = coupling.shape[1]
    tiles = rows // LANES
    own = sides // owners
    anyspace = pl.BlockSpec(memory_space=pl.ANY)
    dma = pltpu.SemaphoreType.DMA
    dims = (sides, rows, members, cap, nodes, width, owners)
    low, top = pl.pallas_call(
        functools.partial(kernel, dims),
        out_shape=(
            jax.ShapeDtypeStruct((sides, rows), BF16),
            jax.ShapeDtypeStruct(top_sides.shape, F32),
        ),
        in_specs=[anyspace] * 7,
        out_specs=(anyspace, anyspace),
        scratch_shapes=[
            pltpu.VMEM((tiles, LANES), jnp.int32),
            pltpu.VMEM((sides, width), F32),
            pltpu.VMEM((sides, rows), BF16),
            pltpu.VMEM((sides, width), F32),
            pltpu.VMEM((tiles * members, LANES), BF16),
            pltpu.VMEM((LANES, rows), BF16),
            pltpu.VMEM((LANES, rows), BF16),
            pltpu.VMEM((2 * members, rows), BF16),
            pltpu.VMEM((LANES, rows), BF16),
            pltpu.VMEM((nodes, width, width), F32),
            pltpu.VMEM((rows, top_cols), BF16),
            pltpu.VMEM((2, width, width), F32),
            pltpu.VMEM((2, width, width), BF16),
            pltpu.VMEM((2, width, width), BF16),
            pltpu.VMEM((2, width, width), BF16),
            pltpu.VMEM((nodes, width, width), BF16),
            pltpu.VMEM((nodes, width, width), BF16),
            pltpu.VMEM((tiles, LANES), F32),
            pltpu.VMEM((tiles, LANES), F32),
            pltpu.VMEM((tiles, LANES), F32),
            pltpu.VMEM((sides, rows), F32),
            pltpu.VMEM((rows // TILE, 2 * sides + 16, TILE), BF16),
            pltpu.VMEM((rows // TILE // 4, 2 * sides, TILE), BF16),
            pltpu.VMEM((members, 1, LANES), F32),
            pltpu.VMEM((members, 1, LANES), F32),
            pltpu.VMEM((rows // TILE, TILE, TILE), BF16),
            pltpu.VMEM((rows // TILE, TILE, TILE), BF16),
            pltpu.VMEM((rows // TILE, TILE, TILE), BF16),
            pltpu.VMEM((rows // TILE, TILE), F32),
            pltpu.VMEM((rows // TILE, TILE), F32),
            pltpu.VMEM((rows // TILE, TILE), F32),
            pltpu.VMEM((2 * sides, rows), F32),
            pltpu.VMEM((sides, rows), F32),
            pltpu.VMEM((sides, rows), F32),
            pltpu.VMEM((rows, top_cols), BF16),
            pltpu.VMEM((sides, rows), BF16),
            pltpu.VMEM((rows // TILE, sides, TILE), BF16),
            pltpu.VMEM((rows // TILE // 4, sides, TILE), BF16),
            pltpu.VMEM((sides, rows), F32),
            pltpu.VMEM((members, cap, LANES), jnp.int16),
            pltpu.VMEM((members, cap, LANES), jnp.int16),
            pltpu.VMEM((members, cap, LANES), BF16),
            pltpu.VMEM((members, cap, LANES), BF16),
            pltpu.VMEM((sides, width), F32),
            pltpu.VMEM((sides, width), F32),
            pltpu.VMEM((sides, width), F32),
            pltpu.VMEM((owners, own, width), F32),
            pltpu.VMEM((members, own, width), F32),
            pltpu.VMEM((2, own, width), F32),
            pltpu.VMEM((own, width), F32),
            pltpu.VMEM((owners, own, width), F32),
            pltpu.VMEM((2, sides, width), BF16),
            dma((7,)),
            dma((5,)),
            dma((5,)),
            dma((4,)),
            dma,
            dma((4,)),
            dma,
            dma,
            dma,
            dma((4,)),
            dma,
            dma,
            dma,
            dma,
            dma((4,)),
        ],
        compiler_params=pltpu.CompilerParams(
            collective_id=0, has_side_effects=True, vmem_limit_bytes=56 << 20
        ),
        name="substitution",
    )(
        super_index.reshape(tiles, LANES),
        drop_sides,
        low_inverse,
        coupling,
        top_sides,
        top_inverse,
        top_coupling,
    )
    return pl.pallas_call(
        widen,
        grid=(2,),
        out_shape=(jax.ShapeDtypeStruct((sides, rows), F32), jax.ShapeDtypeStruct(top_sides.shape, F32)),
        in_specs=[
            pl.BlockSpec((sides, rows // 2), lambda at: (0, at)),
            pl.BlockSpec(top_sides.shape, lambda at: (0, 0)),
        ],
        out_specs=(
            pl.BlockSpec((sides, rows // 2), lambda at: (0, at)),
            pl.BlockSpec(top_sides.shape, lambda at: (0, 0)),
        ),
        name="widen",
    )(low, top)


def solution(mesh):
    placed = (
        P(None, ("leaf", "wide")),
        P(("leaf", "wide")),
        P(("leaf", "wide"), None, None),
        P(("leaf", "wide"), None),
        P(None, "leaf"),
        P("leaf", None, None),
        P(None, "leaf", None, None),
    )
    return jax.shard_map(
        shards,
        mesh=mesh,
        in_specs=placed,
        out_specs=(P(None, ("leaf", "wide")), P(None, "leaf")),
        check_vma=False,
    )
```

```python
import functools
import random

import jax
import jax.numpy as jnp
from jax import lax
from jax.experimental import pallas as pl
from jax.experimental.pallas import tpu as pltpu
from jax.sharding import PartitionSpec as P

MESH = pl.DeviceIdType.MESH
F32 = jnp.float32
BF16 = jnp.bfloat16
LANES = 128
TILE = 256


def order_of_partners():
    steps = [(z, y, x) for z in range(4) for y in range(4) for x in range(4)][1:]
    random.Random(2).shuffle(steps)
    return sorted(steps, key=lambda step: -sum((0, 1, 2, 1)[one] for one in step)) + [(0, 0, 0)]


ORDER = order_of_partners()


def dot(a, b):
    return jnp.dot(a, b, preferred_element_type=F32)


def dot_t(a, b):
    return lax.dot_general(a, b, (((1,), (1,)), ((), ())), preferred_element_type=F32)


def split(x):
    high = x.astype(BF16)
    return high, (x - high.astype(F32)).astype(BF16)


def iota(shape, dim):
    return lax.broadcasted_iota(jnp.int32, shape, dim)


def onehot(rows, values):
    shape = (rows, values.shape[1])
    match = iota(shape, 0).astype(F32) == jnp.broadcast_to(values, shape)
    return jnp.where(match, 1.0, 0.0).astype(BF16)


def invert_step(high, low, place, rows):
    first = onehot(rows, high).astype(F32)
    lane = iota((rows, LANES), 1).astype(F32)
    left = jnp.concatenate([first * place, first * lane], axis=0).astype(BF16)
    return dot_t(left, onehot(LANES, low))


def pick(data_ref, source):
    blocks, height, _ = data_ref.shape
    high = jnp.floor(source * (1.0 / TILE))
    chooser = onehot(TILE, source - TILE * high)
    parts = dot(data_ref[...].reshape(blocks * height, TILE), chooser)
    result = parts[:height]
    for block in range(1, blocks):
        part = parts[block * height : (block + 1) * height]
        result = jnp.where(jnp.broadcast_to(high == float(block), part.shape), part, result)
    return result


def merge(data_ref, chooser, high, blocks, result):
    count, height, _ = data_ref.shape
    parts = dot(data_ref[...].reshape(count * height, TILE), chooser)
    for at in range(count):
        part = parts[at * height : (at + 1) * height]
        if result is None:
            result = part
        else:
            result = jnp.where(jnp.broadcast_to(high == float(blocks + at), part.shape), part, result)
    return result


def make_choosers(ref, chooser_ref, high_ref):
    def one(pair, _):
        source = row_pair(ref, pair)
        high = jnp.floor(source * (1.0 / TILE))
        chooser_ref[pair] = onehot(TILE, source - TILE * high)
        high_ref[pl.ds(pair, 1), :] = high
        return 0

    lax.fori_loop(0, chooser_ref.shape[0], one, 0)


def row_pair(ref, pair):
    two = ref[pl.ds(2 * pair, 2), :]
    return jnp.concatenate([two[0:1], two[1:2]], axis=1)


def turned(x):
    height = x.shape[0]
    if height < LANES:
        x = jnp.concatenate([x, jnp.zeros((LANES - height, x.shape[1]), x.dtype)], axis=0)
    return x.T


def kernel(
    dims,
    index_any,
    drop_any,
    inverse_any,
    coupling_any,
    top_sides_any,
    top_inverse_any,
    top_coupling_any,
    out_any,
    top_out_any,
    index_v,
    top_sides_v,
    out_v,
    top_out_v,
    here_ref,
    left_slot,
    right_slot,
    left_place,
    right_place,
    inverse_v,
    coupling_v,
    top_inv_f32,
    top_inv_high,
    top_inv_low,
    top_coup,
    inv_high,
    inv_low,
    slot_ref,
    source_ref,
    place_ref,
    drop_v,
    data,
    turned_in,
    pos_send,
    pos_recv,
    choose_in,
    choose_out,
    choose_last,
    high_in,
    high_out,
    high_last,
    super_n,
    low_solved,
    base,
    weighed,
    low_half,
    low_final,
    turned_back,
    out_sum,
    send_buf,
    recv_buf,
    back_send,
    back_recv,
    partial,
    half_send,
    half_recv,
    rs_send,
    rs_recv,
    pair_buf,
    ag_send,
    ag_recv,
    sol_half,
    load_sem,
    core_send,
    core_recv,
    local_sem,
    there_send,
    there_recv,
    pos_send_sem,
    pos_recv_sem,
    back_send_sem,
    back_recv_sem,
    rs_send_sem,
    rs_recv_sem,
    ag_send_sem,
    ag_recv_sem,
    out_sem,
):
    sides, rows, members, cap, nodes, width, owners = dims
    tiles = rows // LANES
    pairs = rows // TILE
    groups = 4
    chunks = members // groups
    group_rows = rows // groups
    group_pairs = pairs // groups
    group_tiles = tiles // groups
    own_rows = sides // owners
    me = lax.axis_index("wide")
    leaf = lax.axis_index("leaf")
    my_z, my_y, my_x = me // 16, lax.rem(me // 4, 4), lax.rem(me, 4)
    z_at = [16 * lax.rem(my_z + step, 4) for step in range(4)]
    y_at = [4 * lax.rem(my_y + step, 4) for step in range(4)]
    x_at = [lax.rem(my_x + step, 4) for step in range(4)]

    def partner(chunk):
        dz, dy, dx = ORDER[chunk]
        return z_at[dz] + y_at[dy] + x_at[dx]

    def origin(chunk):
        dz, dy, dx = ORDER[chunk]
        return z_at[(4 - dz) % 4] + y_at[(4 - dy) % 4] + x_at[(4 - dx) % 4]


    barrier = pltpu.get_barrier_semaphore()

    def greet(step, _):
        pl.semaphore_signal(
            barrier,
            inc=1,
            device_id={"wide": lax.rem(me + step, members)},
            device_id_type=MESH,
        )
        return 0

    lax.fori_loop(1, members, greet, 0)
    pl.semaphore_signal(barrier, inc=1, device_id={"leaf": 1 - leaf}, device_id_type=MESH)

    load_index = pltpu.make_async_copy(index_any, index_v, load_sem.at[5])
    load_sides = pltpu.make_async_copy(top_sides_any, top_sides_v, load_sem.at[6])
    load_drop = pltpu.make_async_copy(drop_any, drop_v, load_sem.at[4])
    load_inverse = pltpu.make_async_copy(inverse_any, inverse_v, load_sem.at[0])
    load_coupling = pltpu.make_async_copy(coupling_any, coupling_v, load_sem.at[1])
    load_top = pltpu.make_async_copy(top_inverse_any.at[0], top_inv_f32.at[leaf], load_sem.at[2])
    load_tc = pltpu.make_async_copy(top_coupling_any.at[0, 0], top_coup.at[leaf], load_sem.at[3])
    load_index.start()
    load_drop.start()
    load_inverse.start()
    load_coupling.start()
    load_top.start()
    load_tc.start()
    load_sides.start()

    order = jnp.zeros((members, LANES), F32)
    chunk_of = iota((members, LANES), 0)
    for chunk, (dz, dy, dx) in enumerate(ORDER):
        order = jnp.where(chunk_of == chunk, float(16 * dz + 4 * dy + dx), order)
    begin = (cap * chunk_of).astype(F32)
    below = (iota((LANES, LANES), 0) < iota((LANES, LANES), 1)).astype(F32)
    counter = jnp.concatenate([below, jnp.ones((LANES, LANES), F32)], axis=1).astype(BF16)
    load_index.wait()
    local = index_v[...] - leaf * (members * rows)
    target = ((local.astype(F32) + 0.5) * (1.0 / rows)).astype(jnp.int32)
    position = (local - target * rows).astype(F32)
    step_of = (
        16 * (((target >> 4) - my_z) & 3) + 4 * (((target >> 2) - my_y) & 3) + ((target - my_x) & 3)
    ).astype(F32)
    place_high = jnp.floor(position * (1.0 / LANES))
    place_low = position - LANES * place_high

    def here_of(tile):
        return jnp.where(order == step_of[tile : tile + 1], 1.0, 0.0)

    for tile in range(tiles):
        here_ref[tile * members : (tile + 1) * members, :] = here_of(tile).astype(BF16)
    counts = dot(here_ref[...], counter)
    carry = jnp.zeros((members, LANES), F32)
    lane = iota((tiles, LANES), 1).astype(F32)
    extras = []
    for tile in range(tiles):
        here = here_of(tile)
        count = counts[tile * members : (tile + 1) * members]
        rank = jnp.sum(here * (count[:, :LANES] + carry), axis=0, keepdims=True)
        slot = rank + jnp.sum(here * begin, axis=0, keepdims=True)
        carry = carry + count[:, LANES:]
        slot_ref[tile : tile + 1, :] = slot
        slot_high = jnp.floor(slot * (1.0 / LANES))
        span = pl.ds(tile * LANES, LANES)
        first = onehot(tiles, slot_high).astype(F32)
        left_slot[:, span] = jnp.concatenate(
            [first * float(tile), first * lane, jnp.zeros((LANES - 2 * tiles, LANES), F32)], axis=0
        ).astype(BF16)
        right_slot[:, span] = onehot(LANES, slot - LANES * slot_high)
        left_place[:, span] = jnp.concatenate(
            [here * place_high[tile : tile + 1], here * place_low[tile : tile + 1]], axis=0
        ).astype(BF16)
        right_place[:, span] = onehot(LANES, rank)
        extra = iota((16, LANES), 0)
        extras.append(
            jnp.where(
                extra == 0, place_high[tile : tile + 1], jnp.where(extra == 1, place_low[tile : tile + 1], 0.0)
            )
        )
    inverse_sum = dot_t(right_slot[...], left_slot[...]).T
    source_ref[...] = LANES * inverse_sum[:tiles] + inverse_sum[tiles : 2 * tiles]
    places = dot_t(left_place[...], right_place[...])
    places = jnp.where(iota((members, LANES), 1) < cap, LANES * places[:members] + places[members:], -1.0)
    for member in range(members):
        pos_send[member] = places[member : member + 1]
    pos_recv[members - 1] = places[members - 1 : members]

    load_drop.wait()
    for tile in range(tiles):
        block, lanes = tile // 2, pl.ds((tile % 2) * LANES, LANES)
        values = drop_v[:, tile * LANES : (tile + 1) * LANES]
        most = jnp.maximum(jnp.max(jnp.abs(values), axis=0, keepdims=True), 2.0**-100)
        power = jnp.ceil(jnp.log2(most) - 14.99)
        code = jnp.floor(values * jnp.exp2(-power) + 0.5)
        upper = jnp.floor(code * (1.0 / 256.0))
        data[block, 0:sides, lanes] = upper.astype(BF16)
        data[block, sides : 2 * sides, lanes] = (code - 256.0 * upper).astype(BF16)
        extra = jnp.where(iota((16, LANES), 0) == 2, power, extras[tile])
        data[block, 2 * sides : 2 * sides + 16, lanes] = extra.astype(BF16)

    def store_chunks(buf, first, block):
        for piece in range(TILE // 16):
            at = first + piece
            buf[at // 3, pl.ds(pl.multiple_of((at % 3) * 16, 16), 16), :] = block[
                piece * 16 : (piece + 1) * 16
            ]

    def pack(group):
        for pair in range(group * group_pairs, (group + 1) * group_pairs):
            block = pick(data, row_pair(source_ref, pair))
            code = jnp.concatenate(
                [256.0 * block[:sides] + block[sides : 2 * sides], block[2 * sides :]], axis=0
            )
            code = turned(code).astype(jnp.int32).astype(jnp.int16)
            store_chunks(send_buf, pair * (TILE // 16), code)

    pack(0)

    pl.semaphore_wait(barrier, members)

    def dummy(src, dst, send, recv):
        return pltpu.make_async_remote_copy(
            src_ref=src,
            dst_ref=dst,
            send_sem=send,
            recv_sem=recv,
            device_id={"wide": me},
            device_id_type=MESH,
        )

    def ahead(chunk):
        return pltpu.make_async_remote_copy(
            src_ref=pos_send.at[chunk],
            dst_ref=pos_recv.at[chunk],
            send_sem=pos_send_sem,
            recv_sem=pos_recv_sem,
            device_id={"wide": partner(chunk)},
            device_id_type=MESH,
        )

    for chunk in range(members - 1):
        ahead(chunk).start()

    load_top.wait()
    load_tc.wait()
    core_top = pltpu.make_async_remote_copy(
        src_ref=top_inv_f32.at[leaf],
        dst_ref=top_inv_f32.at[leaf],
        send_sem=core_send.at[0],
        recv_sem=core_recv.at[0],
        device_id={"leaf": 1 - leaf},
        device_id_type=MESH,
    )
    core_tc = pltpu.make_async_remote_copy(
        src_ref=top_coup.at[leaf],
        dst_ref=top_coup.at[leaf],
        send_sem=core_send.at[1],
        recv_sem=core_recv.at[1],
        device_id={"leaf": 1 - leaf},
        device_id_type=MESH,
    )
    core_top.start()
    core_tc.start()

    def there(chunk):
        return pltpu.make_async_remote_copy(
            src_ref=send_buf.at[chunk],
            dst_ref=recv_buf.at[chunk],
            send_sem=there_send,
            recv_sem=there_recv.at[chunk // chunks],
            device_id={"wide": partner(chunk)},
            device_id_type=MESH,
        )

    def back(chunk):
        return pltpu.make_async_remote_copy(
            src_ref=back_send.at[chunk],
            dst_ref=back_recv.at[chunk],
            send_sem=back_send_sem,
            recv_sem=back_recv_sem.at[chunk // chunks],
            device_id={"wide": origin(chunk)},
            device_id_type=MESH,
        )

    def start_group(copy, group):
        last = (group + 1) * chunks
        if group == groups - 1:
            last -= 1

        for chunk in range(group * chunks, last):
            copy(chunk).start()

    def wait_group(buf, sem, group, dst=True):
        count = chunks - 1 if group == groups - 1 else chunks
        part = buf.at[pl.ds(group * chunks, count)]
        pltpu.make_async_remote_copy(
            src_ref=part,
            dst_ref=part,
            send_sem=there_send,
            recv_sem=sem.at[group],
            device_id={"wide": me},
            device_id_type=MESH,
        ).wait_recv()

    own_there = pltpu.make_async_copy(
        send_buf.at[members - 1], recv_buf.at[members - 1], local_sem.at[0]
    )
    own_back = pltpu.make_async_copy(
        back_send.at[members - 1], back_recv.at[members - 1], local_sem.at[1]
    )

    start_group(there, 0)
    for group in range(1, groups):
        pack(group)
        start_group(there, group)
    own_there.start()

    load_inverse.wait()

    def halves(node, _):
        high, low = split(inverse_v[node])
        inv_high[node] = high
        inv_low[node] = low
        return 0

    lax.fori_loop(0, nodes, halves, 0)
    core_top.wait()
    core_tc.wait()
    for half in range(2):
        high, low = split(top_inv_f32[half])
        top_inv_high[half] = high
        top_inv_low[half] = low

    arrived = pos_recv.at[pl.ds(0, members - 1)]
    dummy(arrived, arrived, pos_send_sem, pos_recv_sem).wait_recv()
    lane = iota((1, LANES), 1)
    second = (lane >= LANES // 2).astype(F32)
    offset = lane.astype(F32) - second * (LANES // 2)
    inverse_sum = jnp.zeros((2 * tiles, LANES), F32)
    for member in range(members // 2):
        other = pltpu.roll(pos_recv[member + members // 2], LANES // 2, 1)
        place = jnp.where(lane < LANES // 2, pos_recv[member], other)
        high = jnp.floor(place * (1.0 / LANES))
        first = onehot(tiles, high).astype(F32)
        left = jnp.concatenate([first * (second * (members // 2) + float(member)), first * offset], axis=0)
        inverse_sum += dot_t(left.astype(BF16), onehot(LANES, place - LANES * high))
    source_ref[...] = cap * inverse_sum[:tiles] + inverse_sum[tiles:]
    make_choosers(source_ref, choose_in, high_in)
    make_choosers(slot_ref, choose_last, high_last)

    for group in range(groups):
        wait_group(recv_buf, there_recv, group)
        if group == groups - 1:
            own_there.wait()
        for tile in range(group_tiles):
            at = group * group_tiles + tile
            first = group * chunks + (tile * LANES) // cap
            last = group * chunks + ((tile + 1) * LANES - 1) // cap
            skip = (tile * LANES) % cap
            block = recv_buf[first : last + 1].astype(jnp.int32).astype(F32)
            columns = block.reshape((last + 1 - first) * cap, LANES)[skip : skip + LANES].T
            place_ref[at : at + 1, :] = LANES * columns[sides : sides + 1] + columns[sides + 1 : sides + 2]
            values = columns[:sides] * jnp.exp2(columns[sides + 2 : sides + 3])
            high, low = split(values)
            lanes = pl.ds((tile % 2) * LANES, LANES)
            turned_in[tile // 2, :sides, lanes] = high
            turned_in[tile // 2, sides:, lanes] = low

        for pair in range(pairs):
            span = pl.ds(pair * TILE, TILE)
            before = super_n[:, span] if group > 0 else None
            super_n[:, span] = merge(
                turned_in, choose_in[pair], high_in[pair : pair + 1], group * group_pairs, before
            )

    for node in range(nodes):
        span = pl.ds(node * width, width)
        side = super_n[:, span].astype(BF16)
        value = dot(side, inv_high[node])
        value = value[:sides] + value[sides:] + dot(side[:sides], inv_low[node])
        low_solved[:, span] = value
        low_half[:, span] = value.astype(BF16)

    load_coupling.wait()

    def half_sum(half):
        return dot(low_half[...], coupling_v[:, pl.ds(pl.multiple_of(half * width, LANES), width)])

    half_send[...] = half_sum(1 - leaf)
    core_half = pltpu.make_async_remote_copy(
        src_ref=half_send,
        dst_ref=half_recv,
        send_sem=core_send.at[3],
        recv_sem=core_recv.at[3],
        device_id={"leaf": 1 - leaf},
        device_id_type=MESH,
    )
    core_half.start()
    first = jnp.where(me == 0, 1.0, 0.0).astype(F32)
    load_sides.wait()
    partial[...] = half_sum(leaf) - top_sides_v[...] * first
    core_half.wait()
    partial[...] = partial[...] + half_recv[...]
    for owner in range(owners):
        rs_send[owner] = partial[owner * own_rows : (owner + 1) * own_rows, :]

    def turn_of(chip):
        line = chip // 4
        return lax.rem(chip - 4 * line + 8 * members - line - line // 4, 4)

    my_turn = turn_of(me)
    is_owner = my_turn < 3
    my_owner = 3 * (me // 4) + jnp.minimum(my_turn, 2)

    def send_part(chunk):
        chip = partner(chunk)
        turn = turn_of(chip)

        @pl.when(turn < 3)
        def _():
            pltpu.make_async_remote_copy(
                src_ref=rs_send.at[3 * (chip // 4) + jnp.minimum(turn, 2)],
                dst_ref=rs_recv.at[chunk],
                send_sem=rs_send_sem,
                recv_sem=rs_recv_sem,
                device_id={"wide": chip},
                device_id_type=MESH,
            ).start()

    for chunk in range(members - 1):
        send_part(chunk)
    make_choosers(place_ref, choose_out, high_out)

    def weigh(node, _):
        span = pl.ds(pl.multiple_of(node * width, width), width)
        block = coupling_v[span, :]
        weighed[span, :] = (dot(inv_high[node], block) + dot(inv_low[node], block)).astype(BF16)
        return 0

    lax.fori_loop(0, nodes // 2, weigh, 0)

    def ag_copy(chunk):
        return pltpu.make_async_remote_copy(
            src_ref=ag_send,
            dst_ref=ag_recv.at[my_owner],
            send_sem=ag_send_sem,
            recv_sem=ag_recv_sem,
            device_id={"wide": partner(chunk)},
            device_id_type=MESH,
        )

    @pl.when(is_owner)
    def _():
        rs_recv[members - 1] = rs_send[my_owner]
        arrived = rs_recv.at[pl.ds(0, members - 1)]
        dummy(arrived, arrived, rs_send_sem, rs_recv_sem).wait_recv()
        pair_buf[leaf] = jnp.sum(rs_recv[...], axis=0)
        swap = pltpu.make_async_remote_copy(
            src_ref=pair_buf.at[leaf],
            dst_ref=pair_buf.at[leaf],
            send_sem=core_send.at[2],
            recv_sem=core_recv.at[2],
            device_id={"leaf": 1 - leaf},
            device_id_type=MESH,
        )
        swap.start()
        swap.wait()

        def times(product, x, half):
            high, low = split(x)
            both = product(jnp.concatenate([high, low], axis=0), top_inv_high[half])
            return both[:own_rows] + both[own_rows:] + product(high, top_inv_low[half])

        solved0 = times(dot, -pair_buf[0], 0)
        solved1 = times(dot, -pair_buf[1] - dot(solved0.astype(BF16), top_coup[1]), 1)
        answer1 = times(dot_t, solved1, 1)
        answer0 = times(dot_t, solved0 - dot_t(answer1.astype(BF16), top_coup[1]), 0)
        ag_send[...] = jnp.where(leaf == 0, answer0, answer1)
        ag_recv[my_owner] = ag_send[...]

        for chunk in range(members - 1):
            ag_copy(chunk).start()

    for node in range(nodes):
        span = pl.ds(node * width, width)
        high, low = split(low_solved[:, span])
        value = dot_t(jnp.concatenate([high, low], axis=0), inv_high[node])
        base[:, span] = value[:sides] + value[sides:] + dot_t(high, inv_low[node])

    lax.fori_loop(nodes // 2, nodes, weigh, 0)

    @pl.when(is_owner)
    def _():
        arrived = ag_recv.at[pl.ds(0, owners - 1)]
        dummy(arrived, arrived, ag_send_sem, ag_recv_sem).wait_recv()

    @pl.when(jnp.logical_not(is_owner))
    def _():
        dummy(ag_recv, ag_recv, ag_send_sem, ag_recv_sem).wait_recv()

    for owner in range(owners):
        top_out_v[owner * own_rows : (owner + 1) * own_rows, :] = ag_recv[owner]
    sol_half[leaf] = top_out_v[...].astype(BF16)
    core_sol = pltpu.make_async_remote_copy(
        src_ref=sol_half.at[leaf],
        dst_ref=sol_half.at[leaf],
        send_sem=core_send.at[4],
        recv_sem=core_recv.at[4],
        device_id={"leaf": 1 - leaf},
        device_id_type=MESH,
    )
    core_sol.start()
    store_top = pltpu.make_async_copy(top_out_v, top_out_any, local_sem.at[2])
    store_top.start()

    own_half = pl.ds(pl.multiple_of(leaf * width, LANES), width)
    other_half = pl.ds(pl.multiple_of((1 - leaf) * width, LANES), width)
    for node in range(nodes):
        span = pl.ds(node * width, width)
        base[:, span] = base[:, span] - dot_t(sol_half[leaf], weighed[node * width : (node + 1) * width, own_half])
    core_sol.wait()

    for node in range(nodes):
        span = pl.ds(node * width, width)
        rows_here = slice(node * width, (node + 1) * width)
        term = dot_t(sol_half[1 - leaf], weighed[rows_here, other_half])
        value = (base[:, span] - term).astype(BF16)
        for piece in range(width // LANES):
            at = node * width + piece * LANES
            low_final[at // TILE, :, pl.ds(at % TILE, LANES)] = value[:, piece * LANES : (piece + 1) * LANES]

    for half in range(2):
        for pair in range(half * pairs // 2, (half + 1) * pairs // 2):
            block = merge(low_final, choose_out[pair], high_out[pair : pair + 1], 0, None)
            store_chunks(back_send, pair * (TILE // 16), turned(block).astype(BF16))
        start_group(back, 2 * half)
        start_group(back, 2 * half + 1)
    own_back.start()

    def store_out(part):
        span = pl.ds(part * 3 * TILE, 3 * TILE)
        return pltpu.make_async_copy(out_v.at[:, span], out_any.at[:, span], out_sem.at[part])

    for group in range(groups):
        wait_group(back_recv, back_recv_sem, group)
        if group == groups - 1:
            own_back.wait()
        block = back_recv[group * chunks : (group + 1) * chunks].reshape(group_rows, LANES)
        for tile in range(group_tiles):
            columns = block[tile * LANES : (tile + 1) * LANES].astype(F32).T
            turned_back[tile // 2, :, pl.ds((tile % 2) * LANES, LANES)] = columns[:sides].astype(BF16)

        for pair in range(pairs):
            span = pl.ds(pair * TILE, TILE)
            before = out_sum[:, span] if group > 0 else None
            value = merge(
                turned_back, choose_last[pair], high_last[pair : pair + 1], group * group_pairs, before
            )
            if group < groups - 1:
                out_sum[:, span] = value
            else:
                out_v[:, span] = value.astype(BF16)
                if pair % 3 == 2:
                    store_out(pair // 3).start()

    store_top.wait()
    for part in range(pairs // 3):
        store_out(part).wait()
    sent = pos_send.at[pl.ds(0, members - 1)]
    dummy(sent, sent, pos_send_sem, pos_send_sem).wait_send()
    sent = send_buf.at[pl.ds(0, members - 1)]
    dummy(sent, sent, there_send, there_send).wait_send()
    sent = back_send.at[pl.ds(0, members - 1)]
    dummy(sent, sent, back_send_sem, back_send_sem).wait_send()

    @pl.when(is_owner)
    def _():
        part = rs_send.at[pl.ds(0, owners - 1)]
        dummy(part, part, rs_send_sem, rs_send_sem).wait_send()
        part = rs_recv.at[pl.ds(0, members - 1)]
        dummy(part, part, ag_send_sem, ag_send_sem).wait_send()

    @pl.when(jnp.logical_not(is_owner))
    def _():
        dummy(rs_send, rs_send, rs_send_sem, rs_send_sem).wait_send()


def widen(low_ref, top_ref, out_ref, top_out_ref):
    out_ref[...] = low_ref[...].astype(F32)

    @pl.when(pl.program_id(0) == 0)
    def _():
        top_out_ref[...] = top_ref[...]


def shards(drop_sides, super_index, low_inverse, coupling, top_sides, top_inverse, top_coupling):
    sides, rows = drop_sides.shape
    nodes, width, _ = low_inverse.shape
    members = lax.axis_size("wide")
    cap = rows // members
    owners = 48
    top_cols = coupling.shape[1]
    tiles = rows // LANES
    own = sides // owners
    anyspace = pl.BlockSpec(memory_space=pl.ANY)
    dma = pltpu.SemaphoreType.DMA
    dims = (sides, rows, members, cap, nodes, width, owners)
    low, top = pl.pallas_call(
        functools.partial(kernel, dims),
        out_shape=(
            jax.ShapeDtypeStruct((sides, rows), BF16),
            jax.ShapeDtypeStruct(top_sides.shape, F32),
        ),
        in_specs=[anyspace] * 7,
        out_specs=(anyspace, anyspace),
        scratch_shapes=[
            pltpu.VMEM((tiles, LANES), jnp.int32),
            pltpu.VMEM((sides, width), F32),
            pltpu.VMEM((sides, rows), BF16),
            pltpu.VMEM((sides, width), F32),
            pltpu.VMEM((tiles * members, LANES), BF16),
            pltpu.VMEM((LANES, rows), BF16),
            pltpu.VMEM((LANES, rows), BF16),
            pltpu.VMEM((2 * members, rows), BF16),
            pltpu.VMEM((LANES, rows), BF16),
            pltpu.VMEM((nodes, width, width), F32),
            pltpu.VMEM((rows, top_cols), BF16),
            pltpu.VMEM((2, width, width), F32),
            pltpu.VMEM((2, width, width), BF16),
            pltpu.VMEM((2, width, width), BF16),
            pltpu.VMEM((2, width, width), BF16),
            pltpu.VMEM((nodes, width, width), BF16),
            pltpu.VMEM((nodes, width, width), BF16),
            pltpu.VMEM((tiles, LANES), F32),
            pltpu.VMEM((tiles, LANES), F32),
            pltpu.VMEM((tiles, LANES), F32),
            pltpu.VMEM((sides, rows), F32),
            pltpu.VMEM((rows // TILE, 2 * sides + 16, TILE), BF16),
            pltpu.VMEM((rows // TILE // 4, 2 * sides, TILE), BF16),
            pltpu.VMEM((members, 1, LANES), F32),
            pltpu.VMEM((members, 1, LANES), F32),
            pltpu.VMEM((rows // TILE, TILE, TILE), BF16),
            pltpu.VMEM((rows // TILE, TILE, TILE), BF16),
            pltpu.VMEM((rows // TILE, TILE, TILE), BF16),
            pltpu.VMEM((rows // TILE, TILE), F32),
            pltpu.VMEM((rows // TILE, TILE), F32),
            pltpu.VMEM((rows // TILE, TILE), F32),
            pltpu.VMEM((2 * sides, rows), F32),
            pltpu.VMEM((sides, rows), F32),
            pltpu.VMEM((sides, rows), F32),
            pltpu.VMEM((rows, top_cols), BF16),
            pltpu.VMEM((sides, rows), BF16),
            pltpu.VMEM((rows // TILE, sides, TILE), BF16),
            pltpu.VMEM((rows // TILE // 4, sides, TILE), BF16),
            pltpu.VMEM((sides, rows), F32),
            pltpu.VMEM((members, cap, LANES), jnp.int16),
            pltpu.VMEM((members, cap, LANES), jnp.int16),
            pltpu.VMEM((members, cap, LANES), BF16),
            pltpu.VMEM((members, cap, LANES), BF16),
            pltpu.VMEM((sides, width), F32),
            pltpu.VMEM((sides, width), F32),
            pltpu.VMEM((sides, width), F32),
            pltpu.VMEM((owners, own, width), F32),
            pltpu.VMEM((members, own, width), F32),
            pltpu.VMEM((2, own, width), F32),
            pltpu.VMEM((own, width), F32),
            pltpu.VMEM((owners, own, width), F32),
            pltpu.VMEM((2, sides, width), BF16),
            dma((7,)),
            dma((5,)),
            dma((5,)),
            dma((4,)),
            dma,
            dma((4,)),
            dma,
            dma,
            dma,
            dma((4,)),
            dma,
            dma,
            dma,
            dma,
            dma((4,)),
        ],
        compiler_params=pltpu.CompilerParams(
            collective_id=0, has_side_effects=True, vmem_limit_bytes=56 << 20
        ),
        name="substitution",
    )(
        super_index.reshape(tiles, LANES),
        drop_sides,
        low_inverse,
        coupling,
        top_sides,
        top_inverse,
        top_coupling,
    )
    return pl.pallas_call(
        widen,
        grid=(2,),
        out_shape=(jax.ShapeDtypeStruct((sides, rows), F32), jax.ShapeDtypeStruct(top_sides.shape, F32)),
        in_specs=[
            pl.BlockSpec((sides, rows // 2), lambda at: (0, at)),
            pl.BlockSpec(top_sides.shape, lambda at: (0, 0)),
        ],
        out_specs=(
            pl.BlockSpec((sides, rows // 2), lambda at: (0, at)),
            pl.BlockSpec(top_sides.shape, lambda at: (0, 0)),
        ),
        name="widen",
    )(low, top)


def solution(mesh):
    placed = (
        P(None, ("leaf", "wide")),
        P(("leaf", "wide")),
        P(("leaf", "wide"), None, None),
        P(("leaf", "wide"), None),
        P(None, "leaf"),
        P("leaf", None, None),
        P(None, "leaf", None, None),
    )
    return jax.shard_map(
        shards,
        mesh=mesh,
        in_specs=placed,
        out_specs=(P(None, ("leaf", "wide")), P(None, "leaf")),
        check_vma=False,
    )
```

```python
import functools
import random

import jax
import jax.numpy as jnp
from jax import lax
from jax.experimental import pallas as pl
from jax.experimental.pallas import tpu as pltpu
from jax.sharding import PartitionSpec as P

MESH = pl.DeviceIdType.MESH
F32 = jnp.float32
BF16 = jnp.bfloat16
LANES = 128
TILE = 256


def order_of_partners():
    steps = [(z, y, x) for z in range(4) for y in range(4) for x in range(4)][1:]
    random.Random(2).shuffle(steps)
    return sorted(steps, key=lambda step: -sum((0, 1, 2, 1)[one] for one in step)) + [(0, 0, 0)]


ORDER = order_of_partners()


def dot(a, b):
    return jnp.dot(a, b, preferred_element_type=F32)


def dot_t(a, b):
    return lax.dot_general(a, b, (((1,), (1,)), ((), ())), preferred_element_type=F32)


def split(x):
    high = x.astype(BF16)
    return high, (x - high.astype(F32)).astype(BF16)


def iota(shape, dim):
    return lax.broadcasted_iota(jnp.int32, shape, dim)


def onehot(rows, values):
    shape = (rows, values.shape[1])
    match = iota(shape, 0).astype(F32) == jnp.broadcast_to(values, shape)
    return jnp.where(match, 1.0, 0.0).astype(BF16)


def invert_step(high, low, place, rows):
    first = onehot(rows, high).astype(F32)
    lane = iota((rows, LANES), 1).astype(F32)
    left = jnp.concatenate([first * place, first * lane], axis=0).astype(BF16)
    return dot_t(left, onehot(LANES, low))


def pick(data_ref, source):
    blocks, height, _ = data_ref.shape
    high = jnp.floor(source * (1.0 / TILE))
    chooser = onehot(TILE, source - TILE * high)
    parts = dot(data_ref[...].reshape(blocks * height, TILE), chooser)
    result = parts[:height]
    for block in range(1, blocks):
        part = parts[block * height : (block + 1) * height]
        result = jnp.where(jnp.broadcast_to(high == float(block), part.shape), part, result)
    return result


def merge(data_ref, chooser, high, blocks, result):
    count, height, _ = data_ref.shape
    parts = dot(data_ref[...].reshape(count * height, TILE), chooser)
    for at in range(count):
        part = parts[at * height : (at + 1) * height]
        if result is None:
            result = part
        else:
            result = jnp.where(jnp.broadcast_to(high == float(blocks + at), part.shape), part, result)
    return result


def make_choosers(ref, chooser_ref, high_ref):
    def one(pair, _):
        source = row_pair(ref, pair)
        high = jnp.floor(source * (1.0 / TILE))
        chooser_ref[pair] = onehot(TILE, source - TILE * high)
        high_ref[pl.ds(pair, 1), :] = high
        return 0

    lax.fori_loop(0, chooser_ref.shape[0], one, 0)


def row_pair(ref, pair):
    two = ref[pl.ds(2 * pair, 2), :]
    return jnp.concatenate([two[0:1], two[1:2]], axis=1)


def turned(x):
    height = x.shape[0]
    if height < LANES:
        x = jnp.concatenate([x, jnp.zeros((LANES - height, x.shape[1]), x.dtype)], axis=0)
    return x.T


def kernel(
    dims,
    index_any,
    drop_any,
    inverse_any,
    coupling_any,
    top_sides_any,
    top_inverse_any,
    top_coupling_any,
    out_any,
    top_out_any,
    index_v,
    top_sides_v,
    out_v,
    top_out_v,
    here_ref,
    left_slot,
    right_slot,
    left_place,
    right_place,
    inverse_v,
    coupling_v,
    top_inv_f32,
    top_inv_high,
    top_inv_low,
    top_coup,
    inv_high,
    inv_low,
    slot_ref,
    source_ref,
    place_ref,
    drop_v,
    data,
    turned_in,
    pos_send,
    pos_recv,
    choose_in,
    choose_out,
    choose_last,
    high_in,
    high_out,
    high_last,
    super_n,
    low_solved,
    base,
    weighed,
    low_half,
    low_final,
    turned_back,
    out_sum,
    send_buf,
    recv_buf,
    back_send,
    back_recv,
    partial,
    half_send,
    half_recv,
    rs_send,
    rs_recv,
    pair_buf,
    ag_send,
    ag_recv,
    sol_half,
    load_sem,
    core_send,
    core_recv,
    local_sem,
    there_send,
    there_recv,
    pos_send_sem,
    pos_recv_sem,
    back_send_sem,
    back_recv_sem,
    rs_send_sem,
    rs_recv_sem,
    ag_send_sem,
    ag_recv_sem,
    out_sem,
):
    sides, rows, members, cap, nodes, width, owners = dims
    tiles = rows // LANES
    pairs = rows // TILE
    groups = 4
    chunks = members // groups
    group_rows = rows // groups
    group_pairs = pairs // groups
    group_tiles = tiles // groups
    own_rows = sides // owners
    me = lax.axis_index("wide")
    leaf = lax.axis_index("leaf")
    my_z, my_y, my_x = me // 16, lax.rem(me // 4, 4), lax.rem(me, 4)
    z_at = [16 * lax.rem(my_z + step, 4) for step in range(4)]
    y_at = [4 * lax.rem(my_y + step, 4) for step in range(4)]
    x_at = [lax.rem(my_x + step, 4) for step in range(4)]

    def partner(chunk):
        dz, dy, dx = ORDER[chunk]
        return z_at[dz] + y_at[dy] + x_at[dx]

    def origin(chunk):
        dz, dy, dx = ORDER[chunk]
        return z_at[(4 - dz) % 4] + y_at[(4 - dy) % 4] + x_at[(4 - dx) % 4]


    barrier = pltpu.get_barrier_semaphore()

    def greet(step, _):
        pl.semaphore_signal(
            barrier,
            inc=1,
            device_id={"wide": lax.rem(me + step, members)},
            device_id_type=MESH,
        )
        return 0

    lax.fori_loop(1, members, greet, 0)
    pl.semaphore_signal(barrier, inc=1, device_id={"leaf": 1 - leaf}, device_id_type=MESH)

    load_index = pltpu.make_async_copy(index_any, index_v, load_sem.at[5])
    load_sides = pltpu.make_async_copy(top_sides_any, top_sides_v, load_sem.at[6])
    load_drop = pltpu.make_async_copy(drop_any, drop_v, load_sem.at[4])
    load_inverse = pltpu.make_async_copy(inverse_any, inverse_v, load_sem.at[0])
    load_coupling = pltpu.make_async_copy(coupling_any, coupling_v, load_sem.at[1])
    load_top = pltpu.make_async_copy(top_inverse_any.at[0], top_inv_f32.at[leaf], load_sem.at[2])
    load_tc = pltpu.make_async_copy(top_coupling_any.at[0, 0], top_coup.at[leaf], load_sem.at[3])
    load_index.start()
    load_drop.start()
    load_inverse.start()
    load_coupling.start()
    load_top.start()
    load_tc.start()
    load_sides.start()

    order = jnp.zeros((members, LANES), F32)
    chunk_of = iota((members, LANES), 0)
    for chunk, (dz, dy, dx) in enumerate(ORDER):
        order = jnp.where(chunk_of == chunk, float(16 * dz + 4 * dy + dx), order)
    begin = (cap * chunk_of).astype(F32)
    below = (iota((LANES, LANES), 0) < iota((LANES, LANES), 1)).astype(F32)
    counter = jnp.concatenate([below, jnp.ones((LANES, LANES), F32)], axis=1).astype(BF16)
    load_index.wait()
    local = index_v[...] - leaf * (members * rows)
    target = ((local.astype(F32) + 0.5) * (1.0 / rows)).astype(jnp.int32)
    position = (local - target * rows).astype(F32)
    step_of = (
        16 * (((target >> 4) - my_z) & 3) + 4 * (((target >> 2) - my_y) & 3) + ((target - my_x) & 3)
    ).astype(F32)
    place_high = jnp.floor(position * (1.0 / LANES))
    place_low = position - LANES * place_high

    def here_of(tile):
        return jnp.where(order == step_of[tile : tile + 1], 1.0, 0.0)

    for tile in range(tiles):
        here_ref[tile * members : (tile + 1) * members, :] = here_of(tile).astype(BF16)
    counts = dot(here_ref[...], counter)
    carry = jnp.zeros((members, LANES), F32)
    lane = iota((tiles, LANES), 1).astype(F32)
    extras = []
    for tile in range(tiles):
        here = here_of(tile)
        count = counts[tile * members : (tile + 1) * members]
        rank = jnp.sum(here * (count[:, :LANES] + carry), axis=0, keepdims=True)
        slot = rank + jnp.sum(here * begin, axis=0, keepdims=True)
        carry = carry + count[:, LANES:]
        slot_ref[tile : tile + 1, :] = slot
        slot_high = jnp.floor(slot * (1.0 / LANES))
        span = pl.ds(tile * LANES, LANES)
        first = onehot(tiles, slot_high).astype(F32)
        left_slot[:, span] = jnp.concatenate(
            [first * float(tile), first * lane, jnp.zeros((LANES - 2 * tiles, LANES), F32)], axis=0
        ).astype(BF16)
        right_slot[:, span] = onehot(LANES, slot - LANES * slot_high)
        left_place[:, span] = jnp.concatenate(
            [here * place_high[tile : tile + 1], here * place_low[tile : tile + 1]], axis=0
        ).astype(BF16)
        right_place[:, span] = onehot(LANES, rank)
        extra = iota((16, LANES), 0)
        extras.append(
            jnp.where(
                extra == 0, place_high[tile : tile + 1], jnp.where(extra == 1, place_low[tile : tile + 1], 0.0)
            )
        )
    inverse_sum = dot_t(right_slot[...], left_slot[...]).T
    source_ref[...] = LANES * inverse_sum[:tiles] + inverse_sum[tiles : 2 * tiles]
    places = dot_t(left_place[...], right_place[...])
    places = jnp.where(iota((members, LANES), 1) < cap, LANES * places[:members] + places[members:], -1.0)
    for member in range(members):
        pos_send[member] = places[member : member + 1]
    pos_recv[members - 1] = places[members - 1 : members]

    load_drop.wait()
    for tile in range(tiles):
        block, lanes = tile // 2, pl.ds((tile % 2) * LANES, LANES)
        values = drop_v[:, tile * LANES : (tile + 1) * LANES]
        most = jnp.maximum(jnp.max(jnp.abs(values), axis=0, keepdims=True), 2.0**-100)
        power = jnp.ceil(jnp.log2(most) - 14.99)
        code = jnp.floor(values * jnp.exp2(-power) + 0.5)
        upper = jnp.floor(code * (1.0 / 256.0))
        data[block, 0:sides, lanes] = upper.astype(BF16)
        data[block, sides : 2 * sides, lanes] = (code - 256.0 * upper).astype(BF16)
        extra = jnp.where(iota((16, LANES), 0) == 2, power, extras[tile])
        data[block, 2 * sides : 2 * sides + 16, lanes] = extra.astype(BF16)

    def store_chunks(buf, first, block):
        for piece in range(TILE // 16):
            at = first + piece
            buf[at // 3, pl.ds(pl.multiple_of((at % 3) * 16, 16), 16), :] = block[
                piece * 16 : (piece + 1) * 16
            ]

    def pack(group):
        for pair in range(group * group_pairs, (group + 1) * group_pairs):
            block = pick(data, row_pair(source_ref, pair))
            code = jnp.concatenate(
                [256.0 * block[:sides] + block[sides : 2 * sides], block[2 * sides :]], axis=0
            )
            code = turned(code).astype(jnp.int32).astype(jnp.int16)
            store_chunks(send_buf, pair * (TILE // 16), code)

    pack(0)

    pl.semaphore_wait(barrier, members)

    def dummy(src, dst, send, recv):
        return pltpu.make_async_remote_copy(
            src_ref=src,
            dst_ref=dst,
            send_sem=send,
            recv_sem=recv,
            device_id={"wide": me},
            device_id_type=MESH,
        )

    def ahead(chunk):
        return pltpu.make_async_remote_copy(
            src_ref=pos_send.at[chunk],
            dst_ref=pos_recv.at[chunk],
            send_sem=pos_send_sem,
            recv_sem=pos_recv_sem,
            device_id={"wide": partner(chunk)},
            device_id_type=MESH,
        )

    for chunk in range(members - 1):
        ahead(chunk).start()


    def there(chunk):
        return pltpu.make_async_remote_copy(
            src_ref=send_buf.at[chunk],
            dst_ref=recv_buf.at[chunk],
            send_sem=there_send,
            recv_sem=there_recv.at[chunk // chunks],
            device_id={"wide": partner(chunk)},
            device_id_type=MESH,
        )

    def back(chunk):
        return pltpu.make_async_remote_copy(
            src_ref=back_send.at[chunk],
            dst_ref=back_recv.at[chunk],
            send_sem=back_send_sem,
            recv_sem=back_recv_sem.at[chunk // chunks],
            device_id={"wide": origin(chunk)},
            device_id_type=MESH,
        )

    def start_group(copy, group):
        last = (group + 1) * chunks
        if group == groups - 1:
            last -= 1

        for chunk in range(group * chunks, last):
            copy(chunk).start()

    def wait_group(buf, sem, group, dst=True):
        count = chunks - 1 if group == groups - 1 else chunks
        part = buf.at[pl.ds(group * chunks, count)]
        pltpu.make_async_remote_copy(
            src_ref=part,
            dst_ref=part,
            send_sem=there_send,
            recv_sem=sem.at[group],
            device_id={"wide": me},
            device_id_type=MESH,
        ).wait_recv()

    own_there = pltpu.make_async_copy(
        send_buf.at[members - 1], recv_buf.at[members - 1], local_sem.at[0]
    )
    own_back = pltpu.make_async_copy(
        back_send.at[members - 1], back_recv.at[members - 1], local_sem.at[1]
    )

    start_group(there, 0)
    for group in range(1, groups):
        pack(group)
        start_group(there, group)
    own_there.start()

    load_top.wait()
    load_tc.wait()
    core_top = pltpu.make_async_remote_copy(
        src_ref=top_inv_f32.at[leaf],
        dst_ref=top_inv_f32.at[leaf],
        send_sem=core_send.at[0],
        recv_sem=core_recv.at[0],
        device_id={"leaf": 1 - leaf},
        device_id_type=MESH,
    )
    core_tc = pltpu.make_async_remote_copy(
        src_ref=top_coup.at[leaf],
        dst_ref=top_coup.at[leaf],
        send_sem=core_send.at[1],
        recv_sem=core_recv.at[1],
        device_id={"leaf": 1 - leaf},
        device_id_type=MESH,
    )
    core_top.start()
    core_tc.start()

    load_inverse.wait()

    def halves(node, _):
        high, low = split(inverse_v[node])
        inv_high[node] = high
        inv_low[node] = low
        return 0

    lax.fori_loop(0, nodes, halves, 0)
    arrived = pos_recv.at[pl.ds(0, members - 1)]
    dummy(arrived, arrived, pos_send_sem, pos_recv_sem).wait_recv()
    lane = iota((1, LANES), 1)
    second = (lane >= LANES // 2).astype(F32)
    offset = lane.astype(F32) - second * (LANES // 2)
    inverse_sum = jnp.zeros((2 * tiles, LANES), F32)
    for member in range(members // 2):
        other = pltpu.roll(pos_recv[member + members // 2], LANES // 2, 1)
        place = jnp.where(lane < LANES // 2, pos_recv[member], other)
        high = jnp.floor(place * (1.0 / LANES))
        first = onehot(tiles, high).astype(F32)
        left = jnp.concatenate([first * (second * (members // 2) + float(member)), first * offset], axis=0)
        inverse_sum += dot_t(left.astype(BF16), onehot(LANES, place - LANES * high))
    source_ref[...] = cap * inverse_sum[:tiles] + inverse_sum[tiles:]
    make_choosers(source_ref, choose_in, high_in)
    make_choosers(slot_ref, choose_last, high_last)

    for group in range(groups):
        wait_group(recv_buf, there_recv, group)
        if group == groups - 1:
            own_there.wait()
        for tile in range(group_tiles):
            at = group * group_tiles + tile
            first = group * chunks + (tile * LANES) // cap
            last = group * chunks + ((tile + 1) * LANES - 1) // cap
            skip = (tile * LANES) % cap
            block = recv_buf[first : last + 1].astype(jnp.int32).astype(F32)
            columns = block.reshape((last + 1 - first) * cap, LANES)[skip : skip + LANES].T
            place_ref[at : at + 1, :] = LANES * columns[sides : sides + 1] + columns[sides + 1 : sides + 2]
            values = columns[:sides] * jnp.exp2(columns[sides + 2 : sides + 3])
            high, low = split(values)
            lanes = pl.ds((tile % 2) * LANES, LANES)
            turned_in[tile // 2, :sides, lanes] = high
            turned_in[tile // 2, sides:, lanes] = low

        for pair in range(pairs):
            span = pl.ds(pair * TILE, TILE)
            before = super_n[:, span] if group > 0 else None
            super_n[:, span] = merge(
                turned_in, choose_in[pair], high_in[pair : pair + 1], group * group_pairs, before
            )

    for node in range(nodes):
        span = pl.ds(node * width, width)
        side = super_n[:, span].astype(BF16)
        value = dot(side, inv_high[node])
        value = value[:sides] + value[sides:] + dot(side[:sides], inv_low[node])
        low_solved[:, span] = value
        low_half[:, span] = value.astype(BF16)

    load_coupling.wait()

    def half_sum(half):
        return dot(low_half[...], coupling_v[:, pl.ds(pl.multiple_of(half * width, LANES), width)])

    half_send[...] = half_sum(1 - leaf)
    core_half = pltpu.make_async_remote_copy(
        src_ref=half_send,
        dst_ref=half_recv,
        send_sem=core_send.at[3],
        recv_sem=core_recv.at[3],
        device_id={"leaf": 1 - leaf},
        device_id_type=MESH,
    )
    core_half.start()
    first = jnp.where(me == 0, 1.0, 0.0).astype(F32)
    load_sides.wait()
    partial[...] = half_sum(leaf) - top_sides_v[...] * first
    core_half.wait()
    partial[...] = partial[...] + half_recv[...]
    for owner in range(owners):
        rs_send[owner] = partial[owner * own_rows : (owner + 1) * own_rows, :]

    def turn_of(chip):
        line = chip // 4
        return lax.rem(chip - 4 * line + 8 * members - line - line // 4, 4)

    my_turn = turn_of(me)
    is_owner = my_turn < 3
    my_owner = 3 * (me // 4) + jnp.minimum(my_turn, 2)

    def send_part(chunk):
        chip = partner(chunk)
        turn = turn_of(chip)

        @pl.when(turn < 3)
        def _():
            pltpu.make_async_remote_copy(
                src_ref=rs_send.at[3 * (chip // 4) + jnp.minimum(turn, 2)],
                dst_ref=rs_recv.at[chunk],
                send_sem=rs_send_sem,
                recv_sem=rs_recv_sem,
                device_id={"wide": chip},
                device_id_type=MESH,
            ).start()

    for chunk in range(members - 1):
        send_part(chunk)
    core_top.wait()
    core_tc.wait()
    for half in range(2):
        high, low = split(top_inv_f32[half])
        top_inv_high[half] = high
        top_inv_low[half] = low
    make_choosers(place_ref, choose_out, high_out)

    def weigh(node, _):
        span = pl.ds(pl.multiple_of(node * width, width), width)
        block = coupling_v[span, :]
        weighed[span, :] = (dot(inv_high[node], block) + dot(inv_low[node], block)).astype(BF16)
        return 0

    lax.fori_loop(0, nodes // 2, weigh, 0)

    def ag_copy(chunk):
        return pltpu.make_async_remote_copy(
            src_ref=ag_send,
            dst_ref=ag_recv.at[my_owner],
            send_sem=ag_send_sem,
            recv_sem=ag_recv_sem,
            device_id={"wide": partner(chunk)},
            device_id_type=MESH,
        )

    @pl.when(is_owner)
    def _():
        rs_recv[members - 1] = rs_send[my_owner]
        arrived = rs_recv.at[pl.ds(0, members - 1)]
        dummy(arrived, arrived, rs_send_sem, rs_recv_sem).wait_recv()
        pair_buf[leaf] = jnp.sum(rs_recv[...], axis=0)
        swap = pltpu.make_async_remote_copy(
            src_ref=pair_buf.at[leaf],
            dst_ref=pair_buf.at[leaf],
            send_sem=core_send.at[2],
            recv_sem=core_recv.at[2],
            device_id={"leaf": 1 - leaf},
            device_id_type=MESH,
        )
        swap.start()
        swap.wait()

        def times(product, x, half):
            high, low = split(x)
            both = product(jnp.concatenate([high, low], axis=0), top_inv_high[half])
            return both[:own_rows] + both[own_rows:] + product(high, top_inv_low[half])

        solved0 = times(dot, -pair_buf[0], 0)
        solved1 = times(dot, -pair_buf[1] - dot(solved0.astype(BF16), top_coup[1]), 1)
        answer1 = times(dot_t, solved1, 1)
        answer0 = times(dot_t, solved0 - dot_t(answer1.astype(BF16), top_coup[1]), 0)
        ag_send[...] = jnp.where(leaf == 0, answer0, answer1)
        ag_recv[my_owner] = ag_send[...]

        for chunk in range(members - 1):
            ag_copy(chunk).start()

    for node in range(nodes):
        span = pl.ds(node * width, width)
        high, low = split(low_solved[:, span])
        value = dot_t(jnp.concatenate([high, low], axis=0), inv_high[node])
        base[:, span] = value[:sides] + value[sides:] + dot_t(high, inv_low[node])

    lax.fori_loop(nodes // 2, nodes, weigh, 0)

    @pl.when(is_owner)
    def _():
        arrived = ag_recv.at[pl.ds(0, owners - 1)]
        dummy(arrived, arrived, ag_send_sem, ag_recv_sem).wait_recv()

    @pl.when(jnp.logical_not(is_owner))
    def _():
        dummy(ag_recv, ag_recv, ag_send_sem, ag_recv_sem).wait_recv()

    for owner in range(owners):
        top_out_v[owner * own_rows : (owner + 1) * own_rows, :] = ag_recv[owner]
    sol_half[leaf] = top_out_v[...].astype(BF16)
    core_sol = pltpu.make_async_remote_copy(
        src_ref=sol_half.at[leaf],
        dst_ref=sol_half.at[leaf],
        send_sem=core_send.at[4],
        recv_sem=core_recv.at[4],
        device_id={"leaf": 1 - leaf},
        device_id_type=MESH,
    )
    core_sol.start()
    store_top = pltpu.make_async_copy(top_out_v, top_out_any, local_sem.at[2])
    store_top.start()

    own_half = pl.ds(pl.multiple_of(leaf * width, LANES), width)
    other_half = pl.ds(pl.multiple_of((1 - leaf) * width, LANES), width)
    for node in range(nodes):
        span = pl.ds(node * width, width)
        base[:, span] = base[:, span] - dot_t(sol_half[leaf], weighed[node * width : (node + 1) * width, own_half])
    core_sol.wait()

    for node in range(nodes):
        span = pl.ds(node * width, width)
        rows_here = slice(node * width, (node + 1) * width)
        term = dot_t(sol_half[1 - leaf], weighed[rows_here, other_half])
        value = (base[:, span] - term).astype(BF16)
        for piece in range(width // LANES):
            at = node * width + piece * LANES
            low_final[at // TILE, :, pl.ds(at % TILE, LANES)] = value[:, piece * LANES : (piece + 1) * LANES]

    for half in range(2):
        for pair in range(half * pairs // 2, (half + 1) * pairs // 2):
            block = merge(low_final, choose_out[pair], high_out[pair : pair + 1], 0, None)
            store_chunks(back_send, pair * (TILE // 16), turned(block).astype(BF16))
        start_group(back, 2 * half)
        start_group(back, 2 * half + 1)
    own_back.start()

    def store_out(part):
        span = pl.ds(part * 3 * TILE, 3 * TILE)
        return pltpu.make_async_copy(out_v.at[:, span], out_any.at[:, span], out_sem.at[part])

    for group in range(groups):
        wait_group(back_recv, back_recv_sem, group)
        if group == groups - 1:
            own_back.wait()
        block = back_recv[group * chunks : (group + 1) * chunks].reshape(group_rows, LANES)
        for tile in range(group_tiles):
            columns = block[tile * LANES : (tile + 1) * LANES].astype(F32).T
            turned_back[tile // 2, :, pl.ds((tile % 2) * LANES, LANES)] = columns[:sides].astype(BF16)

        for pair in range(pairs):
            span = pl.ds(pair * TILE, TILE)
            before = out_sum[:, span] if group > 0 else None
            value = merge(
                turned_back, choose_last[pair], high_last[pair : pair + 1], group * group_pairs, before
            )
            if group < groups - 1:
                out_sum[:, span] = value
            else:
                out_v[:, span] = value.astype(BF16)
                if pair % 3 == 2:
                    store_out(pair // 3).start()

    store_top.wait()
    for part in range(pairs // 3):
        store_out(part).wait()
    sent = pos_send.at[pl.ds(0, members - 1)]
    dummy(sent, sent, pos_send_sem, pos_send_sem).wait_send()
    sent = send_buf.at[pl.ds(0, members - 1)]
    dummy(sent, sent, there_send, there_send).wait_send()
    sent = back_send.at[pl.ds(0, members - 1)]
    dummy(sent, sent, back_send_sem, back_send_sem).wait_send()

    @pl.when(is_owner)
    def _():
        part = rs_send.at[pl.ds(0, owners - 1)]
        dummy(part, part, rs_send_sem, rs_send_sem).wait_send()
        part = rs_recv.at[pl.ds(0, members - 1)]
        dummy(part, part, ag_send_sem, ag_send_sem).wait_send()

    @pl.when(jnp.logical_not(is_owner))
    def _():
        dummy(rs_send, rs_send, rs_send_sem, rs_send_sem).wait_send()


def widen(low_ref, top_ref, out_ref, top_out_ref):
    out_ref[...] = low_ref[...].astype(F32)

    @pl.when(pl.program_id(0) == 0)
    def _():
        top_out_ref[...] = top_ref[...]


def shards(drop_sides, super_index, low_inverse, coupling, top_sides, top_inverse, top_coupling):
    sides, rows = drop_sides.shape
    nodes, width, _ = low_inverse.shape
    members = lax.axis_size("wide")
    cap = rows // members
    owners = 48
    top_cols = coupling.shape[1]
    tiles = rows // LANES
    own = sides // owners
    anyspace = pl.BlockSpec(memory_space=pl.ANY)
    dma = pltpu.SemaphoreType.DMA
    dims = (sides, rows, members, cap, nodes, width, owners)
    low, top = pl.pallas_call(
        functools.partial(kernel, dims),
        out_shape=(
            jax.ShapeDtypeStruct((sides, rows), BF16),
            jax.ShapeDtypeStruct(top_sides.shape, F32),
        ),
        in_specs=[anyspace] * 7,
        out_specs=(anyspace, anyspace),
        scratch_shapes=[
            pltpu.VMEM((tiles, LANES), jnp.int32),
            pltpu.VMEM((sides, width), F32),
            pltpu.VMEM((sides, rows), BF16),
            pltpu.VMEM((sides, width), F32),
            pltpu.VMEM((tiles * members, LANES), BF16),
            pltpu.VMEM((LANES, rows), BF16),
            pltpu.VMEM((LANES, rows), BF16),
            pltpu.VMEM((2 * members, rows), BF16),
            pltpu.VMEM((LANES, rows), BF16),
            pltpu.VMEM((nodes, width, width), F32),
            pltpu.VMEM((rows, top_cols), BF16),
            pltpu.VMEM((2, width, width), F32),
            pltpu.VMEM((2, width, width), BF16),
            pltpu.VMEM((2, width, width), BF16),
            pltpu.VMEM((2, width, width), BF16),
            pltpu.VMEM((nodes, width, width), BF16),
            pltpu.VMEM((nodes, width, width), BF16),
            pltpu.VMEM((tiles, LANES), F32),
            pltpu.VMEM((tiles, LANES), F32),
            pltpu.VMEM((tiles, LANES), F32),
            pltpu.VMEM((sides, rows), F32),
            pltpu.VMEM((rows // TILE, 2 * sides + 16, TILE), BF16),
            pltpu.VMEM((rows // TILE // 4, 2 * sides, TILE), BF16),
            pltpu.VMEM((members, 1, LANES), F32),
            pltpu.VMEM((members, 1, LANES), F32),
            pltpu.VMEM((rows // TILE, TILE, TILE), BF16),
            pltpu.VMEM((rows // TILE, TILE, TILE), BF16),
            pltpu.VMEM((rows // TILE, TILE, TILE), BF16),
            pltpu.VMEM((rows // TILE, TILE), F32),
            pltpu.VMEM((rows // TILE, TILE), F32),
            pltpu.VMEM((rows // TILE, TILE), F32),
            pltpu.VMEM((2 * sides, rows), F32),
            pltpu.VMEM((sides, rows), F32),
            pltpu.VMEM((sides, rows), F32),
            pltpu.VMEM((rows, top_cols), BF16),
            pltpu.VMEM((sides, rows), BF16),
            pltpu.VMEM((rows // TILE, sides, TILE), BF16),
            pltpu.VMEM((rows // TILE // 4, sides, TILE), BF16),
            pltpu.VMEM((sides, rows), F32),
            pltpu.VMEM((members, cap, LANES), jnp.int16),
            pltpu.VMEM((members, cap, LANES), jnp.int16),
            pltpu.VMEM((members, cap, LANES), BF16),
            pltpu.VMEM((members, cap, LANES), BF16),
            pltpu.VMEM((sides, width), F32),
            pltpu.VMEM((sides, width), F32),
            pltpu.VMEM((sides, width), F32),
            pltpu.VMEM((owners, own, width), F32),
            pltpu.VMEM((members, own, width), F32),
            pltpu.VMEM((2, own, width), F32),
            pltpu.VMEM((own, width), F32),
            pltpu.VMEM((owners, own, width), F32),
            pltpu.VMEM((2, sides, width), BF16),
            dma((7,)),
            dma((5,)),
            dma((5,)),
            dma((4,)),
            dma,
            dma((4,)),
            dma,
            dma,
            dma,
            dma((4,)),
            dma,
            dma,
            dma,
            dma,
            dma((4,)),
        ],
        compiler_params=pltpu.CompilerParams(
            collective_id=0, has_side_effects=True, vmem_limit_bytes=56 << 20
        ),
        name="substitution",
    )(
        super_index.reshape(tiles, LANES),
        drop_sides,
        low_inverse,
        coupling,
        top_sides,
        top_inverse,
        top_coupling,
    )
    return pl.pallas_call(
        widen,
        grid=(2,),
        out_shape=(jax.ShapeDtypeStruct((sides, rows), F32), jax.ShapeDtypeStruct(top_sides.shape, F32)),
        in_specs=[
            pl.BlockSpec((sides, rows // 2), lambda at: (0, at)),
            pl.BlockSpec(top_sides.shape, lambda at: (0, 0)),
        ],
        out_specs=(
            pl.BlockSpec((sides, rows // 2), lambda at: (0, at)),
            pl.BlockSpec(top_sides.shape, lambda at: (0, 0)),
        ),
        name="widen",
    )(low, top)


def solution(mesh):
    placed = (
        P(None, ("leaf", "wide")),
        P(("leaf", "wide")),
        P(("leaf", "wide"), None, None),
        P(("leaf", "wide"), None),
        P(None, "leaf"),
        P("leaf", None, None),
        P(None, "leaf", None, None),
    )
    return jax.shard_map(
        shards,
        mesh=mesh,
        in_specs=placed,
        out_specs=(P(None, ("leaf", "wide")), P(None, "leaf")),
        check_vma=False,
    )
```
